512 devices in a mesh: span: 16 (over z, x_hi), flow: 32 (over y, x_lo, core).
Axes of the slice: x: 4 (x_hi: 2, x_lo: 2; x = x_hi * 2 + x_lo), y: 8, z: 8, core: 2. Of those that a mesh axis runs over, the one named last changes fastest.
Arguments:
- rhs_fluid: float32 [6, 32, 256, 128], P(None, 'span', 'flow'), may hold values from -6 to 6
- rhs_solid: float32 [512, 128], P('span'), may hold values from -6 to 6
- blocks: float32 [6, 6, 32, 256, 128], P(None, None, 'span', 'flow')
- weights: float32 [6, 32, 256, 128], P(None, 'span', 'flow'), may hold values from 0.5 to 1.1
- kdiag: float32 [512, 128], P('span'), may hold values from 1 to 4
- wall_fluid: int32 [16, 32], P('span', 'flow'), may hold values from 0 to 15
- wall_solid: int32 [16, 32], P('span', 'flow'), may hold values from 0 to 31, each once within a row
- wall_coef: float32 [16, 32, 128], P('span', 'flow'), may hold values from 0.3 to 1.5
Outputs:
- x_fluid: float32 [6, 32, 256, 128], P(None, 'span', 'flow')
- x_solid: float32 [512, 128], P('span')
The draws below stay inside these ranges and needn't reach their ends.
Inputs may be any that keep to these rules, and one draw needn't show every extreme that they name: `wall_fluid`: a local row a * 8 + b of the fluid tile of span index i and flow index q; rows may repeat. `wall_solid`: each row is a permutation of the 32 metal rows of band i.
All inputs are finite; a program needn't handle non-finite values.
Results may differ from the reference program's by a relative error of at most 0.0003.
Values sent between devices are 32-bit elements; how exact they have to be, the bound alone decides.
A program may use at most 64 MiB of HBM per device.

```python
import math
import jax
import jax.numpy as jnp
from jax import lax

FIELDS = 6
CA = 2
CB = 8
NC = 128
K = 1
KRYLOV = 6
NA = 32
NB = 256
SROWS = 32
NSOL = 512
N_SPAN = 16


def draw_blocks(key, part):
    key_diag = jax.random.fold_in(key, 11)
    key_off = jax.random.fold_in(key, 12)
    diag_part = jax.random.uniform(key_diag, (6, NA, NB, NC), jnp.float32, 8.0, 10.0)
    off_part = 0.3 * jax.random.normal(key_off, (6, 6, NA, NB, NC), jnp.float32)
    off_part = jnp.clip(off_part, -0.45, 0.45)
    unit = jnp.eye(6, dtype=jnp.float32)[:, :, None, None, None]
    return off_part * (1.0 - unit) + unit * diag_part[:, None]


def with_ends(result, rng, least, largest):
    spot = [jax.random.randint(jax.random.fold_in(rng, axis), (), 0, length) for axis, length in enumerate(result.shape)]
    main_axis = result.shape.index(max(result.shape))
    neighbour = spot[:main_axis] + [(spot[main_axis] + 1) % result.shape[main_axis]] + spot[main_axis + 1:]
    return result.at[tuple(spot)].set(least).at[tuple(neighbour)].set(largest)


def block_levels(own_key, extent, split, smallest, high):
    factor_of = 1.0
    for position, parts in split:
        draws = jax.random.uniform(jax.random.fold_in(jax.random.fold_in(own_key, 6), position), (parts,), jnp.float32, smallest / len(split), high / len(split))
        factor_of = factor_of * jnp.repeat(jnp.exp(draws), extent[position] // parts).reshape((-1,) + (1,) * (len(extent) - 1 - position))
    return factor_of


def bell_draw(stream_key, shape, spread, reach, split=(), kind=jnp.bfloat16):
    gain = block_levels(stream_key, shape, split, -0.22, 0.18) if split else 1.0
    entries = jax.random.normal(stream_key, shape, jnp.float32) * spread * gain
    return jnp.minimum(jnp.maximum(entries, -reach), reach).astype(kind)


def setup_inputs(seed: int = 0) -> dict:
    seeds = jax.random.split(jax.random.key(seed), 9)
    rhs_fluid = bell_draw(seeds[0], (FIELDS, NA, NB, NC), 1.0, 6.0, ((1, 16), (2, 32)), jnp.float32)
    rhs_solid = bell_draw(seeds[1], (NSOL, NC), 1.0, 6.0, ((0, 16),), jnp.float32)
    blocks = draw_blocks(jax.random.fold_in(seeds[8], 71), 0)
    weights = jnp.clip(0.5 + 0.6 * jax.random.uniform(seeds[3], (6, NA, NB, NC), jnp.float32) ** block_levels(seeds[3], (6, NA, NB, NC), ((1, 16), (2, 32)), -0.2, 0.2), 0.5, 1.1)
    kdiag = jnp.clip(jnp.exp(math.log(4.0) - 1.3862944 * jax.random.uniform(seeds[4], (NSOL, NC), jnp.float32) ** block_levels(seeds[4], (NSOL, NC), ((0, 16),), -0.2, 0.2)), 1.0, 4.0)
    wall_fluid = with_ends(jax.random.randint(seeds[5], (N_SPAN, SROWS), 0, CA * CB), jax.random.fold_in(seeds[5], 1), 0, (CA * CB) - 1).astype(jnp.int32)
    wall_solid = jax.vmap(lambda own: jax.random.permutation(own, SROWS))(jax.random.split(seeds[6], N_SPAN)).reshape((N_SPAN, SROWS)).astype(jnp.int32)
    wall_coef = jnp.clip(jnp.exp(math.log(1.5) - 1.60943787 * jax.random.uniform(seeds[7], (N_SPAN, SROWS, NC), jnp.float32) ** block_levels(seeds[7], (N_SPAN, SROWS, NC), ((0, 16), (1, 32)), -0.2, 0.2)), 0.3, 1.5)
    return {"rhs_fluid": rhs_fluid, "rhs_solid": rhs_solid, "blocks": blocks, "weights": weights, "kdiag": kdiag, "wall_fluid": wall_fluid, "wall_solid": wall_solid, "wall_coef": wall_coef}


def patch_index(wall_fluid, wall_solid):
    band = jnp.arange(N_SPAN, dtype=jnp.int32)[:, None]
    slot = jnp.arange(SROWS, dtype=jnp.int32)[None, :]
    fluid_a = (band * CA + wall_fluid // CB).reshape(-1)
    fluid_b = (slot // K * CB + wall_fluid % CB).reshape(-1)
    metal = (band * SROWS + wall_solid).reshape(-1)
    return (fluid_a, fluid_b, metal)

def apply_all(field, metal_u, blocks, weights, kdiag, fluid_a, fluid_b, metal, coef):
    local = jnp.einsum('fgabc,gabc->fabc', blocks, field, precision=lax.Precision.HIGHEST)
    padded = jnp.pad(field, ((0, 0), (1, 1), (1, 1), (0, 0)))
    beside = weights[0][None] * padded[:, :-2, 1:-1] + weights[1][None] * padded[:, 2:, 1:-1]
    beside = beside + weights[2][None] * padded[:, 1:-1, :-2] + weights[3][None] * padded[:, 1:-1, 2:]
    beside = beside + weights[4][None] * jnp.roll(field, 1, axis=3) + weights[5][None] * jnp.roll(field, -1, axis=3)
    inflow = jnp.zeros((NA, NB, NC), jnp.float32).at[fluid_a, fluid_b].add(coef * metal_u[metal])
    image_f = (local - beside).at[5].add(-inflow)
    upad = jnp.pad(metal_u, ((1, 1), (0, 0)))
    sink = jnp.zeros((NSOL, NC), jnp.float32).at[metal].add(coef * field[5, fluid_a, fluid_b])
    image_s = (4.0 + kdiag) * metal_u - (upad[:-2] + upad[2:] + jnp.roll(metal_u, 1, axis=1) + jnp.roll(metal_u, -1, axis=1)) - sink
    return (image_f, image_s)

def inner(left, right):
    return jnp.sum(left[0] * right[0]) + jnp.sum(left[1] * right[1])

def least_squares(hess, beta, steps):
    cos_list, sin_list, upper = ([], [], [])
    rhs_g = [beta] + [jnp.float32(0.0) for _ in range(steps)]
    for j in range(steps):
        column = [hess[i][j] for i in range(j + 2)]
        for i in range(j):
            top = cos_list[i] * column[i] + sin_list[i] * column[i + 1]
            column[i + 1] = -sin_list[i] * column[i] + cos_list[i] * column[i + 1]
            column[i] = top
        radius = jnp.sqrt(column[j] * column[j] + column[j + 1] * column[j + 1])
        cos_now = column[j] / radius
        sin_now = column[j + 1] / radius
        column[j] = radius
        rhs_g[j + 1] = -sin_now * rhs_g[j]
        rhs_g[j] = cos_now * rhs_g[j]
        cos_list.append(cos_now)
        sin_list.append(sin_now)
        upper.append(column[:j + 1])
    coeffs = [None] * steps
    for j in range(steps - 1, -1, -1):
        total = rhs_g[j]
        for k in range(j + 1, steps):
            total = total - upper[k][j] * coeffs[k]
        coeffs[j] = total / upper[j][j]
    return coeffs

def reference(rhs_fluid, rhs_solid, blocks, weights, kdiag, wall_fluid, wall_solid, wall_coef):
    fluid_a, fluid_b, metal = patch_index(wall_fluid, wall_solid)
    coef = wall_coef.reshape(-1, NC)
    start = (rhs_fluid, rhs_solid)
    beta = jnp.sqrt(inner(start, start))
    basis = [(rhs_fluid / beta, rhs_solid / beta)]
    hess = [[jnp.float32(0.0) for _ in range(KRYLOV)] for _ in range(KRYLOV + 1)]
    for j in range(KRYLOV):
        image_f, image_s = apply_all(basis[j][0], basis[j][1], blocks, weights, kdiag, fluid_a, fluid_b, metal, coef)
        image = (image_f, image_s)
        values = [inner(basis[i], image) for i in range(j + 1)]
        for i in range(j + 1):
            hess[i][j] = values[i]
            image_f = image_f - values[i] * basis[i][0]
            image_s = image_s - values[i] * basis[i][1]
        rest = jnp.sqrt(inner((image_f, image_s), (image_f, image_s)))
        hess[j + 1][j] = rest
        basis.append((image_f / rest, image_s / rest))
    coeffs = least_squares(hess, beta, KRYLOV)
    x_fluid = jnp.zeros_like(rhs_fluid)
    x_solid = jnp.zeros_like(rhs_solid)
    for j in range(KRYLOV):
        x_fluid = x_fluid + coeffs[j] * basis[j][0]
        x_solid = x_solid + coeffs[j] * basis[j][1]
    return (x_fluid, x_solid)
```

```python
import functools

import jax
import jax.numpy as jnp
from jax import lax
from jax.experimental import pallas as pl
from jax.experimental.pallas import tpu as pltpu
from jax.sharding import PartitionSpec as P

KRYLOV = 6
MESH = pl.DeviceIdType.MESH
EARLY = 4


def extended(shard, sides, width):
    for axis, dim in sides:
        count, length = (lax.axis_size(axis), shard.shape[dim])
        up = [(i, (i + 1) % count) for i in range(count - 1)]
        down = [(j, i) for i, j in up]
        last = lax.slice_in_dim(shard, length - width, length, axis=dim)
        first = lax.slice_in_dim(shard, 0, width, axis=dim)
        before = lax.ppermute(last, axis, up)
        after = lax.ppermute(first, axis, down)
        shard = jnp.concatenate([before, shard, after], axis=dim)
    return shard


def back_substitute(upper, rhs_g, steps):
    coeffs = [None] * steps
    for j in range(steps - 1, -1, -1):
        total = rhs_g[j]
        for k in range(j + 1, steps):
            total = total - upper[k][j] * coeffs[k]
        coeffs[j] = total / upper[j][j]
    return coeffs


def least_squares(hess, beta, zero, steps):
    cos_list, sin_list, upper = ([], [], [])
    rhs_g = [beta] + [zero for _ in range(steps)]
    for j in range(steps):
        column = [hess[i][j] for i in range(j + 2)]
        for i in range(j):
            top = cos_list[i] * column[i] + sin_list[i] * column[i + 1]
            column[i + 1] = -sin_list[i] * column[i] + cos_list[i] * column[i + 1]
            column[i] = top
        radius = jnp.sqrt(column[j] * column[j] + column[j + 1] * column[j + 1])
        cos_now = column[j] / radius
        sin_now = column[j + 1] / radius
        column[j] = radius
        rhs_g[j + 1] = -sin_now * rhs_g[j]
        rhs_g[j] = cos_now * rhs_g[j]
        cos_list.append(cos_now)
        sin_list.append(sin_now)
        upper.append(column[: j + 1])
    return back_substitute(upper, rhs_g, steps)


def arnoldi(rhs_fluid, rhs_solid, blocks, weights, kdiag, wall_fluid, wall_solid, wall_coef):
    rows_a = rhs_fluid.shape[1]
    rows_b = rhs_fluid.shape[2]
    width = rhs_fluid.shape[3]
    cells = rows_a * rows_b
    band_rows = rhs_solid.shape[0]
    patch_rows = wall_fluid[0]
    patch_metal = wall_solid[0]
    coef = wall_coef[0]
    fluid_pick = (jnp.arange(cells, dtype=jnp.int32)[:, None] == patch_rows[None, :]).astype(
        jnp.float32
    )
    metal_pick = (jnp.arange(band_rows, dtype=jnp.int32)[:, None] == patch_metal[None, :]).astype(
        jnp.float32
    )
    first_flow = (lax.axis_index("flow") == 0).astype(jnp.float32)
    highest = lax.Precision.HIGHEST

    def local_inner(left, right):
        return jnp.sum(left[0] * right[0]) + first_flow * jnp.sum(left[1] * right[1])

    beta = jnp.sqrt(
        lax.psum(local_inner((rhs_fluid, rhs_solid), (rhs_fluid, rhs_solid)), ("span", "flow"))
    )
    basis = [(rhs_fluid / beta, rhs_solid / beta)]
    hess = [[jnp.float32(0.0) for _ in range(KRYLOV)] for _ in range(KRYLOV + 1)]
    for j in range(KRYLOV):
        field = basis[j][0]
        metal_u = basis[j][1]
        padded = extended(field, (("span", 1), ("flow", 2)), 1)
        local = jnp.einsum("fgabc,gabc->fabc", blocks, field, precision=highest)
        beside = weights[0][None] * padded[:, :-2, 1:-1] + weights[1][None] * padded[:, 2:, 1:-1]
        beside = (
            beside
            + weights[2][None] * padded[:, 1:-1, :-2]
            + weights[3][None] * padded[:, 1:-1, 2:]
        )
        beside = (
            beside
            + weights[4][None] * jnp.roll(field, 1, axis=3)
            + weights[5][None] * jnp.roll(field, -1, axis=3)
        )
        metal_at = jnp.dot(metal_pick.T, metal_u, precision=highest)
        inflow = jnp.dot(fluid_pick, coef * metal_at, precision=highest).reshape(
            rows_a, rows_b, width
        )
        image_f = (local - beside).at[5].add(-inflow)
        wall_vals = coef * jnp.dot(fluid_pick.T, field[5].reshape(cells, width), precision=highest)
        sink = lax.psum(jnp.dot(metal_pick, wall_vals, precision=highest), "flow")
        upad = extended(metal_u, (("span", 0),), 1)
        beside_all = (
            upad[:-2] + upad[2:] + jnp.roll(metal_u, 1, axis=1) + jnp.roll(metal_u, -1, axis=1)
        )
        image_s = (4.0 + kdiag) * metal_u - beside_all - sink
        terms = jnp.stack([local_inner(basis[i], (image_f, image_s)) for i in range(j + 1)])
        values = lax.psum(terms, ("span", "flow"))
        for i in range(j + 1):
            image_f = image_f - values[i] * basis[i][0]
            image_s = image_s - values[i] * basis[i][1]
        rest = jnp.sqrt(
            lax.psum(local_inner((image_f, image_s), (image_f, image_s)), ("span", "flow"))
        )
        for i in range(j + 1):
            hess[i][j] = values[i]
        hess[j + 1][j] = rest
        basis.append((image_f / rest, image_s / rest))
    coeffs = least_squares(hess, beta, jnp.float32(0.0), KRYLOV)
    x_fluid = jnp.zeros_like(rhs_fluid)
    x_solid = jnp.zeros_like(rhs_solid)
    for j in range(KRYLOV):
        x_fluid = x_fluid + coeffs[j] * basis[j][0]
        x_solid = x_solid + coeffs[j] * basis[j][1]
    return (x_fluid, x_solid)


def kernel(
    ns, nf,
    rf_hbm, rs_hbm, bl_hbm, we_hbm, kd_hbm, wf_ref, ws_ref, wc_ref,
    xf_ref, xs_ref, ok_ref,
    z, u, q, bl, we, wm, kd, hs, hq, sq, he, wall, place, pairs, scal, ra, rb,
    in_sem, s_halo, r_halo, s_edge, r_edge, s_wall, r_wall, s_red, r_red,
):
    f32 = jnp.float32
    s = lax.axis_index("span")
    f = lax.axis_index("flow")
    up = (lax.rem(s + 1, ns), f)
    down = (lax.rem(s + ns - 1, ns), f)
    right = (s, lax.rem(f + 1, nf))
    left = (s, lax.rem(f + nf - 1, nf))

    loads = [
        pltpu.make_async_copy(rf_hbm, z.at[0], in_sem.at[0]),
        pltpu.make_async_copy(rs_hbm, u.at[0], in_sem.at[1]),
        pltpu.make_async_copy(we_hbm, we, in_sem.at[2]),
        pltpu.make_async_copy(bl_hbm, bl, in_sem.at[3]),
        pltpu.make_async_copy(kd_hbm, kd, in_sem.at[4]),
    ]
    for load in loads:
        load.start()

    barrier = pltpu.get_barrier_semaphore()

    def greet_flow(d, c):
        pl.semaphore_signal(barrier, inc=1, device_id=(s, lax.rem(f + d, nf)), device_id_type=MESH)
        return c

    def greet_span(d, c):
        pl.semaphore_signal(barrier, inc=1, device_id=(lax.rem(s + d, ns), f), device_id_type=MESH)
        return c

    lax.fori_loop(1, ns, greet_span, 0)
    lax.fori_loop(1, nf, greet_flow, 0)

    row8 = lax.broadcasted_iota(jnp.int32, (8, 128), 0)
    row16 = lax.broadcasted_iota(jnp.int32, (2, 8, 128), 0) * 8 + lax.broadcasted_iota(
        jnp.int32, (2, 8, 128), 1
    )
    row32 = lax.broadcasted_iota(jnp.int32, (32, 128), 0)
    lane32 = lax.broadcasted_iota(jnp.int32, (32, 128), 1)
    eye = row32 == lane32
    patch = wf_ref[0, 0]
    metal_row = ws_ref[0, 0]
    coef = wc_ref[0]
    wall_mask = jnp.where(row16 == patch, 1.0, 0.0).astype(f32)
    metal_mask = jnp.where(row32 == metal_row, 1.0, 0.0).astype(f32)
    lane1 = lax.broadcasted_iota(jnp.int32, (1, 128), 1)
    place[pl.ds(f, 1), :] = jnp.where(lane1 == f, metal_row.astype(f32), 0.0)
    has_down = jnp.where(s > 0, 1.0, 0.0).astype(f32)
    has_up = jnp.where(s < ns - 1, 1.0, 0.0).astype(f32)
    has_left = jnp.where(f > 0, 1.0, 0.0).astype(f32)
    has_right = jnp.where(f < nf - 1, 1.0, 0.0).astype(f32)

    def send_rows_flow(buf, k):
        def one(d, c):
            pltpu.make_async_remote_copy(
                src_ref=buf.at[pl.ds(f, 1)], dst_ref=buf.at[pl.ds(f, 1)],
                send_sem=s_wall.at[k], recv_sem=r_wall.at[k],
                device_id=(s, lax.rem(f + d, nf)), device_id_type=MESH,
            ).start()
            return c

        lax.fori_loop(1, nf, one, 0)

    def rows_flow(buf, k):
        return pltpu.make_async_remote_copy(
            src_ref=buf.at[pl.ds(0, nf - 1)], dst_ref=buf.at[pl.ds(0, nf - 1)],
            send_sem=s_wall.at[k], recv_sem=r_wall.at[k], device_id=right, device_id_type=MESH,
        )

    def send_rows_span(buf, k):
        def one(d, c):
            pltpu.make_async_remote_copy(
                src_ref=buf.at[pl.ds(s, 1)], dst_ref=buf.at[pl.ds(s, 1)],
                send_sem=s_red.at[k], recv_sem=r_red.at[k],
                device_id=(lax.rem(s + d, ns), f), device_id_type=MESH,
            ).start()
            return c

        lax.fori_loop(1, ns, one, 0)

    def rows_span(buf, k):
        return pltpu.make_async_remote_copy(
            src_ref=buf.at[pl.ds(0, ns - 1)], dst_ref=buf.at[pl.ds(0, ns - 1)],
            send_sem=s_red.at[k], recv_sem=r_red.at[k], device_id=up, device_id_type=MESH,
        )

    def halos(k):
        def copy(n, src, dst, to):
            return pltpu.make_async_remote_copy(
                src_ref=src, dst_ref=dst, send_sem=s_halo.at[k, n], recv_sem=r_halo.at[k, n],
                device_id=to, device_id_type=MESH,
            )

        return [
            copy(0, z.at[k, :, 1], hs.at[k, 0], up),
            copy(1, z.at[k, :, 0], hs.at[k, 1], down),
            copy(2, sq.at[k, 0], hq.at[k, 0], right),
            copy(3, sq.at[k, 1], hq.at[k, 1], left),
        ]

    def edges(k):
        def copy(n, src, dst, to):
            return pltpu.make_async_remote_copy(
                src_ref=src, dst_ref=dst, send_sem=s_edge.at[k, n], recv_sem=r_edge.at[k, n],
                device_id=to, device_id_type=MESH,
            )

        return [
            copy(0, u.at[k, pl.ds(31, 1)], he.at[k, 0, pl.ds(0, 1)], up),
            copy(1, u.at[k, pl.ds(0, 1)], he.at[k, 1, pl.ds(0, 1)], down),
        ]

    def send_halos(k):
        out = halos(k)
        out[0].start()
        out[1].start()
        for g in range(6):
            for a in range(2):
                i = 2 * g + a
                sq[k, 0, i : i + 1, :] = z[k, g, a, 7:8, :]
                sq[k, 1, i : i + 1, :] = z[k, g, a, 0:1, :]
        out[2].start()
        out[3].start()

    def local_part(k):
        field = [z[k, g] for g in range(6)]
        for g in range(6):
            v = field[g]
            total = bl[g, 0] * field[0]
            for h in range(1, 6):
                total = total + bl[g, h] * field[h]
            total = total - we[4] * pltpu.roll(v, 1, 2) - we[5] * pltpu.roll(v, 127, 2)
            total = total - wm[0] * pltpu.roll(v, 1, 1) - wm[1] * pltpu.roll(v, 7, 1)
            z[k + 1, g, 0] = total[0] - we[1, 0] * v[1]
            z[k + 1, g, 1] = total[1] - we[0, 1] * v[0]

    def halo_part(k, metal_here):
        inflow = coef * metal_here
        for g in range(6):
            for a in range(2):
                i = 2 * g + a
                total = z[k + 1, g, a]
                if a == 0:
                    total = total - wm[4, 0] * hs[k, 0, g]
                else:
                    total = total - wm[4, 1] * hs[k, 1, g]
                total = total - wm[2, a] * hq[k, 0, i : i + 1, :] - wm[3, a] * hq[k, 1, i : i + 1, :]
                if g == 5:
                    total = total - wall_mask[a] * inflow
                z[k + 1, g, a] = total

    def own_metal(values):
        return jnp.sum(metal_mask * values, axis=0, keepdims=True)

    def wall_value(k):
        picked = wall_mask[0] * z[k, 5, 0] + wall_mask[1] * z[k, 5, 1]
        return coef * jnp.sum(picked, axis=0, keepdims=True)

    def metal_local(k):
        v = u[k]
        total = (4.0 + kd[...]) * v - pltpu.roll(v, 1, 1) - pltpu.roll(v, 127, 1)
        below = jnp.where(row32 == 0, has_down * he[k, 0, 0:1, :], pltpu.roll(v, 1, 0))
        above = jnp.where(row32 == 31, has_up * he[k, 1, 0:1, :], pltpu.roll(v, 31, 0))
        return total - below - above

    def dot_row(store, i, j, own_i, own_j):
        total = store[i, 0, 0] * store[j, 0, 0] + store[i, 0, 1] * store[j, 0, 1]
        for g in range(1, 6):
            total = total + store[i, g, 0] * store[j, g, 0] + store[i, g, 1] * store[j, g, 1]
        return jnp.sum(total, axis=0, keepdims=True) + own_i * own_j

    def packed():
        sums = jnp.sum(pairs[...], axis=1, keepdims=True)
        return jnp.sum(jnp.where(eye, sums, 0.0), axis=0, keepdims=True)

    def unpack(total):
        sums = jnp.sum(jnp.where(eye, total, 0.0), axis=1, keepdims=True)
        scal[...] = jnp.broadcast_to(sums, (32, 128))

    loads[0].wait()
    for g in range(6):
        for a in range(2):
            i = 2 * g + a
            sq[0, 0, i : i + 1, :] = z[0, g, a, 7:8, :]
            sq[0, 1, i : i + 1, :] = z[0, g, a, 0:1, :]
    sq[:, :, 12:16, :] = jnp.zeros((KRYLOV, 2, 4, 128), f32)
    pl.semaphore_wait(barrier, ns + nf - 2)
    for copy in halos(0):
        copy.start()
    loads[1].wait()
    for copy in edges(0):
        copy.start()
    pairs[...] = jnp.zeros((32, 128), f32)
    loads[2].wait()
    wm[0] = jnp.where(row8 == 0, 0.0, we[2])
    wm[1] = jnp.where(row8 == 7, 0.0, we[3])
    wm[2] = jnp.where(row8 == 0, has_left * we[2], 0.0)
    wm[3] = jnp.where(row8 == 7, has_right * we[3], 0.0)
    wm[4, 0] = has_down * we[0, 0]
    wm[4, 1] = has_up * we[1, 1]
    loads[3].wait()
    loads[4].wait()

    own = []
    walls = []
    pick = None
    coef_a = coef_b = None
    for k in range(KRYLOV):
        if k > 0:
            send_halos(k)
        mine = wall_value(k)
        walls.append(mine)
        if k < KRYLOV - 1:
            wall[k, pl.ds(f, 1), :] = mine
            send_rows_flow(wall.at[k], k)
        if k == 0:
            send_rows_flow(place, KRYLOV - 1)
        local_part(k)
        if k > 0:
            if k == 1:
                rows_flow(place, KRYLOV - 1).wait_recv()
                places = jnp.sum(place[...], axis=0, keepdims=True)
                pick = jnp.where((row32.astype(f32) == places) & (lane32 < 32), 1.0, 0.0)[:, 0:32]
            rows_flow(wall.at[k - 1], k - 1).wait_recv()
            sink = jnp.dot(
                pick, wall[k - 1], precision=lax.Precision.HIGHEST, preferred_element_type=f32
            )
            for copy in edges(k - 1):
                copy.wait_recv()
            u[k] = metal_local(k - 1) - sink
            for copy in edges(k):
                copy.start()
        own.append(own_metal(u[k]))
        if k == EARLY - 1:
            n = 0
            for i in range(EARLY):
                for j in range(i, EARLY):
                    pairs[n : n + 1, :] = dot_row(z, i, j, own[i], own[j])
                    n += 1
            ra[0, pl.ds(f, 1), :] = packed()
            send_rows_flow(ra.at[0], KRYLOV)
        if k == EARLY:
            rows_flow(ra.at[0], KRYLOV).wait_recv()
            rb[0, pl.ds(s, 1), :] = jnp.sum(ra[0], axis=0, keepdims=True)
            send_rows_span(rb.at[0], 0)
        if k == EARLY + 1:
            rows_span(rb.at[0], 0).wait_recv()
            unpack(jnp.sum(rb[0], axis=0, keepdims=True))
            gram = {}
            n = 0
            for i in range(EARLY):
                for j in range(i, EARLY):
                    gram[i, j] = scal[n : n + 1, :]
                    n += 1
            r = {}
            inv = []
            trust = []
            for i in range(EARLY):
                for j in range(i, EARLY):
                    t = gram[i, j]
                    for h in range(i):
                        t = t - r[h, i] * r[h, j]
                    if i == j:
                        floor = gram[i, i] * 1e-5
                        trust.append(t > floor)
                        t = jnp.maximum(t, floor)
                        inv.append(lax.rsqrt(t))
                    r[i, j] = t * inv[i]
            ratio = [r[i, i + 1] * inv[i] for i in range(EARLY - 1)]
            coef_a = [ratio[0]]
            coef_b = [None, r[1, 1] * inv[0]]
            good = trust[1]
            for i in range(1, EARLY - 1):
                good = good & trust[i + 1]
                coef_a.append(jnp.where(good, ratio[i] - ratio[i - 1], coef_a[i - 1]))
                guess = coef_b[1] * 1.22
                coef_b.append(jnp.where(good, r[i + 1, i + 1] * inv[i], guess))
            while len(coef_a) < KRYLOV:
                coef_a.append(coef_a[-1])
            while len(coef_b) < KRYLOV + 1:
                coef_b.append(coef_b[-1])
            poly = [[inv[0]]]
            for i in range(KRYLOV):
                back = 1.0 / coef_b[i + 1]
                new = []
                for j in range(i + 2):
                    t = None
                    if j >= 1:
                        t = poly[i][j - 1]
                    if j <= i:
                        t = -coef_a[i] * poly[i][j] if t is None else t - coef_a[i] * poly[i][j]
                    if i >= 1 and j <= i - 1:
                        t = t - coef_b[i] * poly[i - 1][j]
                    new.append(t * back)
                poly.append(new)
            size = [jnp.sqrt(gram[i, i]) for i in range(EARLY)]
            growth = size[-1] / size[-2]
            while len(size) < KRYLOV:
                size.append(size[-1] * growth)
            spread = []
            for i in range(KRYLOV):
                t = jnp.abs(poly[i][0]) * size[0]
                for j in range(1, i + 1):
                    t = t + jnp.abs(poly[i][j]) * size[j]
                spread.append(t)
            qown = []
            for i in range(KRYLOV + 1):
                for g in range(6):
                    t = poly[i][0] * z[0, g]
                    for j in range(1, min(i, KRYLOV - 1) + 1):
                        t = t + poly[i][j] * z[j, g]
                    q[i, g] = t
                t = poly[i][0] * own[0]
                for j in range(1, min(i, KRYLOV - 1) + 1):
                    t = t + poly[i][j] * own[j]
                qown.append(t)
            n = 0
            for i in range(KRYLOV):
                for j in range(i + 1):
                    pairs[n : n + 1, :] = dot_row(q, j, i, qown[j], qown[i])
                    n += 1
        for copy in halos(k):
            copy.wait_recv()
        halo_part(k, own[k])

    last = KRYLOV
    for g in range(6):
        q[last, g] = q[last, g] + poly[last][last] * z[last, g]
    for copy in edges(last - 1):
        copy.wait_recv()
    own_last = own_metal(metal_local(last - 1)) - walls[last - 1]
    qown[last] = qown[last] + poly[last][last] * own_last
    for j in range(last + 1):
        n = 21 + j
        pairs[n : n + 1, :] = dot_row(q, j, last, qown[j], qown[last])
    ra[1, pl.ds(f, 1), :] = packed()
    send_rows_flow(ra.at[1], KRYLOV + 1)
    rows_flow(ra.at[1], KRYLOV + 1).wait_recv()
    rb[1, pl.ds(s, 1), :] = jnp.sum(ra[1], axis=0, keepdims=True)
    send_rows_span(rb.at[1], 1)
    for k in range(KRYLOV):
        for copy in halos(k):
            copy.wait_send()
        for copy in edges(k):
            copy.wait_send()
    for k in range(KRYLOV - 1):
        rows_flow(wall.at[k], k).wait_send()
    rows_flow(place, KRYLOV - 1).wait_send()
    rows_flow(ra.at[0], KRYLOV).wait_send()
    rows_flow(ra.at[1], KRYLOV + 1).wait_send()
    rows_span(rb.at[0], 0).wait_send()
    rows_span(rb.at[1], 1).wait()
    unpack(jnp.sum(rb[1], axis=0, keepdims=True))
    gram = {}
    n = 0
    for i in range(KRYLOV + 1):
        for j in range(i + 1):
            gram[j, i] = scal[n : n + 1, :]
            n += 1
    r = {}
    low = None
    for i in range(KRYLOV + 1):
        scale = None
        for j in range(i, KRYLOV + 1):
            t = gram[i, j]
            for h in range(i):
                t = t - r[h, i] * r[h, j]
            if i == j:
                rel = t / gram[i, i]
                low = rel if low is None else jnp.minimum(low, rel)
                scale = lax.rsqrt(t)
            r[i, j] = t * scale
    zero = jnp.zeros((1, 128), f32)
    hess = [[zero] * KRYLOV for _ in range(KRYLOV + 1)]
    for j in range(KRYLOV):
        for i in range(j + 2):
            t = r[i, j + 1] * coef_b[j + 1]
            if i <= j:
                t = t + r[i, j] * coef_a[j]
            if i <= j - 1:
                t = t + r[i, j - 1] * coef_b[j]
            hess[i][j] = t
    y = least_squares(hess, r[0, 0] / poly[0][0], zero, KRYLOV)
    top = jnp.abs(y[0])
    total = jnp.abs(y[0]) * spread[0]
    for k in range(1, KRYLOV):
        top = jnp.maximum(top, jnp.abs(y[k]))
        total = total + jnp.abs(y[k]) * spread[k]
    fine = (low > 1e-2) & (total < 1e3 * top)
    ok_ref[...] = jnp.where(fine, 1.0, 0.0)
    for g in range(6):
        t = y[0] * q[0, g]
        for k in range(1, KRYLOV):
            t = t + y[k] * q[k, g]
        xf_ref[g] = t
    out = None
    for j in range(KRYLOV):
        c = y[j] * poly[j][j]
        for k in range(j + 1, KRYLOV):
            c = c + y[k] * poly[k][j]
        out = c * u[j] if out is None else out + c * u[j]
    xs_ref[...] = out


def shards(ns, nf, *args):
    rhs_fluid, rhs_solid = args[0], args[1]
    f32 = jnp.float32
    hbm = pl.BlockSpec(memory_space=pl.ANY)
    vmem = pl.BlockSpec(memory_space=pltpu.VMEM)
    smem = pl.BlockSpec(memory_space=pltpu.SMEM)
    dma = pltpu.SemaphoreType.DMA
    x_fluid, x_solid, ok = pl.pallas_call(
        functools.partial(kernel, ns, nf),
        name="gmres",
        out_shape=(
            jax.ShapeDtypeStruct(rhs_fluid.shape, f32),
            jax.ShapeDtypeStruct(rhs_solid.shape, f32),
            jax.ShapeDtypeStruct((1, 128), f32),
        ),
        in_specs=[hbm] * 5 + [smem] * 2 + [vmem],
        out_specs=(vmem, vmem, vmem),
        scratch_shapes=[
            pltpu.VMEM((KRYLOV + 1, 6, 2, 8, 128), f32),
            pltpu.VMEM((KRYLOV, 32, 128), f32),
            pltpu.VMEM((KRYLOV + 1, 6, 2, 8, 128), f32),
            pltpu.VMEM((6, 6, 2, 8, 128), f32),
            pltpu.VMEM((6, 2, 8, 128), f32),
            pltpu.VMEM((5, 2, 8, 128), f32),
            pltpu.VMEM((32, 128), f32),
            pltpu.VMEM((KRYLOV, 2, 6, 8, 128), f32),
            pltpu.VMEM((KRYLOV, 2, 16, 128), f32),
            pltpu.VMEM((KRYLOV, 2, 16, 128), f32),
            pltpu.VMEM((KRYLOV, 2, 8, 128), f32),
            pltpu.VMEM((KRYLOV - 1, 32, 128), f32),
            pltpu.VMEM((32, 128), f32),
            pltpu.VMEM((32, 128), f32),
            pltpu.VMEM((32, 128), f32),
            pltpu.VMEM((2, 32, 128), f32),
            pltpu.VMEM((2, 16, 128), f32),
            dma((5,)),
            dma((KRYLOV, 4)), dma((KRYLOV, 4)),
            dma((KRYLOV, 2)), dma((KRYLOV, 2)),
            dma((KRYLOV + 2,)), dma((KRYLOV + 2,)),
            dma((2,)), dma((2,)),
        ],
        compiler_params=pltpu.CompilerParams(
            collective_id=0, has_side_effects=True, vmem_limit_bytes=8 * 1024 * 1024
        ),
    )(*args)
    return lax.cond(
        ok[0, 0] > 0.5, lambda *a: (x_fluid, x_solid), lambda *a: arnoldi(*a), *args
    )


def solution(mesh):
    in_specs = (
        P(None, "span", "flow", None),
        P("span", None),
        P(None, None, "span", "flow", None),
        P(None, "span", "flow", None),
        P("span", None),
        P("span", "flow"),
        P("span", "flow"),
        P("span", "flow", None),
    )
    out_specs = (P(None, "span", "flow", None), P("span", None))
    return jax.shard_map(
        functools.partial(shards, mesh.shape["span"], mesh.shape["flow"]),
        mesh=mesh, in_specs=in_specs, out_specs=out_specs, check_vma=False,
    )
```

```python
import functools

import jax
import jax.numpy as jnp
from jax import lax
from jax.experimental import pallas as pl
from jax.experimental.pallas import tpu as pltpu
from jax.sharding import PartitionSpec as P

KRYLOV = 6
MESH = pl.DeviceIdType.MESH
EARLY = 4


def extended(shard, sides, width):
    for axis, dim in sides:
        count, length = (lax.axis_size(axis), shard.shape[dim])
        up = [(i, (i + 1) % count) for i in range(count - 1)]
        down = [(j, i) for i, j in up]
        last = lax.slice_in_dim(shard, length - width, length, axis=dim)
        first = lax.slice_in_dim(shard, 0, width, axis=dim)
        before = lax.ppermute(last, axis, up)
        after = lax.ppermute(first, axis, down)
        shard = jnp.concatenate([before, shard, after], axis=dim)
    return shard


def back_substitute(upper, rhs_g, steps):
    coeffs = [None] * steps
    for j in range(steps - 1, -1, -1):
        total = rhs_g[j]
        for k in range(j + 1, steps):
            total = total - upper[k][j] * coeffs[k]
        coeffs[j] = total / upper[j][j]
    return coeffs


def least_squares(hess, beta, zero, steps):
    cos_list, sin_list, upper = ([], [], [])
    rhs_g = [beta] + [zero for _ in range(steps)]
    for j in range(steps):
        column = [hess[i][j] for i in range(j + 2)]
        for i in range(j):
            top = cos_list[i] * column[i] + sin_list[i] * column[i + 1]
            column[i + 1] = -sin_list[i] * column[i] + cos_list[i] * column[i + 1]
            column[i] = top
        radius = jnp.sqrt(column[j] * column[j] + column[j + 1] * column[j + 1])
        cos_now = column[j] / radius
        sin_now = column[j + 1] / radius
        column[j] = radius
        rhs_g[j + 1] = -sin_now * rhs_g[j]
        rhs_g[j] = cos_now * rhs_g[j]
        cos_list.append(cos_now)
        sin_list.append(sin_now)
        upper.append(column[: j + 1])
    return back_substitute(upper, rhs_g, steps)


def arnoldi(rhs_fluid, rhs_solid, blocks, weights, kdiag, wall_fluid, wall_solid, wall_coef):
    rows_a = rhs_fluid.shape[1]
    rows_b = rhs_fluid.shape[2]
    width = rhs_fluid.shape[3]
    cells = rows_a * rows_b
    band_rows = rhs_solid.shape[0]
    patch_rows = wall_fluid[0]
    patch_metal = wall_solid[0]
    coef = wall_coef[0]
    fluid_pick = (jnp.arange(cells, dtype=jnp.int32)[:, None] == patch_rows[None, :]).astype(
        jnp.float32
    )
    metal_pick = (jnp.arange(band_rows, dtype=jnp.int32)[:, None] == patch_metal[None, :]).astype(
        jnp.float32
    )
    first_flow = (lax.axis_index("flow") == 0).astype(jnp.float32)
    highest = lax.Precision.HIGHEST

    def local_inner(left, right):
        return jnp.sum(left[0] * right[0]) + first_flow * jnp.sum(left[1] * right[1])

    beta = jnp.sqrt(
        lax.psum(local_inner((rhs_fluid, rhs_solid), (rhs_fluid, rhs_solid)), ("span", "flow"))
    )
    basis = [(rhs_fluid / beta, rhs_solid / beta)]
    hess = [[jnp.float32(0.0) for _ in range(KRYLOV)] for _ in range(KRYLOV + 1)]
    for j in range(KRYLOV):
        field = basis[j][0]
        metal_u = basis[j][1]
        padded = extended(field, (("span", 1), ("flow", 2)), 1)
        local = jnp.einsum("fgabc,gabc->fabc", blocks, field, precision=highest)
        beside = weights[0][None] * padded[:, :-2, 1:-1] + weights[1][None] * padded[:, 2:, 1:-1]
        beside = (
            beside
            + weights[2][None] * padded[:, 1:-1, :-2]
            + weights[3][None] * padded[:, 1:-1, 2:]
        )
        beside = (
            beside
            + weights[4][None] * jnp.roll(field, 1, axis=3)
            + weights[5][None] * jnp.roll(field, -1, axis=3)
        )
        metal_at = jnp.dot(metal_pick.T, metal_u, precision=highest)
        inflow = jnp.dot(fluid_pick, coef * metal_at, precision=highest).reshape(
            rows_a, rows_b, width
        )
        image_f = (local - beside).at[5].add(-inflow)
        wall_vals = coef * jnp.dot(fluid_pick.T, field[5].reshape(cells, width), precision=highest)
        sink = lax.psum(jnp.dot(metal_pick, wall_vals, precision=highest), "flow")
        upad = extended(metal_u, (("span", 0),), 1)
        beside_all = (
            upad[:-2] + upad[2:] + jnp.roll(metal_u, 1, axis=1) + jnp.roll(metal_u, -1, axis=1)
        )
        image_s = (4.0 + kdiag) * metal_u - beside_all - sink
        terms = jnp.stack([local_inner(basis[i], (image_f, image_s)) for i in range(j + 1)])
        values = lax.psum(terms, ("span", "flow"))
        for i in range(j + 1):
            image_f = image_f - values[i] * basis[i][0]
            image_s = image_s - values[i] * basis[i][1]
        rest = jnp.sqrt(
            lax.psum(local_inner((image_f, image_s), (image_f, image_s)), ("span", "flow"))
        )
        for i in range(j + 1):
            hess[i][j] = values[i]
        hess[j + 1][j] = rest
        basis.append((image_f / rest, image_s / rest))
    coeffs = least_squares(hess, beta, jnp.float32(0.0), KRYLOV)
    x_fluid = jnp.zeros_like(rhs_fluid)
    x_solid = jnp.zeros_like(rhs_solid)
    for j in range(KRYLOV):
        x_fluid = x_fluid + coeffs[j] * basis[j][0]
        x_solid = x_solid + coeffs[j] * basis[j][1]
    return (x_fluid, x_solid)


def kernel(
    ns, nf,
    rf_hbm, rs_hbm, bl_hbm, we_hbm, kd_hbm, wf_ref, ws_ref, wc_hbm,
    xf_ref, xs_ref, ok_ref, wc,
    z, u, q, qm, bl, we, wm, kd, hs, hq, sq, he, wall, place, pairs, mpairs, scal, ra, rb,
    in_sem, s_halo, r_halo, s_edge, r_edge, s_wall, r_wall, s_red, r_red,
):
    f32 = jnp.float32
    s = lax.axis_index("span")
    f = lax.axis_index("flow")
    up = (lax.rem(s + 1, ns), f)
    down = (lax.rem(s + ns - 1, ns), f)
    right = (s, lax.rem(f + 1, nf))
    left = (s, lax.rem(f + nf - 1, nf))

    loads = [
        pltpu.make_async_copy(rf_hbm, z.at[0], in_sem.at[0]),
        pltpu.make_async_copy(rs_hbm, u.at[0], in_sem.at[1]),
        pltpu.make_async_copy(we_hbm, we, in_sem.at[2]),
        pltpu.make_async_copy(bl_hbm, bl, in_sem.at[3]),
        pltpu.make_async_copy(kd_hbm, kd, in_sem.at[4]),
        pltpu.make_async_copy(wc_hbm, wc, in_sem.at[5]),
    ]
    for load in loads:
        load.start()

    barrier = pltpu.get_barrier_semaphore()

    def far_first(n, i):
        half = lax.div(i + 1, 2)
        return n // 2 + jnp.where(lax.rem(i, 2) == 1, half, -half)

    def greet_flow(i, c):
        to = (s, lax.rem(f + far_first(nf, i), nf))
        pl.semaphore_signal(barrier, inc=1, device_id=to, device_id_type=MESH)
        return c

    def greet_span(i, c):
        to = (lax.rem(s + far_first(ns, i), ns), f)
        pl.semaphore_signal(barrier, inc=1, device_id=to, device_id_type=MESH)
        return c

    lax.fori_loop(0, ns - 1, greet_span, 0)
    lax.fori_loop(0, nf - 1, greet_flow, 0)

    row8 = lax.broadcasted_iota(jnp.int32, (8, 128), 0)
    row16 = lax.broadcasted_iota(jnp.int32, (2, 8, 128), 0) * 8 + lax.broadcasted_iota(
        jnp.int32, (2, 8, 128), 1
    )
    row32 = lax.broadcasted_iota(jnp.int32, (32, 128), 0)
    lane32 = lax.broadcasted_iota(jnp.int32, (32, 128), 1)
    lane1 = lax.broadcasted_iota(jnp.int32, (1, 128), 1)
    eye = row32 == lane32
    loads[5].wait()
    patch = wf_ref[0, 0]
    metal_row = ws_ref[0, 0]
    coef = wc[0]
    wall_mask = jnp.where(row16 == patch, 1.0, 0.0).astype(f32)
    metal_mask = jnp.where(row32 == metal_row, 1.0, 0.0).astype(f32)
    place[pl.ds(f, 1), :] = jnp.where(lane1 == f, metal_row.astype(f32), 0.0)
    has_down = jnp.where(s > 0, 1.0, 0.0).astype(f32)
    has_up = jnp.where(s < ns - 1, 1.0, 0.0).astype(f32)
    has_left = jnp.where(f > 0, 1.0, 0.0).astype(f32)
    has_right = jnp.where(f < nf - 1, 1.0, 0.0).astype(f32)

    def send_rows_flow(buf, k):
        def one(i, c):
            pltpu.make_async_remote_copy(
                src_ref=buf.at[pl.ds(f, 1)], dst_ref=buf.at[pl.ds(f, 1)],
                send_sem=s_wall.at[k], recv_sem=r_wall.at[k],
                device_id=(s, lax.rem(f + far_first(nf, i), nf)), device_id_type=MESH,
            ).start()
            return c

        lax.fori_loop(0, nf - 1, one, 0)

    def rows_flow(buf, k):
        return pltpu.make_async_remote_copy(
            src_ref=buf.at[pl.ds(0, nf - 1)], dst_ref=buf.at[pl.ds(0, nf - 1)],
            send_sem=s_wall.at[k], recv_sem=r_wall.at[k], device_id=right, device_id_type=MESH,
        )

    def send_rows_span(buf, k):
        def one(i, c):
            pltpu.make_async_remote_copy(
                src_ref=buf.at[pl.ds(s, 1)], dst_ref=buf.at[pl.ds(s, 1)],
                send_sem=s_red.at[k], recv_sem=r_red.at[k],
                device_id=(lax.rem(s + far_first(ns, i), ns), f), device_id_type=MESH,
            ).start()
            return c

        lax.fori_loop(0, ns - 1, one, 0)

    def rows_span(buf, k):
        return pltpu.make_async_remote_copy(
            src_ref=buf.at[pl.ds(0, ns - 1)], dst_ref=buf.at[pl.ds(0, ns - 1)],
            send_sem=s_red.at[k], recv_sem=r_red.at[k], device_id=up, device_id_type=MESH,
        )

    def halos(k):
        def copy(n, src, dst, to):
            return pltpu.make_async_remote_copy(
                src_ref=src, dst_ref=dst, send_sem=s_halo.at[k, n], recv_sem=r_halo.at[k, n],
                device_id=to, device_id_type=MESH,
            )

        return [
            copy(0, z.at[k, :, 1], hs.at[k, 0], up),
            copy(1, z.at[k, :, 0], hs.at[k, 1], down),
            copy(2, sq.at[k, 0], hq.at[k, 0], right),
            copy(3, sq.at[k, 1], hq.at[k, 1], left),
        ]

    def edges(k):
        def copy(n, src, dst, to):
            return pltpu.make_async_remote_copy(
                src_ref=src, dst_ref=dst, send_sem=s_edge.at[k, n], recv_sem=r_edge.at[k, n],
                device_id=to, device_id_type=MESH,
            )

        return [
            copy(0, u.at[k, pl.ds(31, 1)], he.at[k, 0, pl.ds(0, 1)], up),
            copy(1, u.at[k, pl.ds(0, 1)], he.at[k, 1, pl.ds(0, 1)], down),
        ]

    def send_halos(k):
        out = halos(k)
        out[0].start()
        out[1].start()
        for g in range(6):
            for a in range(2):
                i = 2 * g + a
                sq[k, 0, i : i + 1, :] = z[k, g, a, 7:8, :]
                sq[k, 1, i : i + 1, :] = z[k, g, a, 0:1, :]
        out[2].start()
        out[3].start()

    def local_part(k):
        field = [z[k, g] for g in range(6)]
        for g in range(6):
            v = field[g]
            total = bl[g, 0] * field[0]
            for h in range(1, 6):
                total = total + bl[g, h] * field[h]
            total = total - we[4] * pltpu.roll(v, 1, 2) - we[5] * pltpu.roll(v, 127, 2)
            total = total - wm[0] * pltpu.roll(v, 1, 1) - wm[1] * pltpu.roll(v, 7, 1)
            z[k + 1, g, 0] = total[0] - we[1, 0] * v[1]
            z[k + 1, g, 1] = total[1] - we[0, 1] * v[0]

    def halo_part(k, metal_here):
        inflow = coef * metal_here
        for g in range(6):
            for a in range(2):
                i = 2 * g + a
                total = z[k + 1, g, a]
                if a == 0:
                    total = total - wm[4, 0] * hs[k, 0, g]
                else:
                    total = total - wm[4, 1] * hs[k, 1, g]
                total = total - wm[2, a] * hq[k, 0, i : i + 1, :] - wm[3, a] * hq[k, 1, i : i + 1, :]
                if g == 5:
                    total = total - wall_mask[a] * inflow
                z[k + 1, g, a] = total

    def own_metal(values):
        return jnp.sum(metal_mask * values, axis=0, keepdims=True)

    def wall_value(k):
        picked = wall_mask[0] * z[k, 5, 0] + wall_mask[1] * z[k, 5, 1]
        return coef * jnp.sum(picked, axis=0, keepdims=True)

    def metal_local(k):
        v = u[k]
        total = (4.0 + kd[...]) * v - pltpu.roll(v, 1, 1) - pltpu.roll(v, 127, 1)
        below = jnp.where(row32 == 0, has_down * he[k, 0, 0:1, :], pltpu.roll(v, 1, 0))
        above = jnp.where(row32 == 31, has_up * he[k, 1, 0:1, :], pltpu.roll(v, 31, 0))
        return total - below - above

    def dot_row(store, i, j):
        total = store[i, 0, 0] * store[j, 0, 0] + store[i, 0, 1] * store[j, 0, 1]
        for g in range(1, 6):
            total = total + store[i, g, 0] * store[j, g, 0] + store[i, g, 1] * store[j, g, 1]
        return jnp.sum(total, axis=0, keepdims=True)

    def metal_dot_row(i, j):
        t = qm[i] * qm[j]
        t = (t[0:8] + t[8:16]) + (t[16:24] + t[24:32])
        return jnp.sum(t, axis=0, keepdims=True)

    def packed(rows, low, high):
        sums = jnp.sum(rows[low:high, :], axis=1, keepdims=True)
        return jnp.sum(jnp.where(eye[low:high], sums, 0.0), axis=0, keepdims=True)

    def unpack(total):
        sums = jnp.sum(jnp.where(eye, total, 0.0), axis=1, keepdims=True)
        scal[...] = jnp.broadcast_to(sums, (32, 128))

    loads[0].wait()
    for g in range(6):
        for a in range(2):
            i = 2 * g + a
            sq[0, 0, i : i + 1, :] = z[0, g, a, 7:8, :]
            sq[0, 1, i : i + 1, :] = z[0, g, a, 0:1, :]
    sq[:, :, 12:16, :] = jnp.zeros((KRYLOV, 2, 4, 128), f32)
    pl.semaphore_wait(barrier, ns + nf - 2)
    for copy in halos(0):
        copy.start()
    loads[1].wait()
    for copy in edges(0):
        copy.start()
    pairs[...] = jnp.zeros((32, 128), f32)
    mpairs[...] = jnp.zeros((32, 128), f32)
    loads[2].wait()
    wm[0] = jnp.where(row8 == 0, 0.0, we[2])
    wm[1] = jnp.where(row8 == 7, 0.0, we[3])
    wm[2] = jnp.where(row8 == 0, has_left * we[2], 0.0)
    wm[3] = jnp.where(row8 == 7, has_right * we[3], 0.0)
    wm[4, 0] = has_down * we[0, 0]
    wm[4, 1] = has_up * we[1, 1]
    loads[3].wait()
    loads[4].wait()

    own = []
    pick = None
    coef_a = coef_b = None
    for k in range(KRYLOV):
        if k > 0:
            send_halos(k)
        mine = wall_value(k)
        wall[k, pl.ds(f, 1), :] = mine
        send_rows_flow(wall.at[k], k)
        if k == 0:
            send_rows_flow(place, KRYLOV)
        local_part(k)
        if k > 0:
            if k == 1:
                rows_flow(place, KRYLOV).wait_recv()
                places = jnp.sum(place[...], axis=0, keepdims=True)
                pick = jnp.where((row32.astype(f32) == places) & (lane32 < 32), 1.0, 0.0)[:, 0:32]
            rows_flow(wall.at[k - 1], k - 1).wait_recv()
            sink = jnp.dot(
                pick, wall[k - 1], precision=lax.Precision.HIGHEST, preferred_element_type=f32
            )
            for copy in edges(k - 1):
                copy.wait_recv()
            u[k] = metal_local(k - 1) - sink
            for copy in edges(k):
                copy.start()
        own.append(own_metal(u[k]))
        if k == EARLY - 1:
            n = 0
            for i in range(EARLY):
                for j in range(i, EARLY):
                    pairs[n : n + 1, :] = dot_row(z, i, j) + own[i] * own[j]
                    n += 1
            ra[0, pl.ds(f, 1), :] = packed(pairs, 0, 32)
            send_rows_flow(ra.at[0], KRYLOV + 1)
        if k == EARLY:
            rows_flow(ra.at[0], KRYLOV + 1).wait_recv()
            rb[0, pl.ds(s, 1), :] = jnp.sum(ra[0], axis=0, keepdims=True)
            send_rows_span(rb.at[0], 0)
        if k == EARLY + 1:
            rows_span(rb.at[0], 0).wait_recv()
            unpack(jnp.sum(rb[0], axis=0, keepdims=True))
            gram = {}
            n = 0
            for i in range(EARLY):
                for j in range(i, EARLY):
                    gram[i, j] = scal[n : n + 1, :]
                    n += 1
            r = {}
            inv = []
            trust = []
            for i in range(EARLY):
                for j in range(i, EARLY):
                    t = gram[i, j]
                    for h in range(i):
                        t = t - r[h, i] * r[h, j]
                    if i == j:
                        floor = gram[i, i] * 1e-5
                        trust.append(t > floor)
                        t = jnp.maximum(t, floor)
                        inv.append(lax.rsqrt(t))
                    r[i, j] = t * inv[i]
            ratio = [r[i, i + 1] * inv[i] for i in range(EARLY - 1)]
            coef_a = [ratio[0]]
            coef_b = [None, r[1, 1] * inv[0]]
            good = trust[1]
            for i in range(1, EARLY - 1):
                good = good & trust[i + 1]
                coef_a.append(jnp.where(good, ratio[i] - ratio[i - 1], coef_a[i - 1]))
                guess = coef_b[1] * 1.22
                coef_b.append(jnp.where(good, r[i + 1, i + 1] * inv[i], guess))
            while len(coef_a) < KRYLOV:
                coef_a.append(coef_a[-1])
            while len(coef_b) < KRYLOV + 1:
                coef_b.append(coef_b[-1])
            poly = [[inv[0]]]
            for i in range(KRYLOV):
                back = 1.0 / coef_b[i + 1]
                new = []
                for j in range(i + 2):
                    t = None
                    if j >= 1:
                        t = poly[i][j - 1]
                    if j <= i:
                        t = -coef_a[i] * poly[i][j] if t is None else t - coef_a[i] * poly[i][j]
                    if i >= 1 and j <= i - 1:
                        t = t - coef_b[i] * poly[i - 1][j]
                    new.append(t * back)
                poly.append(new)
            size = [jnp.sqrt(gram[i, i]) for i in range(EARLY)]
            growth = size[-1] / size[-2]
            while len(size) < KRYLOV:
                size.append(size[-1] * growth)
            spread = []
            for i in range(KRYLOV):
                t = jnp.abs(poly[i][0]) * size[0]
                for j in range(1, i + 1):
                    t = t + jnp.abs(poly[i][j]) * size[j]
                spread.append(t)
            for i in range(KRYLOV + 1):
                for g in range(6):
                    t = poly[i][0] * z[0, g]
                    for j in range(1, min(i, KRYLOV - 1) + 1):
                        t = t + poly[i][j] * z[j, g]
                    q[i, g] = t
                t = poly[i][0] * u[0]
                for j in range(1, min(i, KRYLOV - 1) + 1):
                    t = t + poly[i][j] * u[j]
                qm[i] = t
            n = 0
            for i in range(KRYLOV):
                for j in range(i + 1):
                    pairs[n : n + 1, :] = dot_row(q, j, i)
                    mpairs[n : n + 1, :] = metal_dot_row(j, i)
                    n += 1
            done = packed(pairs, 0, 24)
            metal_done = packed(mpairs, 0, 24)
        for copy in halos(k):
            copy.wait_recv()
        halo_part(k, own[k])

    last = KRYLOV
    for g in range(6):
        q[last, g] = q[last, g] + poly[last][last] * z[last, g]
    for j in range(last + 1):
        pairs[24 + j : 25 + j, :] = dot_row(q, j, last)
    ra[1, pl.ds(f, 1), :] = done + packed(pairs, 24, 32)
    send_rows_flow(ra.at[1], KRYLOV + 2)
    rows_flow(wall.at[last - 1], last - 1).wait_recv()
    sink = jnp.dot(
        pick, wall[last - 1], precision=lax.Precision.HIGHEST, preferred_element_type=f32
    )
    for copy in edges(last - 1):
        copy.wait_recv()
    qm[last] = qm[last] + poly[last][last] * (metal_local(last - 1) - sink)
    for j in range(last + 1):
        mpairs[24 + j : 25 + j, :] = metal_dot_row(j, last)
    metal_done = metal_done + packed(mpairs, 24, 32)
    rows_flow(ra.at[1], KRYLOV + 2).wait_recv()
    rb[1, pl.ds(s, 1), :] = jnp.sum(ra[1], axis=0, keepdims=True) + metal_done
    send_rows_span(rb.at[1], 1)
    for k in range(KRYLOV):
        for copy in halos(k):
            copy.wait_send()
        for copy in edges(k):
            copy.wait_send()
    for k in range(KRYLOV):
        rows_flow(wall.at[k], k).wait_send()
    rows_flow(place, KRYLOV).wait_send()
    rows_flow(ra.at[0], KRYLOV + 1).wait_send()
    rows_flow(ra.at[1], KRYLOV + 2).wait_send()
    rows_span(rb.at[0], 0).wait_send()
    rows_span(rb.at[1], 1).wait()
    unpack(jnp.sum(rb[1], axis=0, keepdims=True))
    gram = {}
    n = 0
    for i in range(KRYLOV + 1):
        for j in range(i + 1):
            m = 24 + j if i == KRYLOV else n
            gram[j, i] = scal[m : m + 1, :]
            n += 1
    r = {}
    low = None
    for i in range(KRYLOV + 1):
        scale = None
        for j in range(i, KRYLOV + 1):
            t = gram[i, j]
            for h in range(i):
                t = t - r[h, i] * r[h, j]
            if i == j:
                rel = t / gram[i, i]
                low = rel if low is None else jnp.minimum(low, rel)
                scale = lax.rsqrt(t)
            r[i, j] = t * scale
    zero = jnp.zeros((1, 128), f32)
    hess = [[zero] * KRYLOV for _ in range(KRYLOV + 1)]
    for j in range(KRYLOV):
        for i in range(j + 2):
            t = r[i, j + 1] * coef_b[j + 1]
            if i <= j:
                t = t + r[i, j] * coef_a[j]
            if i <= j - 1:
                t = t + r[i, j - 1] * coef_b[j]
            hess[i][j] = t
    y = least_squares(hess, r[0, 0] / poly[0][0], zero, KRYLOV)
    top = jnp.abs(y[0])
    total = jnp.abs(y[0]) * spread[0]
    for k in range(1, KRYLOV):
        top = jnp.maximum(top, jnp.abs(y[k]))
        total = total + jnp.abs(y[k]) * spread[k]
    fine = (low > 1e-2) & (total < 1e3 * top)
    ok_ref[...] = jnp.where(fine, 1.0, 0.0)
    for g in range(6):
        t = y[0] * q[0, g]
        for k in range(1, KRYLOV):
            t = t + y[k] * q[k, g]
        xf_ref[g] = t
    out = None
    for j in range(KRYLOV):
        c = y[j] * poly[j][j]
        for k in range(j + 1, KRYLOV):
            c = c + y[k] * poly[k][j]
        out = c * u[j] if out is None else out + c * u[j]
    xs_ref[...] = out


def shards(ns, nf, *args):
    rhs_fluid, rhs_solid = args[0], args[1]
    f32 = jnp.float32
    hbm = pl.BlockSpec(memory_space=pltpu.HBM)
    vmem = pl.BlockSpec(memory_space=pltpu.VMEM)
    smem = pl.BlockSpec(memory_space=pltpu.SMEM)
    dma = pltpu.SemaphoreType.DMA
    x_fluid, x_solid, ok, coef = pl.pallas_call(
        functools.partial(kernel, ns, nf),
        name="gmres",
        out_shape=(
            jax.ShapeDtypeStruct(rhs_fluid.shape, f32),
            jax.ShapeDtypeStruct(rhs_solid.shape, f32),
            jax.ShapeDtypeStruct((1, 128), f32),
            jax.ShapeDtypeStruct(args[-1].shape, f32),
        ),
        in_specs=[hbm] * 5 + [smem] * 2 + [hbm],
        out_specs=(vmem,) * 4,
        scratch_shapes=[
            pltpu.VMEM((KRYLOV + 1, 6, 2, 8, 128), f32),
            pltpu.VMEM((KRYLOV, 32, 128), f32),
            pltpu.VMEM((KRYLOV + 1, 6, 2, 8, 128), f32),
            pltpu.VMEM((KRYLOV + 1, 32, 128), f32),
            pltpu.VMEM((6, 6, 2, 8, 128), f32),
            pltpu.VMEM((6, 2, 8, 128), f32),
            pltpu.VMEM((5, 2, 8, 128), f32),
            pltpu.VMEM((32, 128), f32),
            pltpu.VMEM((KRYLOV, 2, 6, 8, 128), f32),
            pltpu.VMEM((KRYLOV, 2, 16, 128), f32),
            pltpu.VMEM((KRYLOV, 2, 16, 128), f32),
            pltpu.VMEM((KRYLOV, 2, 8, 128), f32),
            pltpu.VMEM((KRYLOV, 32, 128), f32),
            pltpu.VMEM((32, 128), f32),
            pltpu.VMEM((32, 128), f32),
            pltpu.VMEM((32, 128), f32),
            pltpu.VMEM((32, 128), f32),
            pltpu.VMEM((2, 32, 128), f32),
            pltpu.VMEM((2, 16, 128), f32),
            dma((6,)),
            dma((KRYLOV, 4)), dma((KRYLOV, 4)),
            dma((KRYLOV, 2)), dma((KRYLOV, 2)),
            dma((KRYLOV + 3,)), dma((KRYLOV + 3,)),
            dma((2,)), dma((2,)),
        ],
        compiler_params=pltpu.CompilerParams(
            collective_id=0, has_side_effects=True, vmem_limit_bytes=8 * 1024 * 1024
        ),
    )(*args)
    return lax.cond(
        ok[0, 0] > 0.5, lambda *a: (x_fluid, x_solid), lambda *a: arnoldi(*a), *args[:-1], coef
    )


def solution(mesh):
    in_specs = (
        P(None, "span", "flow", None),
        P("span", None),
        P(None, None, "span", "flow", None),
        P(None, "span", "flow", None),
        P("span", None),
        P("span", "flow"),
        P("span", "flow"),
        P("span", "flow", None),
    )
    out_specs = (P(None, "span", "flow", None), P("span", None))
    return jax.shard_map(
        functools.partial(shards, mesh.shape["span"], mesh.shape["flow"]),
        mesh=mesh, in_specs=in_specs, out_specs=out_specs, check_vma=False,
    )
```

```python
import functools

import jax
import jax.numpy as jnp
from jax import lax
from jax.experimental import pallas as pl
from jax.experimental.pallas import tpu as pltpu
from jax.sharding import PartitionSpec as P

KRYLOV = 6
MESH = pl.DeviceIdType.MESH
EARLY = 3
PLAN = ((0, 1), (1, 1), (2, 1), (3, 1), (4, 2))
PAIRS = tuple(k for k, width in PLAN if width == 2)
CHUNKS = ((0, 2), (2, 4), (4, 6))


def extended(shard, sides, width):
    for axis, dim in sides:
        count, length = (lax.axis_size(axis), shard.shape[dim])
        up = [(i, (i + 1) % count) for i in range(count - 1)]
        down = [(j, i) for i, j in up]
        last = lax.slice_in_dim(shard, length - width, length, axis=dim)
        first = lax.slice_in_dim(shard, 0, width, axis=dim)
        before = lax.ppermute(last, axis, up)
        after = lax.ppermute(first, axis, down)
        shard = jnp.concatenate([before, shard, after], axis=dim)
    return shard


def back_substitute(upper, rhs_g, steps):
    coeffs = [None] * steps
    for j in range(steps - 1, -1, -1):
        total = rhs_g[j]
        for k in range(j + 1, steps):
            total = total - upper[k][j] * coeffs[k]
        coeffs[j] = total / upper[j][j]
    return coeffs


def least_squares(hess, beta, zero, steps):
    cos_list, sin_list, upper = ([], [], [])
    rhs_g = [beta] + [zero for _ in range(steps)]
    for j in range(steps):
        column = [hess[i][j] for i in range(j + 2)]
        for i in range(j):
            top = cos_list[i] * column[i] + sin_list[i] * column[i + 1]
            column[i + 1] = -sin_list[i] * column[i] + cos_list[i] * column[i + 1]
            column[i] = top
        radius = jnp.sqrt(column[j] * column[j] + column[j + 1] * column[j + 1])
        cos_now = column[j] / radius
        sin_now = column[j + 1] / radius
        column[j] = radius
        rhs_g[j + 1] = -sin_now * rhs_g[j]
        rhs_g[j] = cos_now * rhs_g[j]
        cos_list.append(cos_now)
        sin_list.append(sin_now)
        upper.append(column[: j + 1])
    return back_substitute(upper, rhs_g, steps)


def arnoldi(rhs_fluid, rhs_solid, blocks, weights, kdiag, wall_fluid, wall_solid, wall_coef):
    rows_a = rhs_fluid.shape[1]
    rows_b = rhs_fluid.shape[2]
    width = rhs_fluid.shape[3]
    cells = rows_a * rows_b
    band_rows = rhs_solid.shape[0]
    patch_rows = wall_fluid[0]
    patch_metal = wall_solid[0]
    coef = wall_coef[0]
    fluid_pick = (jnp.arange(cells, dtype=jnp.int32)[:, None] == patch_rows[None, :]).astype(
        jnp.float32
    )
    metal_pick = (jnp.arange(band_rows, dtype=jnp.int32)[:, None] == patch_metal[None, :]).astype(
        jnp.float32
    )
    first_flow = (lax.axis_index("flow") == 0).astype(jnp.float32)
    highest = lax.Precision.HIGHEST

    def local_inner(left, right):
        return jnp.sum(left[0] * right[0]) + first_flow * jnp.sum(left[1] * right[1])

    beta = jnp.sqrt(
        lax.psum(local_inner((rhs_fluid, rhs_solid), (rhs_fluid, rhs_solid)), ("span", "flow"))
    )
    basis = [(rhs_fluid / beta, rhs_solid / beta)]
    hess = [[jnp.float32(0.0) for _ in range(KRYLOV)] for _ in range(KRYLOV + 1)]
    for j in range(KRYLOV):
        field = basis[j][0]
        metal_u = basis[j][1]
        padded = extended(field, (("span", 1), ("flow", 2)), 1)
        local = jnp.einsum("fgabc,gabc->fabc", blocks, field, precision=highest)
        beside = weights[0][None] * padded[:, :-2, 1:-1] + weights[1][None] * padded[:, 2:, 1:-1]
        beside = (
            beside
            + weights[2][None] * padded[:, 1:-1, :-2]
            + weights[3][None] * padded[:, 1:-1, 2:]
        )
        beside = (
            beside
            + weights[4][None] * jnp.roll(field, 1, axis=3)
            + weights[5][None] * jnp.roll(field, -1, axis=3)
        )
        metal_at = jnp.dot(metal_pick.T, metal_u, precision=highest)
        inflow = jnp.dot(fluid_pick, coef * metal_at, precision=highest).reshape(
            rows_a, rows_b, width
        )
        image_f = (local - beside).at[5].add(-inflow)
        wall_vals = coef * jnp.dot(fluid_pick.T, field[5].reshape(cells, width), precision=highest)
        sink = lax.psum(jnp.dot(metal_pick, wall_vals, precision=highest), "flow")
        upad = extended(metal_u, (("span", 0),), 1)
        beside_all = (
            upad[:-2] + upad[2:] + jnp.roll(metal_u, 1, axis=1) + jnp.roll(metal_u, -1, axis=1)
        )
        image_s = (4.0 + kdiag) * metal_u - beside_all - sink
        terms = jnp.stack([local_inner(basis[i], (image_f, image_s)) for i in range(j + 1)])
        values = lax.psum(terms, ("span", "flow"))
        for i in range(j + 1):
            image_f = image_f - values[i] * basis[i][0]
            image_s = image_s - values[i] * basis[i][1]
        rest = jnp.sqrt(
            lax.psum(local_inner((image_f, image_s), (image_f, image_s)), ("span", "flow"))
        )
        for i in range(j + 1):
            hess[i][j] = values[i]
        hess[j + 1][j] = rest
        basis.append((image_f / rest, image_s / rest))
    coeffs = least_squares(hess, beta, jnp.float32(0.0), KRYLOV)
    x_fluid = jnp.zeros_like(rhs_fluid)
    x_solid = jnp.zeros_like(rhs_solid)
    for j in range(KRYLOV):
        x_fluid = x_fluid + coeffs[j] * basis[j][0]
        x_solid = x_solid + coeffs[j] * basis[j][1]
    return (x_fluid, x_solid)


def kernel(
    ns, nf,
    rf_hbm, rs_hbm, bl_hbm, we_hbm, kd_hbm, wf_ref, ws_ref, wc_hbm,
    xf_ref, xs_ref, ok_ref, wc,
    z, u, q, qm, bl, we, wm, kd, hs, hq, sq, he, wall, place, pairs, mpairs, scal, ra, rb,
    tl, th, sb, pk, cb, ir, ib, blo, bhi, bs, pbs, wl, wh, wsr, pws, wn, pid, el, eh, es,
    in_sem, s_halo, r_halo, s_edge, r_edge, s_wall, r_wall, s_red, r_red, s_pair, r_pair, s_once, r_once,
):
    f32 = jnp.float32
    s = lax.axis_index("span")
    f = lax.axis_index("flow")
    up = (lax.rem(s + 1, ns), f)
    down = (lax.rem(s + ns - 1, ns), f)
    right = (s, lax.rem(f + 1, nf))
    left = (s, lax.rem(f + nf - 1, nf))
    corners = ((up[0], right[1]), (down[0], right[1]), (up[0], left[1]), (down[0], left[1]))

    loads = [
        pltpu.make_async_copy(rf_hbm, z.at[0], in_sem.at[0]),
        pltpu.make_async_copy(rs_hbm, u.at[0], in_sem.at[1]),
        pltpu.make_async_copy(we_hbm, we, in_sem.at[2]),
        pltpu.make_async_copy(bl_hbm, bl, in_sem.at[3]),
        pltpu.make_async_copy(kd_hbm, kd, in_sem.at[4]),
        pltpu.make_async_copy(wc_hbm, wc, in_sem.at[5]),
    ]
    for load in loads:
        load.start()

    cb[...] = jnp.zeros((len(PAIRS), 6, 8, 128), f32)

    barrier = pltpu.get_barrier_semaphore()

    def far_first(n, i):
        half = lax.div(i + 1, 2)
        return n // 2 + jnp.where(lax.rem(i, 2) == 1, half, -half)

    def greet_flow(i, c):
        to = (s, lax.rem(f + far_first(nf, i), nf))
        pl.semaphore_signal(barrier, inc=1, device_id=to, device_id_type=MESH)
        return c

    def greet_span(i, c):
        to = (lax.rem(s + far_first(ns, i), ns), f)
        pl.semaphore_signal(barrier, inc=1, device_id=to, device_id_type=MESH)
        return c

    for to in corners:
        pl.semaphore_signal(barrier, inc=1, device_id=to, device_id_type=MESH)
    lax.fori_loop(0, ns - 1, greet_span, 0)
    lax.fori_loop(0, nf - 1, greet_flow, 0)

    row8 = lax.broadcasted_iota(jnp.int32, (8, 128), 0)
    row16 = lax.broadcasted_iota(jnp.int32, (2, 8, 128), 0) * 8 + lax.broadcasted_iota(
        jnp.int32, (2, 8, 128), 1
    )
    row32 = lax.broadcasted_iota(jnp.int32, (32, 128), 0)
    lane32 = lax.broadcasted_iota(jnp.int32, (32, 128), 1)
    lane1 = lax.broadcasted_iota(jnp.int32, (1, 128), 1)
    eye = row32 == lane32
    loads[5].wait()
    patch = wf_ref[0, 0]
    metal_row = ws_ref[0, 0]
    coef = wc[0]
    wall_mask = jnp.where(row16 == patch, 1.0, 0.0).astype(f32)
    metal_mask = jnp.where(row32 == metal_row, 1.0, 0.0).astype(f32)
    place[pl.ds(f, 1), :] = jnp.where(lane1 == f, metal_row.astype(f32), 0.0)
    has_down = jnp.where(s > 0, 1.0, 0.0).astype(f32)
    has_up = jnp.where(s < ns - 1, 1.0, 0.0).astype(f32)
    has_left = jnp.where(f > 0, 1.0, 0.0).astype(f32)
    has_right = jnp.where(f < nf - 1, 1.0, 0.0).astype(f32)

    def send_rows_flow(buf, k):
        def one(i, c):
            pltpu.make_async_remote_copy(
                src_ref=buf.at[pl.ds(f, 1)], dst_ref=buf.at[pl.ds(f, 1)],
                send_sem=s_wall.at[k], recv_sem=r_wall.at[k],
                device_id=(s, lax.rem(f + far_first(nf, i), nf)), device_id_type=MESH,
            ).start()
            return c

        lax.fori_loop(0, nf - 1, one, 0)

    def rows_flow(buf, k):
        return pltpu.make_async_remote_copy(
            src_ref=buf.at[pl.ds(0, nf - 1)], dst_ref=buf.at[pl.ds(0, nf - 1)],
            send_sem=s_wall.at[k], recv_sem=r_wall.at[k], device_id=right, device_id_type=MESH,
        )

    def send_rows_span(buf, k):
        def one(i, c):
            pltpu.make_async_remote_copy(
                src_ref=buf.at[pl.ds(s, 1)], dst_ref=buf.at[pl.ds(s, 1)],
                send_sem=s_red.at[k], recv_sem=r_red.at[k],
                device_id=(lax.rem(s + far_first(ns, i), ns), f), device_id_type=MESH,
            ).start()
            return c

        lax.fori_loop(0, ns - 1, one, 0)

    def rows_span(buf, k):
        return pltpu.make_async_remote_copy(
            src_ref=buf.at[pl.ds(0, ns - 1)], dst_ref=buf.at[pl.ds(0, ns - 1)],
            send_sem=s_red.at[k], recv_sem=r_red.at[k], device_id=up, device_id_type=MESH,
        )

    def halos(k):
        def copy(n, src, dst, to):
            return pltpu.make_async_remote_copy(
                src_ref=src, dst_ref=dst, send_sem=s_halo.at[k, n], recv_sem=r_halo.at[k, n],
                device_id=to, device_id_type=MESH,
            )

        return [
            copy(0, z.at[k, :, 1], hs.at[k, 0], up),
            copy(1, z.at[k, :, 0], hs.at[k, 1], down),
            copy(2, sq.at[k, 0], hq.at[k, 0], right),
            copy(3, sq.at[k, 1], hq.at[k, 1], left),
        ]

    def edges(k):
        def copy(n, src, dst, to):
            return pltpu.make_async_remote_copy(
                src_ref=src, dst_ref=dst, send_sem=s_edge.at[k, n], recv_sem=r_edge.at[k, n],
                device_id=to, device_id_type=MESH,
            )

        return [
            copy(0, u.at[k, pl.ds(31, 1)], he.at[k, 0, pl.ds(0, 1)], up),
            copy(1, u.at[k, pl.ds(0, 1)], he.at[k, 1, pl.ds(0, 1)], down),
        ]

    def send_halos(k):
        out = halos(k)
        out[0].start()
        out[1].start()
        for g in range(6):
            for a in range(2):
                i = 2 * g + a
                sq[k, 0, i : i + 1, :] = z[k, g, a, 7:8, :]
                sq[k, 1, i : i + 1, :] = z[k, g, a, 0:1, :]
        out[2].start()
        out[3].start()

    def remote(src, dst, send, recv, to):
        return pltpu.make_async_remote_copy(
            src_ref=src, dst_ref=dst, send_sem=send, recv_sem=recv, device_id=to, device_id_type=MESH
        )

    def pair_copies(k):
        p = PAIRS.index(k)

        def copy(n, src, dst, to):
            return remote(src, dst, s_pair.at[p, n], r_pair.at[p, n], to)

        return [
            copy(0, z.at[k], tl.at[p], up),
            copy(1, z.at[k], th.at[p], down),
            copy(2, pk.at[p, :, pl.ds(4, 4)], sb.at[p, :, pl.ds(0, 4)], right),
            copy(3, pk.at[p, :, pl.ds(0, 4)], sb.at[p, :, pl.ds(4, 4)], left),
            copy(4, pk.at[p, :, pl.ds(5, 1)], cb.at[p, :, pl.ds(0, 1)], corners[0]),
            copy(5, pk.at[p, :, pl.ds(4, 1)], cb.at[p, :, pl.ds(1, 1)], corners[1]),
            copy(6, pk.at[p, :, pl.ds(1, 1)], cb.at[p, :, pl.ds(4, 1)], corners[2]),
            copy(7, pk.at[p, :, pl.ds(0, 1)], cb.at[p, :, pl.ds(5, 1)], corners[3]),
        ]

    def inflow_copies(k):
        p = PAIRS.index(k)
        return [
            remote(
                ir.at[p, pl.ds(0, 1)], ib.at[p, pl.ds(n, 1)],
                s_pair.at[p, 8 + n], r_pair.at[p, 8 + n], to,
            )
            for n, to in enumerate((up, down, right, left))
        ]

    def once_copies(chunk):
        def copy(n, src, dst, to):
            return remote(src, dst, s_once.at[n], r_once.at[n], to)

        low, high = CHUNKS[chunk]
        rows = pl.ds(low, high - low)
        out = [
            copy(2 * chunk, bl.at[rows, :, 1], blo.at[rows], up),
            copy(2 * chunk + 1, bl.at[rows, :, 0], bhi.at[rows], down),
        ]
        if chunk == 0:
            n = 2 * len(CHUNKS)
            out += [
                copy(n, we.at[:, 1], wl, up),
                copy(n + 1, we.at[:, 0], wh, down),
                copy(n + 2, pbs.at[:, :, pl.ds(4, 4)], bs.at[:, :, pl.ds(0, 4)], right),
                copy(n + 3, pbs.at[:, :, pl.ds(0, 4)], bs.at[:, :, pl.ds(4, 4)], left),
                copy(n + 4, pws.at[:, pl.ds(4, 4)], wsr.at[:, pl.ds(0, 4)], right),
                copy(n + 5, pws.at[:, pl.ds(0, 4)], wsr.at[:, pl.ds(4, 4)], left),
            ]
            out += [
                copy(n + 6 + m, pid.at[pl.ds(4, 1)], pid.at[pl.ds(m, 1)], to)
                for m, to in enumerate((up, down, right, left))
            ]
        return out

    PACK = ((0, 0), (0, 1), (1, 0), (1, 1), (7, 0), (7, 1), (6, 0), (6, 1))

    def pack_once():
        def one(i, c):
            for g in range(6):
                for m, (b, a) in enumerate(PACK):
                    pbs[i, g, m : m + 1, :] = bl[i, g, a, b : b + 1, :]
            for m, (b, a) in enumerate(PACK):
                pws[i, m : m + 1, :] = we[i, a, b : b + 1, :]
            return c

        lax.fori_loop(0, 6, one, 0)
        pid[4:5, :] = jnp.broadcast_to(patch.astype(f32), (1, 128))

    def prepare_pairs():
        wn[0] = wl[2] * jnp.where(row8 == 0, has_left, 1.0)
        wn[1] = wl[3] * jnp.where(row8 == 7, has_right, 1.0)
        wn[2] = wh[2] * jnp.where(row8 == 0, has_left, 1.0)
        wn[3] = wh[3] * jnp.where(row8 == 7, has_right, 1.0)
        wn[4] = wsr[0] * jnp.where((row8 == 0) | (row8 == 4), has_down, 1.0)
        wn[5] = wsr[1] * jnp.where((row8 == 1) | (row8 == 5), has_up, 1.0)
        wn[6] = jnp.where(row8 < 4, wsr[2], wsr[3])
        wn[7] = jnp.where(row8 < 4, wsr[3], wsr[2])
        here = row8.astype(f32)
        wn[8] = jnp.where(here + 8.0 == pid[0:1, :], 1.0, 0.0)
        wn[9] = jnp.where(here == pid[1:2, :], 1.0, 0.0)
        side = jnp.where((row8 == 0) & (pid[2:3, :] == 7.0), 1.0, 0.0)
        side = side + jnp.where((row8 == 1) & (pid[2:3, :] == 15.0), 1.0, 0.0)
        side = side + jnp.where((row8 == 4) & (pid[3:4, :] == 0.0), 1.0, 0.0)
        wn[10] = side + jnp.where((row8 == 5) & (pid[3:4, :] == 8.0), 1.0, 0.0)

    def beside_cells(k):
        p = PAIRS.index(k)
        odd = (row8 & 1) == 1
        for g in range(6):
            v = tl[p, g, 1]
            total = blo[g, 0] * tl[p, 0, 1]
            for h in range(1, 6):
                total = total + blo[g, h] * tl[p, h, 1]
            total = total - wl[0] * tl[p, g, 0] - wl[1] * z[k, g, 0]
            total = total - wn[0] * jnp.where(row8 == 0, cb[p, g, 0:1, :], pltpu.roll(v, 1, 0))
            total = total - wn[1] * jnp.where(row8 == 7, cb[p, g, 4:5, :], pltpu.roll(v, 7, 0))
            el[g] = total - wl[4] * pltpu.roll(v, 1, 1) - wl[5] * pltpu.roll(v, 127, 1)
            v = th[p, g, 0]
            total = bhi[g, 0] * th[p, 0, 0]
            for h in range(1, 6):
                total = total + bhi[g, h] * th[p, h, 0]
            total = total - wh[0] * z[k, g, 1] - wh[1] * th[p, g, 1]
            total = total - wn[2] * jnp.where(row8 == 0, cb[p, g, 1:2, :], pltpu.roll(v, 1, 0))
            total = total - wn[3] * jnp.where(row8 == 7, cb[p, g, 5:6, :], pltpu.roll(v, 7, 0))
            eh[g] = total - wh[4] * pltpu.roll(v, 1, 1) - wh[5] * pltpu.roll(v, 127, 1)
            v = sb[p, g]
            total = bs[g, 0] * sb[p, 0]
            for h in range(1, 6):
                total = total + bs[g, h] * sb[p, h]
            total = total - wn[4] * jnp.where(odd, pltpu.roll(v, 1, 0), cb[p, g])
            total = total - wn[5] * jnp.where(odd, cb[p, g], pltpu.roll(v, 7, 0))
            total = total - wn[6] * pltpu.roll(v, 6, 0) - wn[7] * pk[p, g]
            es[g] = total - wsr[4] * pltpu.roll(v, 1, 1) - wsr[5] * pltpu.roll(v, 127, 1)

    def beside_inflow(k):
        p = PAIRS.index(k)
        el[5] = el[5] - wn[8] * ib[p, 0:1, :]
        eh[5] = eh[5] - wn[9] * ib[p, 1:2, :]
        es[5] = es[5] - wn[10] * jnp.where(row8 < 4, ib[p, 2:3, :], ib[p, 3:4, :])

    def local_part(k):
        field = [z[k, g] for g in range(6)]
        for g in range(6):
            v = field[g]
            total = bl[g, 0] * field[0]
            for h in range(1, 6):
                total = total + bl[g, h] * field[h]
            total = total - we[4] * pltpu.roll(v, 1, 2) - we[5] * pltpu.roll(v, 127, 2)
            total = total - wm[0] * pltpu.roll(v, 1, 1) - wm[1] * pltpu.roll(v, 7, 1)
            z[k + 1, g, 0] = total[0] - we[1, 0] * v[1]
            z[k + 1, g, 1] = total[1] - we[0, 1] * v[0]

    def halo_part(k, metal_here, low, high, west, east):
        inflow = coef * metal_here
        for g in range(6):
            for a in range(2):
                total = z[k + 1, g, a]
                if a == 0:
                    total = total - wm[4, 0] * low(g)
                else:
                    total = total - wm[4, 1] * high(g)
                total = total - wm[2, a] * west(g, a) - wm[3, a] * east(g, a)
                if g == 5:
                    total = total - wall_mask[a] * inflow
                z[k + 1, g, a] = total

    def own_metal(values):
        return jnp.sum(metal_mask * values, axis=0, keepdims=True)

    def wall_value(k):
        picked = wall_mask[0] * z[k, 5, 0] + wall_mask[1] * z[k, 5, 1]
        return coef * jnp.sum(picked, axis=0, keepdims=True)

    def metal_local(k):
        v = u[k]
        total = (4.0 + kd[...]) * v - pltpu.roll(v, 1, 1) - pltpu.roll(v, 127, 1)
        below = jnp.where(row32 == 0, has_down * he[k, 0, 0:1, :], pltpu.roll(v, 1, 0))
        above = jnp.where(row32 == 31, has_up * he[k, 1, 0:1, :], pltpu.roll(v, 31, 0))
        return total - below - above

    def dot_row(store, i, j):
        total = store[i, 0, 0] * store[j, 0, 0] + store[i, 0, 1] * store[j, 0, 1]
        for g in range(1, 6):
            total = total + store[i, g, 0] * store[j, g, 0] + store[i, g, 1] * store[j, g, 1]
        return jnp.sum(total, axis=0, keepdims=True)

    def metal_dot_row(i, j):
        t = qm[i] * qm[j]
        t = (t[0:8] + t[8:16]) + (t[16:24] + t[24:32])
        return jnp.sum(t, axis=0, keepdims=True)

    def packed(rows, low, high):
        sums = jnp.sum(rows[low:high, :], axis=1, keepdims=True)
        return jnp.sum(jnp.where(eye[low:high], sums, 0.0), axis=0, keepdims=True)

    def unpack(total):
        sums = jnp.sum(jnp.where(eye, total, 0.0), axis=1, keepdims=True)
        scal[...] = jnp.broadcast_to(sums, (32, 128))

    loads[0].wait()
    for g in range(6):
        for a in range(2):
            i = 2 * g + a
            sq[0, 0, i : i + 1, :] = z[0, g, a, 7:8, :]
            sq[0, 1, i : i + 1, :] = z[0, g, a, 0:1, :]
    sq[:, :, 12:16, :] = jnp.zeros((KRYLOV, 2, 4, 128), f32)
    pl.semaphore_wait(barrier, ns + nf + 2)
    for copy in halos(0):
        copy.start()
    loads[1].wait()
    for copy in edges(0):
        copy.start()
    pairs[...] = jnp.zeros((32, 128), f32)
    mpairs[...] = jnp.zeros((32, 128), f32)
    loads[2].wait()
    wm[0] = jnp.where(row8 == 0, 0.0, we[2])
    wm[1] = jnp.where(row8 == 7, 0.0, we[3])
    wm[2] = jnp.where(row8 == 0, has_left * we[2], 0.0)
    wm[3] = jnp.where(row8 == 7, has_right * we[3], 0.0)
    wm[4, 0] = has_down * we[0, 0]
    wm[4, 1] = has_up * we[1, 1]
    loads[3].wait()
    loads[4].wait()

    own = []
    state = {}

    def wall_step(k):
        wall[k, pl.ds(f, 1), :] = wall_value(k)
        send_rows_flow(wall.at[k], k)

    def metal_step(k):
        if k == 1:
            rows_flow(place, KRYLOV).wait_recv()
            places = jnp.sum(place[...], axis=0, keepdims=True)
            state["pick"] = jnp.where((row32.astype(f32) == places) & (lane32 < 32), 1.0, 0.0)[:, 0:32]
        if k > 0:
            rows_flow(wall.at[k - 1], k - 1).wait_recv()
            sink = jnp.dot(
                state["pick"], wall[k - 1],
                precision=lax.Precision.HIGHEST, preferred_element_type=f32,
            )
            for copy in edges(k - 1):
                copy.wait_recv()
            u[k] = metal_local(k - 1) - sink
            for copy in edges(k):
                copy.start()
        own.append(own_metal(u[k]))

    def early_gram():
        n = 0
        for i in range(EARLY):
            for j in range(i, EARLY):
                pairs[n : n + 1, :] = dot_row(z, i, j) + own[i] * own[j]
                n += 1
        ra[0, pl.ds(f, 1), :] = packed(pairs, 0, 32)
        send_rows_flow(ra.at[0], KRYLOV + 1)

    def early_span():
        rows_flow(ra.at[0], KRYLOV + 1).wait_recv()
        rb[0, pl.ds(s, 1), :] = jnp.sum(ra[0], axis=0, keepdims=True)
        send_rows_span(rb.at[0], 0)

    def basis():
        rows_span(rb.at[0], 0).wait_recv()
        unpack(jnp.sum(rb[0], axis=0, keepdims=True))
        gram = {}
        n = 0
        for i in range(EARLY):
            for j in range(i, EARLY):
                gram[i, j] = scal[n : n + 1, :]
                n += 1
        r = {}
        inv = []
        trust = []
        for i in range(EARLY):
            for j in range(i, EARLY):
                t = gram[i, j]
                for h in range(i):
                    t = t - r[h, i] * r[h, j]
                if i == j:
                    floor = gram[i, i] * 1e-5
                    trust.append(t > floor)
                    t = jnp.maximum(t, floor)
                    inv.append(lax.rsqrt(t))
                r[i, j] = t * inv[i]
        ratio = [r[i, i + 1] * inv[i] for i in range(EARLY - 1)]
        coef_a = [ratio[0]]
        coef_b = [None, r[1, 1] * inv[0]]
        good = trust[1]
        for i in range(1, EARLY - 1):
            good = good & trust[i + 1]
            coef_a.append(jnp.where(good, ratio[i] - ratio[i - 1], coef_a[i - 1]))
            guess = coef_b[1] * 1.22
            coef_b.append(jnp.where(good, r[i + 1, i + 1] * inv[i], guess))
        while len(coef_a) < KRYLOV:
            coef_a.append(coef_a[-1])
        while len(coef_b) < KRYLOV + 1:
            coef_b.append(coef_b[-1])
        poly = [[inv[0]]]
        for i in range(KRYLOV):
            back = 1.0 / coef_b[i + 1]
            new = []
            for j in range(i + 2):
                t = None
                if j >= 1:
                    t = poly[i][j - 1]
                if j <= i:
                    t = -coef_a[i] * poly[i][j] if t is None else t - coef_a[i] * poly[i][j]
                if i >= 1 and j <= i - 1:
                    t = t - coef_b[i] * poly[i - 1][j]
                new.append(t * back)
            poly.append(new)
        size = [jnp.sqrt(gram[i, i]) for i in range(EARLY)]
        growth = size[-1] / size[-2]
        while len(size) < KRYLOV:
            size.append(size[-1] * growth)
        spread = []
        for i in range(KRYLOV):
            t = jnp.abs(poly[i][0]) * size[0]
            for j in range(1, i + 1):
                t = t + jnp.abs(poly[i][j]) * size[j]
            spread.append(t)
        return coef_a, coef_b, poly, spread

    def combine(low, high, first):
        poly = state["basis"][2]
        for i in range(low, KRYLOV + 1):
            terms = range(low, min(i, high) + 1)
            if not terms:
                continue
            for g in range(6):
                t = None if first else q[i, g]
                for j in terms:
                    t = poly[i][j] * z[j, g] if t is None else t + poly[i][j] * z[j, g]
                q[i, g] = t

    def metal_combine(low, high, first):
        poly = state["basis"][2]
        for i in range(low, KRYLOV + 1):
            t = None if first else qm[i]
            for j in range(low, min(i, high) + 1):
                t = poly[i][j] * u[j] if t is None else t + poly[i][j] * u[j]
            qm[i] = t

    def place_of(j, i):
        return 24 + j if i == KRYLOV else i * (i + 1) // 2 + j

    def gram_rows(low, high):
        for i in range(low, high + 1):
            for j in range(i + 1):
                n = place_of(j, i)
                pairs[n : n + 1, :] = dot_row(q, j, i)

    def metal_gram_rows(low, high):
        for i in range(low, high + 1):
            for j in range(i + 1):
                n = place_of(j, i)
                mpairs[n : n + 1, :] = metal_dot_row(j, i)

    early = [k for k, _ in PLAN if k >= EARLY - 1][0]
    when = [k for k, _ in PLAN].index(early)
    for step, (k, width) in enumerate(PLAN):
        if k > 0:
            if width == 1:
                send_halos(k)
            else:
                p = PAIRS.index(k)
                copies = pair_copies(k)
                copies[0].start()
                copies[1].start()
                for g in range(6):
                    for m, (b, a) in enumerate(PACK):
                        pk[p, g, m : m + 1, :] = z[k, g, a, b : b + 1, :]
                for copy in copies[4:] + copies[2:4]:
                    copy.start()
        wall_step(k)
        if k == 0:
            send_rows_flow(place, KRYLOV)
        local_part(k)
        metal_step(k)
        if width == 2:
            p = PAIRS.index(k)
            ir[p, 0:1, :] = coef * own[k]
            for copy in inflow_copies(k):
                copy.start()
        if step == 0:
            pack_once()
        if step < len(CHUNKS):
            for copy in once_copies(step):
                copy.start()
        if step == when:
            early_gram()
        if step == when + 1:
            early_span()
        if step == when + 2:
            state["basis"] = basis()
            combine(0, k, True)
            gram_rows(0, k)
        if width == 1:
            for copy in halos(k):
                copy.wait_recv()
            halo_part(
                k, own[k], lambda g: hs[k, 0, g], lambda g: hs[k, 1, g],
                lambda g, a: hq[k, 0, 2 * g + a : 2 * g + a + 1, :],
                lambda g, a: hq[k, 1, 2 * g + a : 2 * g + a + 1, :],
            )
        else:
            if k == PAIRS[0]:
                for chunk in range(len(CHUNKS)):
                    for copy in once_copies(chunk):
                        copy.wait_recv()
                prepare_pairs()
            for copy in pair_copies(k):
                copy.wait_recv()
            halo_part(
                k, own[k], lambda g: tl[p, g, 1], lambda g: th[p, g, 0],
                lambda g, a: sb[p, g, a : a + 1, :],
                lambda g, a: sb[p, g, 4 + a : 5 + a, :],
            )
            wall_step(k + 1)
            beside_cells(k)
            local_part(k + 1)
            if k + 1 == KRYLOV - 1:
                combine(k + 1, k + 1, False)
                gram_rows(k + 1, k + 1)
            for copy in inflow_copies(k):
                copy.wait_recv()
            beside_inflow(k)
            metal_step(k + 1)
            halo_part(
                k + 1, own[k + 1], lambda g: el[g], lambda g: eh[g],
                lambda g, a: es[g, a : a + 1, :],
                lambda g, a: es[g, 4 + a : 5 + a, :],
            )

    last = KRYLOV
    combine(last, last, False)
    gram_rows(last, last)
    ra[1, pl.ds(f, 1), :] = packed(pairs, 0, 32)
    send_rows_flow(ra.at[1], KRYLOV + 2)
    coef_a, coef_b, poly, spread = state["basis"]
    metal_combine(0, last - 1, True)
    metal_gram_rows(0, last - 1)
    rows_flow(wall.at[last - 1], last - 1).wait_recv()
    sink = jnp.dot(
        state["pick"], wall[last - 1], precision=lax.Precision.HIGHEST, preferred_element_type=f32
    )
    for copy in edges(last - 1):
        copy.wait_recv()
    qm[last] = qm[last] + poly[last][last] * (metal_local(last - 1) - sink)
    metal_gram_rows(last, last)
    metal_done = packed(mpairs, 0, 32)
    rows_flow(ra.at[1], KRYLOV + 2).wait_recv()
    rb[1, pl.ds(s, 1), :] = jnp.sum(ra[1], axis=0, keepdims=True) + metal_done
    send_rows_span(rb.at[1], 1)
    for k, width in PLAN:
        for copy in halos(k) if width == 1 else pair_copies(k) + inflow_copies(k):
            copy.wait_send()
    for chunk in range(len(CHUNKS)):
        for copy in once_copies(chunk):
            copy.wait_send()
    for k in range(KRYLOV):
        for copy in edges(k):
            copy.wait_send()
    for k in range(KRYLOV):
        rows_flow(wall.at[k], k).wait_send()
    rows_flow(place, KRYLOV).wait_send()
    rows_flow(ra.at[0], KRYLOV + 1).wait_send()
    rows_flow(ra.at[1], KRYLOV + 2).wait_send()
    rows_span(rb.at[0], 0).wait_send()
    rows_span(rb.at[1], 1).wait()
    unpack(jnp.sum(rb[1], axis=0, keepdims=True))
    gram = {}
    n = 0
    for i in range(KRYLOV + 1):
        for j in range(i + 1):
            m = 24 + j if i == KRYLOV else n
            gram[j, i] = scal[m : m + 1, :]
            n += 1
    r = {}
    low = None
    for i in range(KRYLOV + 1):
        scale = None
        for j in range(i, KRYLOV + 1):
            t = gram[i, j]
            for h in range(i):
                t = t - r[h, i] * r[h, j]
            if i == j:
                rel = t / gram[i, i]
                low = rel if low is None else jnp.minimum(low, rel)
                scale = lax.rsqrt(t)
            r[i, j] = t * scale
    zero = jnp.zeros((1, 128), f32)
    hess = [[zero] * KRYLOV for _ in range(KRYLOV + 1)]
    for j in range(KRYLOV):
        for i in range(j + 2):
            t = r[i, j + 1] * coef_b[j + 1]
            if i <= j:
                t = t + r[i, j] * coef_a[j]
            if i <= j - 1:
                t = t + r[i, j - 1] * coef_b[j]
            hess[i][j] = t
    y = least_squares(hess, r[0, 0] / poly[0][0], zero, KRYLOV)
    top = jnp.abs(y[0])
    total = jnp.abs(y[0]) * spread[0]
    for k in range(1, KRYLOV):
        top = jnp.maximum(top, jnp.abs(y[k]))
        total = total + jnp.abs(y[k]) * spread[k]
    fine = (low > 1e-2) & (total < 1e3 * top)
    ok_ref[...] = jnp.where(fine, 1.0, 0.0)
    for g in range(6):
        t = y[0] * q[0, g]
        for k in range(1, KRYLOV):
            t = t + y[k] * q[k, g]
        xf_ref[g] = t
    out = None
    for j in range(KRYLOV):
        c = y[j] * poly[j][j]
        for k in range(j + 1, KRYLOV):
            c = c + y[k] * poly[k][j]
        out = c * u[j] if out is None else out + c * u[j]
    xs_ref[...] = out


def shards(ns, nf, *args):
    rhs_fluid, rhs_solid = args[0], args[1]
    f32 = jnp.float32
    hbm = pl.BlockSpec(memory_space=pltpu.HBM)
    vmem = pl.BlockSpec(memory_space=pltpu.VMEM)
    smem = pl.BlockSpec(memory_space=pltpu.SMEM)
    dma = pltpu.SemaphoreType.DMA
    x_fluid, x_solid, ok, coef = pl.pallas_call(
        functools.partial(kernel, ns, nf),
        name="gmres",
        out_shape=(
            jax.ShapeDtypeStruct(rhs_fluid.shape, f32),
            jax.ShapeDtypeStruct(rhs_solid.shape, f32),
            jax.ShapeDtypeStruct((1, 128), f32),
            jax.ShapeDtypeStruct(args[-1].shape, f32),
        ),
        in_specs=[hbm] * 5 + [smem] * 2 + [hbm],
        out_specs=(vmem,) * 4,
        scratch_shapes=[
            pltpu.VMEM((KRYLOV + 1, 6, 2, 8, 128), f32),
            pltpu.VMEM((KRYLOV, 32, 128), f32),
            pltpu.VMEM((KRYLOV + 1, 6, 2, 8, 128), f32),
            pltpu.VMEM((KRYLOV + 1, 32, 128), f32),
            pltpu.VMEM((6, 6, 2, 8, 128), f32),
            pltpu.VMEM((6, 2, 8, 128), f32),
            pltpu.VMEM((5, 2, 8, 128), f32),
            pltpu.VMEM((32, 128), f32),
            pltpu.VMEM((KRYLOV, 2, 6, 8, 128), f32),
            pltpu.VMEM((KRYLOV, 2, 16, 128), f32),
            pltpu.VMEM((KRYLOV, 2, 16, 128), f32),
            pltpu.VMEM((KRYLOV, 2, 8, 128), f32),
            pltpu.VMEM((KRYLOV, 32, 128), f32),
            pltpu.VMEM((32, 128), f32),
            pltpu.VMEM((32, 128), f32),
            pltpu.VMEM((32, 128), f32),
            pltpu.VMEM((32, 128), f32),
            pltpu.VMEM((2, 32, 128), f32),
            pltpu.VMEM((2, 16, 128), f32),
            pltpu.VMEM((len(PAIRS), 6, 2, 8, 128), f32),
            pltpu.VMEM((len(PAIRS), 6, 2, 8, 128), f32),
            pltpu.VMEM((len(PAIRS), 6, 8, 128), f32),
            pltpu.VMEM((len(PAIRS), 6, 8, 128), f32),
            pltpu.VMEM((len(PAIRS), 6, 8, 128), f32),
            pltpu.VMEM((len(PAIRS), 8, 128), f32),
            pltpu.VMEM((len(PAIRS), 8, 128), f32),
            pltpu.VMEM((6, 6, 8, 128), f32),
            pltpu.VMEM((6, 6, 8, 128), f32),
            pltpu.VMEM((6, 6, 8, 128), f32),
            pltpu.VMEM((6, 6, 8, 128), f32),
            pltpu.VMEM((6, 8, 128), f32),
            pltpu.VMEM((6, 8, 128), f32),
            pltpu.VMEM((6, 8, 128), f32),
            pltpu.VMEM((6, 8, 128), f32),
            pltpu.VMEM((11, 8, 128), f32),
            pltpu.VMEM((8, 128), f32),
            pltpu.VMEM((6, 8, 128), f32),
            pltpu.VMEM((6, 8, 128), f32),
            pltpu.VMEM((6, 8, 128), f32),
            dma((6,)),
            dma((KRYLOV, 4)), dma((KRYLOV, 4)),
            dma((KRYLOV, 2)), dma((KRYLOV, 2)),
            dma((KRYLOV + 3,)), dma((KRYLOV + 3,)),
            dma((2,)), dma((2,)),
            dma((len(PAIRS), 12)), dma((len(PAIRS), 12)),
            dma((2 * len(CHUNKS) + 10,)), dma((2 * len(CHUNKS) + 10,)),
        ],
        compiler_params=pltpu.CompilerParams(
            collective_id=0, has_side_effects=True, vmem_limit_bytes=8 * 1024 * 1024
        ),
    )(*args)
    return lax.cond(
        ok[0, 0] > 0.5, lambda *a: (x_fluid, x_solid), lambda *a: arnoldi(*a), *args[:-1], coef
    )


def solution(mesh):
    in_specs = (
        P(None, "span", "flow", None),
        P("span", None),
        P(None, None, "span", "flow", None),
        P(None, "span", "flow", None),
        P("span", None),
        P("span", "flow"),
        P("span", "flow"),
        P("span", "flow", None),
    )
    out_specs = (P(None, "span", "flow", None), P("span", None))
    return jax.shard_map(
        functools.partial(shards, mesh.shape["span"], mesh.shape["flow"]),
        mesh=mesh, in_specs=in_specs, out_specs=out_specs, check_vma=False,
    )
```

```python
import functools

import jax
import jax.numpy as jnp
from jax import lax
from jax.experimental import pallas as pl
from jax.experimental.pallas import tpu as pltpu
from jax.sharding import PartitionSpec as P

KRYLOV = 6
MESH = pl.DeviceIdType.MESH
EARLY = 2
PLAN = ((0, 1), (1, 1), (2, 1), (3, 1), (4, 2))
PAIRS = tuple(k for k, width in PLAN if width == 2)
CHUNKS = ((0, 1), (1, 3), (3, 5), (5, 6))


def extended(shard, sides, width):
    for axis, dim in sides:
        count, length = (lax.axis_size(axis), shard.shape[dim])
        up = [(i, (i + 1) % count) for i in range(count - 1)]
        down = [(j, i) for i, j in up]
        last = lax.slice_in_dim(shard, length - width, length, axis=dim)
        first = lax.slice_in_dim(shard, 0, width, axis=dim)
        before = lax.ppermute(last, axis, up)
        after = lax.ppermute(first, axis, down)
        shard = jnp.concatenate([before, shard, after], axis=dim)
    return shard


def back_substitute(upper, rhs_g, steps):
    coeffs = [None] * steps
    for j in range(steps - 1, -1, -1):
        total = rhs_g[j]
        for k in range(j + 1, steps):
            total = total - upper[k][j] * coeffs[k]
        coeffs[j] = total / upper[j][j]
    return coeffs


def least_squares(hess, beta, zero, steps):
    cos_list, sin_list, upper = ([], [], [])
    rhs_g = [beta] + [zero for _ in range(steps)]
    for j in range(steps):
        column = [hess[i][j] for i in range(j + 2)]
        for i in range(j):
            top = cos_list[i] * column[i] + sin_list[i] * column[i + 1]
            column[i + 1] = -sin_list[i] * column[i] + cos_list[i] * column[i + 1]
            column[i] = top
        radius = jnp.sqrt(column[j] * column[j] + column[j + 1] * column[j + 1])
        cos_now = column[j] / radius
        sin_now = column[j + 1] / radius
        column[j] = radius
        rhs_g[j + 1] = -sin_now * rhs_g[j]
        rhs_g[j] = cos_now * rhs_g[j]
        cos_list.append(cos_now)
        sin_list.append(sin_now)
        upper.append(column[: j + 1])
    return back_substitute(upper, rhs_g, steps)


def arnoldi(rhs_fluid, rhs_solid, blocks, weights, kdiag, wall_fluid, wall_solid, wall_coef):
    rows_a = rhs_fluid.shape[1]
    rows_b = rhs_fluid.shape[2]
    width = rhs_fluid.shape[3]
    cells = rows_a * rows_b
    band_rows = rhs_solid.shape[0]
    patch_rows = wall_fluid[0]
    patch_metal = wall_solid[0]
    coef = wall_coef[0]
    fluid_pick = (jnp.arange(cells, dtype=jnp.int32)[:, None] == patch_rows[None, :]).astype(
        jnp.float32
    )
    metal_pick = (jnp.arange(band_rows, dtype=jnp.int32)[:, None] == patch_metal[None, :]).astype(
        jnp.float32
    )
    first_flow = (lax.axis_index("flow") == 0).astype(jnp.float32)
    highest = lax.Precision.HIGHEST

    def local_inner(left, right):
        return jnp.sum(left[0] * right[0]) + first_flow * jnp.sum(left[1] * right[1])

    beta = jnp.sqrt(
        lax.psum(local_inner((rhs_fluid, rhs_solid), (rhs_fluid, rhs_solid)), ("span", "flow"))
    )
    basis = [(rhs_fluid / beta, rhs_solid / beta)]
    hess = [[jnp.float32(0.0) for _ in range(KRYLOV)] for _ in range(KRYLOV + 1)]
    for j in range(KRYLOV):
        field = basis[j][0]
        metal_u = basis[j][1]
        padded = extended(field, (("span", 1), ("flow", 2)), 1)
        local = jnp.einsum("fgabc,gabc->fabc", blocks, field, precision=highest)
        beside = weights[0][None] * padded[:, :-2, 1:-1] + weights[1][None] * padded[:, 2:, 1:-1]
        beside = (
            beside
            + weights[2][None] * padded[:, 1:-1, :-2]
            + weights[3][None] * padded[:, 1:-1, 2:]
        )
        beside = (
            beside
            + weights[4][None] * jnp.roll(field, 1, axis=3)
            + weights[5][None] * jnp.roll(field, -1, axis=3)
        )
        metal_at = jnp.dot(metal_pick.T, metal_u, precision=highest)
        inflow = jnp.dot(fluid_pick, coef * metal_at, precision=highest).reshape(
            rows_a, rows_b, width
        )
        image_f = (local - beside).at[5].add(-inflow)
        wall_vals = coef * jnp.dot(fluid_pick.T, field[5].reshape(cells, width), precision=highest)
        sink = lax.psum(jnp.dot(metal_pick, wall_vals, precision=highest), "flow")
        upad = extended(metal_u, (("span", 0),), 1)
        beside_all = (
            upad[:-2] + upad[2:] + jnp.roll(metal_u, 1, axis=1) + jnp.roll(metal_u, -1, axis=1)
        )
        image_s = (4.0 + kdiag) * metal_u - beside_all - sink
        terms = jnp.stack([local_inner(basis[i], (image_f, image_s)) for i in range(j + 1)])
        values = lax.psum(terms, ("span", "flow"))
        for i in range(j + 1):
            image_f = image_f - values[i] * basis[i][0]
            image_s = image_s - values[i] * basis[i][1]
        rest = jnp.sqrt(
            lax.psum(local_inner((image_f, image_s), (image_f, image_s)), ("span", "flow"))
        )
        for i in range(j + 1):
            hess[i][j] = values[i]
        hess[j + 1][j] = rest
        basis.append((image_f / rest, image_s / rest))
    coeffs = least_squares(hess, beta, jnp.float32(0.0), KRYLOV)
    x_fluid = jnp.zeros_like(rhs_fluid)
    x_solid = jnp.zeros_like(rhs_solid)
    for j in range(KRYLOV):
        x_fluid = x_fluid + coeffs[j] * basis[j][0]
        x_solid = x_solid + coeffs[j] * basis[j][1]
    return (x_fluid, x_solid)


def kernel(
    ns, nf,
    rf_hbm, rs_hbm, bl_hbm, we_hbm, kd_hbm, wf_ref, ws_ref, wc_hbm,
    xf_ref, xs_ref, ok_ref, wc,
    z, u, q, qm, bl, we, wm, kd, hs, hq, sq, he, wall, place, pairs, mpairs, scal, ra, rb,
    tl, th, sb, pk, cb, ir, ib, blo, bhi, bs, pbs, wl, wh, wsr, pws, wn, pid, el, eh, es,
    in_sem, s_halo, r_halo, s_edge, r_edge, s_wall, r_wall, s_red, r_red, s_pair, r_pair, s_once, r_once,
):
    f32 = jnp.float32
    s = lax.axis_index("span")
    f = lax.axis_index("flow")
    up = (lax.rem(s + 1, ns), f)
    down = (lax.rem(s + ns - 1, ns), f)
    right = (s, lax.rem(f + 1, nf))
    left = (s, lax.rem(f + nf - 1, nf))
    corners = ((up[0], right[1]), (down[0], right[1]), (up[0], left[1]), (down[0], left[1]))

    loads = [
        pltpu.make_async_copy(rf_hbm, z.at[0], in_sem.at[0]),
        pltpu.make_async_copy(rs_hbm, u.at[0], in_sem.at[1]),
        pltpu.make_async_copy(we_hbm, we, in_sem.at[2]),
        pltpu.make_async_copy(bl_hbm, bl, in_sem.at[3]),
        pltpu.make_async_copy(kd_hbm, kd, in_sem.at[4]),
        pltpu.make_async_copy(wc_hbm, wc, in_sem.at[5]),
    ]
    for load in loads:
        load.start()

    cb[...] = jnp.zeros((len(PAIRS), 6, 8, 128), f32)

    barrier = pltpu.get_barrier_semaphore()

    def far_first(n):
        return sorted(range(1, n), key=lambda d: -min(d, n - d))

    flow_peers = [(s, lax.rem(f + d, nf)) for d in far_first(nf)]
    span_peers = [(lax.rem(s + d, ns), f) for d in far_first(ns)]
    for to in span_peers + flow_peers:
        pl.semaphore_signal(barrier, inc=1, device_id=to, device_id_type=MESH)
    for to in corners:
        pl.semaphore_signal(barrier, inc=1, device_id=to, device_id_type=MESH)
    row8 = lax.broadcasted_iota(jnp.int32, (8, 128), 0)
    row16 = lax.broadcasted_iota(jnp.int32, (2, 8, 128), 0) * 8 + lax.broadcasted_iota(
        jnp.int32, (2, 8, 128), 1
    )
    row32 = lax.broadcasted_iota(jnp.int32, (32, 128), 0)
    lane32 = lax.broadcasted_iota(jnp.int32, (32, 128), 1)
    lane1 = lax.broadcasted_iota(jnp.int32, (1, 128), 1)
    eye = row32 == lane32
    loads[5].wait()
    patch = wf_ref[0, 0]
    metal_row = ws_ref[0, 0]
    coef = wc[0]
    wall_mask = jnp.where(row16 == patch, 1.0, 0.0).astype(f32)
    metal_mask = jnp.where(row32 == metal_row, 1.0, 0.0).astype(f32)
    place[pl.ds(f, 1), :] = jnp.where(lane1 == f, metal_row.astype(f32), 0.0)
    has_down = jnp.where(s > 0, 1.0, 0.0).astype(f32)
    has_up = jnp.where(s < ns - 1, 1.0, 0.0).astype(f32)
    has_left = jnp.where(f > 0, 1.0, 0.0).astype(f32)
    has_right = jnp.where(f < nf - 1, 1.0, 0.0).astype(f32)

    def send_rows_flow(buf, k):
        for to in flow_peers:
            pltpu.make_async_remote_copy(
                src_ref=buf.at[pl.ds(f, 1)], dst_ref=buf.at[pl.ds(f, 1)],
                send_sem=s_wall.at[k], recv_sem=r_wall.at[k], device_id=to, device_id_type=MESH,
            ).start()

    def rows_flow(buf, k):
        return pltpu.make_async_remote_copy(
            src_ref=buf.at[pl.ds(0, nf - 1)], dst_ref=buf.at[pl.ds(0, nf - 1)],
            send_sem=s_wall.at[k], recv_sem=r_wall.at[k], device_id=right, device_id_type=MESH,
        )

    def send_rows_span(buf, k):
        for to in span_peers:
            pltpu.make_async_remote_copy(
                src_ref=buf.at[pl.ds(s, 1)], dst_ref=buf.at[pl.ds(s, 1)],
                send_sem=s_red.at[k], recv_sem=r_red.at[k], device_id=to, device_id_type=MESH,
            ).start()

    def rows_span(buf, k):
        return pltpu.make_async_remote_copy(
            src_ref=buf.at[pl.ds(0, ns - 1)], dst_ref=buf.at[pl.ds(0, ns - 1)],
            send_sem=s_red.at[k], recv_sem=r_red.at[k], device_id=up, device_id_type=MESH,
        )

    def halos(k):
        def copy(n, src, dst, to):
            return pltpu.make_async_remote_copy(
                src_ref=src, dst_ref=dst, send_sem=s_halo.at[k, n], recv_sem=r_halo.at[k, n],
                device_id=to, device_id_type=MESH,
            )

        return [
            copy(0, z.at[k, :, 1], hs.at[k, 0], up),
            copy(1, z.at[k, :, 0], hs.at[k, 1], down),
            copy(2, sq.at[k, 0], hq.at[k, 0], right),
            copy(3, sq.at[k, 1], hq.at[k, 1], left),
        ]

    def edges(k):
        def copy(n, src, dst, to):
            return pltpu.make_async_remote_copy(
                src_ref=src, dst_ref=dst, send_sem=s_edge.at[k, n], recv_sem=r_edge.at[k, n],
                device_id=to, device_id_type=MESH,
            )

        return [
            copy(0, u.at[k, pl.ds(31, 1)], he.at[k, 0, pl.ds(0, 1)], up),
            copy(1, u.at[k, pl.ds(0, 1)], he.at[k, 1, pl.ds(0, 1)], down),
        ]

    def send_halos(k):
        out = halos(k)
        out[0].start()
        out[1].start()
        for g in range(6):
            for a in range(2):
                i = 2 * g + a
                sq[k, 0, i : i + 1, :] = z[k, g, a, 7:8, :]
                sq[k, 1, i : i + 1, :] = z[k, g, a, 0:1, :]
        out[2].start()
        out[3].start()

    def remote(src, dst, send, recv, to):
        return pltpu.make_async_remote_copy(
            src_ref=src, dst_ref=dst, send_sem=send, recv_sem=recv, device_id=to, device_id_type=MESH
        )

    def pair_copies(k):
        p = PAIRS.index(k)

        def copy(n, src, dst, to):
            return remote(src, dst, s_pair.at[p, n], r_pair.at[p, n], to)

        return [
            copy(0, z.at[k], tl.at[p], up),
            copy(1, z.at[k], th.at[p], down),
            copy(2, pk.at[p, :, pl.ds(4, 4)], sb.at[p, :, pl.ds(0, 4)], right),
            copy(3, pk.at[p, :, pl.ds(0, 4)], sb.at[p, :, pl.ds(4, 4)], left),
            copy(4, pk.at[p, :, pl.ds(5, 1)], cb.at[p, :, pl.ds(0, 1)], corners[0]),
            copy(5, pk.at[p, :, pl.ds(4, 1)], cb.at[p, :, pl.ds(1, 1)], corners[1]),
            copy(6, pk.at[p, :, pl.ds(1, 1)], cb.at[p, :, pl.ds(4, 1)], corners[2]),
            copy(7, pk.at[p, :, pl.ds(0, 1)], cb.at[p, :, pl.ds(5, 1)], corners[3]),
        ]

    def inflow_copies(k):
        p = PAIRS.index(k)
        return [
            remote(
                ir.at[p, pl.ds(0, 1)], ib.at[p, pl.ds(n, 1)],
                s_pair.at[p, 8 + n], r_pair.at[p, 8 + n], to,
            )
            for n, to in enumerate((up, down, right, left))
        ]

    def once_copies(chunk):
        def copy(n, src, dst, to):
            return remote(src, dst, s_once.at[n], r_once.at[n], to)

        low, high = CHUNKS[chunk]
        rows = pl.ds(low, high - low)
        out = [
            copy(2 * chunk, bl.at[rows, :, 1], blo.at[rows], up),
            copy(2 * chunk + 1, bl.at[rows, :, 0], bhi.at[rows], down),
        ]
        if chunk == 0:
            n = 2 * len(CHUNKS)
            out += [
                copy(n, we.at[:, 1], wl, up),
                copy(n + 1, we.at[:, 0], wh, down),
                copy(n + 2, pbs.at[:, :, pl.ds(4, 2)], bs.at[:, :, pl.ds(0, 2)], right),
                copy(n + 3, pbs.at[:, :, pl.ds(0, 2)], bs.at[:, :, pl.ds(4, 2)], left),
                copy(n + 4, pws.at[:, pl.ds(4, 4)], wsr.at[:, pl.ds(0, 4)], right),
                copy(n + 5, pws.at[:, pl.ds(0, 4)], wsr.at[:, pl.ds(4, 4)], left),
            ]
            out += [
                copy(n + 6 + m, pid.at[pl.ds(4, 1)], pid.at[pl.ds(m, 1)], to)
                for m, to in enumerate((up, down, right, left))
            ]
        return out

    PACK = ((0, 0), (0, 1), (1, 0), (1, 1), (7, 0), (7, 1), (6, 0), (6, 1))

    def pack_once():
        def one(i, c):
            for g in range(6):
                for m, (b, a) in enumerate(PACK):
                    pbs[i, g, m : m + 1, :] = bl[i, g, a, b : b + 1, :]
            for m, (b, a) in enumerate(PACK):
                pws[i, m : m + 1, :] = we[i, a, b : b + 1, :]
            return c

        lax.fori_loop(0, 6, one, 0)
        pid[4:5, :] = jnp.broadcast_to(patch.astype(f32), (1, 128))

    def prepare_pairs():
        wn[0] = wl[2] * jnp.where(row8 == 0, has_left, 1.0)
        wn[1] = wl[3] * jnp.where(row8 == 7, has_right, 1.0)
        wn[2] = wh[2] * jnp.where(row8 == 0, has_left, 1.0)
        wn[3] = wh[3] * jnp.where(row8 == 7, has_right, 1.0)
        wn[4] = wsr[0] * jnp.where((row8 == 0) | (row8 == 4), has_down, 1.0)
        wn[5] = wsr[1] * jnp.where((row8 == 1) | (row8 == 5), has_up, 1.0)
        wn[6] = jnp.where(row8 < 4, wsr[2], wsr[3])
        wn[7] = jnp.where(row8 < 4, wsr[3], wsr[2])
        here = row8.astype(f32)
        wn[8] = jnp.where(here + 8.0 == pid[0:1, :], 1.0, 0.0)
        wn[9] = jnp.where(here == pid[1:2, :], 1.0, 0.0)
        side = jnp.where((row8 == 0) & (pid[2:3, :] == 7.0), 1.0, 0.0)
        side = side + jnp.where((row8 == 1) & (pid[2:3, :] == 15.0), 1.0, 0.0)
        side = side + jnp.where((row8 == 4) & (pid[3:4, :] == 0.0), 1.0, 0.0)
        wn[10] = side + jnp.where((row8 == 5) & (pid[3:4, :] == 8.0), 1.0, 0.0)

    def beside_cells(k):
        p = PAIRS.index(k)
        odd = (row8 & 1) == 1
        for g in range(6):
            v = tl[p, g, 1]
            total = blo[g, 0] * tl[p, 0, 1]
            for h in range(1, 6):
                total = total + blo[g, h] * tl[p, h, 1]
            total = total - wl[0] * tl[p, g, 0] - wl[1] * z[k, g, 0]
            total = total - wn[0] * jnp.where(row8 == 0, cb[p, g, 0:1, :], pltpu.roll(v, 1, 0))
            total = total - wn[1] * jnp.where(row8 == 7, cb[p, g, 4:5, :], pltpu.roll(v, 7, 0))
            el[g] = total - wl[4] * pltpu.roll(v, 1, 1) - wl[5] * pltpu.roll(v, 127, 1)
            v = th[p, g, 0]
            total = bhi[g, 0] * th[p, 0, 0]
            for h in range(1, 6):
                total = total + bhi[g, h] * th[p, h, 0]
            total = total - wh[0] * z[k, g, 1] - wh[1] * th[p, g, 1]
            total = total - wn[2] * jnp.where(row8 == 0, cb[p, g, 1:2, :], pltpu.roll(v, 1, 0))
            total = total - wn[3] * jnp.where(row8 == 7, cb[p, g, 5:6, :], pltpu.roll(v, 7, 0))
            eh[g] = total - wh[4] * pltpu.roll(v, 1, 1) - wh[5] * pltpu.roll(v, 127, 1)
            v = sb[p, g]
            total = bs[g, 0] * sb[p, 0]
            for h in range(1, 6):
                total = total + bs[g, h] * sb[p, h]
            total = total - wn[4] * jnp.where(odd, pltpu.roll(v, 1, 0), cb[p, g])
            total = total - wn[5] * jnp.where(odd, cb[p, g], pltpu.roll(v, 7, 0))
            total = total - wn[6] * pltpu.roll(v, 6, 0) - wn[7] * pk[p, g]
            es[g] = total - wsr[4] * pltpu.roll(v, 1, 1) - wsr[5] * pltpu.roll(v, 127, 1)

    def beside_inflow(k):
        p = PAIRS.index(k)
        el[5] = el[5] - wn[8] * ib[p, 0:1, :]
        eh[5] = eh[5] - wn[9] * ib[p, 1:2, :]
        es[5] = es[5] - wn[10] * jnp.where(row8 < 4, ib[p, 2:3, :], ib[p, 3:4, :])

    def local_part(k):
        field = [z[k, g] for g in range(6)]
        for g in range(6):
            v = field[g]
            total = bl[g, 0] * field[0]
            for h in range(1, 6):
                total = total + bl[g, h] * field[h]
            total = total - we[4] * pltpu.roll(v, 1, 2) - we[5] * pltpu.roll(v, 127, 2)
            total = total - wm[0] * pltpu.roll(v, 1, 1) - wm[1] * pltpu.roll(v, 7, 1)
            z[k + 1, g, 0] = total[0] - we[1, 0] * v[1]
            z[k + 1, g, 1] = total[1] - we[0, 1] * v[0]

    def halo_part(k, metal_here, low, high, west, east):
        inflow = coef * metal_here
        for g in range(6):
            for a in range(2):
                total = z[k + 1, g, a]
                if a == 0:
                    total = total - wm[4, 0] * low(g)
                else:
                    total = total - wm[4, 1] * high(g)
                total = total - wm[2, a] * west(g, a) - wm[3, a] * east(g, a)
                if g == 5:
                    total = total - wall_mask[a] * inflow
                z[k + 1, g, a] = total

    def own_metal(values):
        return jnp.sum(metal_mask * values, axis=0, keepdims=True)

    def wall_value(k):
        picked = wall_mask[0] * z[k, 5, 0] + wall_mask[1] * z[k, 5, 1]
        return coef * jnp.sum(picked, axis=0, keepdims=True)

    def metal_local(k):
        v = u[k]
        total = (4.0 + kd[...]) * v - pltpu.roll(v, 1, 1) - pltpu.roll(v, 127, 1)
        below = jnp.where(row32 == 0, has_down * he[k, 0, 0:1, :], pltpu.roll(v, 1, 0))
        above = jnp.where(row32 == 31, has_up * he[k, 1, 0:1, :], pltpu.roll(v, 31, 0))
        return total - below - above

    def dot_row(store, i, j):
        total = store[i, 0, 0] * store[j, 0, 0] + store[i, 0, 1] * store[j, 0, 1]
        for g in range(1, 6):
            total = total + store[i, g, 0] * store[j, g, 0] + store[i, g, 1] * store[j, g, 1]
        return jnp.sum(total, axis=0, keepdims=True)

    def metal_dot_row(i, j):
        t = qm[i] * qm[j]
        t = (t[0:8] + t[8:16]) + (t[16:24] + t[24:32])
        return jnp.sum(t, axis=0, keepdims=True)

    def packed(rows, low, high):
        sums = jnp.sum(rows[low:high, :], axis=1, keepdims=True)
        return jnp.sum(jnp.where(eye[low:high], sums, 0.0), axis=0, keepdims=True)

    def unpack(total):
        sums = jnp.sum(jnp.where(eye, total, 0.0), axis=1, keepdims=True)
        scal[...] = jnp.broadcast_to(sums, (32, 128))

    loads[0].wait()
    for g in range(6):
        for a in range(2):
            i = 2 * g + a
            sq[0, 0, i : i + 1, :] = z[0, g, a, 7:8, :]
            sq[0, 1, i : i + 1, :] = z[0, g, a, 0:1, :]
    sq[:, :, 12:16, :] = jnp.zeros((KRYLOV, 2, 4, 128), f32)
    pl.semaphore_wait(barrier, ns + nf + 2)
    for copy in halos(0):
        copy.start()
    loads[1].wait()
    for copy in edges(0):
        copy.start()
    pairs[...] = jnp.zeros((32, 128), f32)
    mpairs[...] = jnp.zeros((32, 128), f32)
    loads[2].wait()
    wm[0] = jnp.where(row8 == 0, 0.0, we[2])
    wm[1] = jnp.where(row8 == 7, 0.0, we[3])
    wm[2] = jnp.where(row8 == 0, has_left * we[2], 0.0)
    wm[3] = jnp.where(row8 == 7, has_right * we[3], 0.0)
    wm[4, 0] = has_down * we[0, 0]
    wm[4, 1] = has_up * we[1, 1]
    loads[3].wait()
    loads[4].wait()

    own = []
    state = {}

    def wall_step(k):
        wall[k, pl.ds(f, 1), :] = wall_value(k)
        send_rows_flow(wall.at[k], k)

    def metal_step(k):
        if k == 1:
            rows_flow(place, KRYLOV).wait_recv()
            places = jnp.sum(place[...], axis=0, keepdims=True)
            state["pick"] = jnp.where((row32.astype(f32) == places) & (lane32 < 32), 1.0, 0.0)[:, 0:32]
        if k > 0:
            rows_flow(wall.at[k - 1], k - 1).wait_recv()
            sink = jnp.dot(
                state["pick"], wall[k - 1],
                precision=lax.Precision.HIGHEST, preferred_element_type=f32,
            )
            for copy in edges(k - 1):
                copy.wait_recv()
            u[k] = metal_local(k - 1) - sink
            for copy in edges(k):
                copy.start()
        own.append(own_metal(u[k]))

    def early_gram():
        n = 0
        for i in range(EARLY):
            for j in range(i, EARLY):
                pairs[n : n + 1, :] = dot_row(z, i, j)
                n += 1
        ra[0, pl.ds(f, 1), :] = packed(pairs, 0, 32)
        send_rows_flow(ra.at[0], KRYLOV + 1)

    def early_span():
        rows_flow(ra.at[0], KRYLOV + 1).wait_recv()
        rb[0, pl.ds(s, 1), :] = jnp.sum(ra[0], axis=0, keepdims=True)
        send_rows_span(rb.at[0], 0)

    def basis():
        rows_span(rb.at[0], 0).wait_recv()
        unpack(jnp.sum(rb[0], axis=0, keepdims=True))
        gram = {}
        n = 0
        for i in range(EARLY):
            for j in range(i, EARLY):
                gram[i, j] = scal[n : n + 1, :]
                n += 1
        r = {}
        inv = []
        trust = []
        for i in range(EARLY):
            for j in range(i, EARLY):
                t = gram[i, j]
                for h in range(i):
                    t = t - r[h, i] * r[h, j]
                if i == j:
                    floor = gram[i, i] * 1e-5
                    trust.append(t > floor)
                    t = jnp.maximum(t, floor)
                    inv.append(lax.rsqrt(t))
                r[i, j] = t * inv[i]
        ratio = [r[i, i + 1] * inv[i] for i in range(EARLY - 1)]
        coef_a = [ratio[0]]
        coef_b = [None, r[1, 1] * inv[0]]
        good = trust[1]
        for i in range(1, EARLY - 1):
            good = good & trust[i + 1]
            coef_a.append(jnp.where(good, ratio[i] - ratio[i - 1], coef_a[i - 1]))
            guess = coef_b[1] * 1.22
            coef_b.append(jnp.where(good, r[i + 1, i + 1] * inv[i], guess))
        while len(coef_a) < KRYLOV:
            coef_a.append(coef_a[-1])
        while len(coef_b) < KRYLOV + 1:
            coef_b.append(coef_b[-1])
        poly = [[inv[0]]]
        for i in range(KRYLOV):
            back = 1.0 / coef_b[i + 1]
            new = []
            for j in range(i + 2):
                t = None
                if j >= 1:
                    t = poly[i][j - 1]
                if j <= i:
                    t = -coef_a[i] * poly[i][j] if t is None else t - coef_a[i] * poly[i][j]
                if i >= 1 and j <= i - 1:
                    t = t - coef_b[i] * poly[i - 1][j]
                new.append(t * back)
            poly.append(new)
        size = [jnp.sqrt(gram[i, i]) for i in range(EARLY)]
        growth = size[-1] / size[-2]
        while len(size) < KRYLOV:
            size.append(size[-1] * growth)
        spread = []
        for i in range(KRYLOV):
            t = jnp.abs(poly[i][0]) * size[0]
            for j in range(1, i + 1):
                t = t + jnp.abs(poly[i][j]) * size[j]
            spread.append(t)
        return coef_a, coef_b, poly, spread

    def combine(low, high, first):
        poly = state["basis"][2]
        for i in range(low, KRYLOV + 1):
            terms = range(low, min(i, high) + 1)
            if not terms:
                continue
            for g in range(6):
                t = None if first else q[i, g]
                for j in terms:
                    t = poly[i][j] * z[j, g] if t is None else t + poly[i][j] * z[j, g]
                q[i, g] = t

    def metal_combine(low, high, first):
        poly = state["basis"][2]
        for i in range(low, KRYLOV + 1):
            t = None if first else qm[i]
            for j in range(low, min(i, high) + 1):
                t = poly[i][j] * u[j] if t is None else t + poly[i][j] * u[j]
            qm[i] = t

    def place_of(j, i):
        return 24 + j if i == KRYLOV else i * (i + 1) // 2 + j

    def gram_rows(low, high):
        for i in range(low, high + 1):
            for j in range(i + 1):
                n = place_of(j, i)
                pairs[n : n + 1, :] = dot_row(q, j, i)

    def metal_gram_rows(low, high):
        for i in range(low, high + 1):
            for j in range(i + 1):
                n = place_of(j, i)
                mpairs[n : n + 1, :] = metal_dot_row(j, i)

    early = [k for k, _ in PLAN if k >= EARLY - 1][0]
    when = [k for k, _ in PLAN].index(early)
    for step, (k, width) in enumerate(PLAN):
        if k > 0:
            if width == 1:
                send_halos(k)
            else:
                p = PAIRS.index(k)
                copies = pair_copies(k)
                copies[0].start()
                copies[1].start()
                for g in range(6):
                    for m, (b, a) in enumerate(PACK):
                        pk[p, g, m : m + 1, :] = z[k, g, a, b : b + 1, :]
                for copy in copies[4:] + copies[2:4]:
                    copy.start()
        if step == when:
            early_gram()
        wall_step(k)
        if k == 0:
            send_rows_flow(place, KRYLOV)
            pack_once()
        if step < len(CHUNKS):
            for copy in once_copies(step):
                copy.start()
        local_part(k)
        metal_step(k)
        if width == 2:
            p = PAIRS.index(k)
            ir[p, 0:1, :] = coef * own[k]
            for copy in inflow_copies(k):
                copy.start()
        if step == when + 1:
            early_span()
        if step == when + 3:
            state["basis"] = basis()
            combine(0, k, True)
            gram_rows(0, k)
        if width == 1:
            for copy in halos(k):
                copy.wait_recv()
            halo_part(
                k, own[k], lambda g: hs[k, 0, g], lambda g: hs[k, 1, g],
                lambda g, a: hq[k, 0, 2 * g + a : 2 * g + a + 1, :],
                lambda g, a: hq[k, 1, 2 * g + a : 2 * g + a + 1, :],
            )
        else:
            if k == PAIRS[0]:
                for chunk in range(len(CHUNKS)):
                    for copy in once_copies(chunk):
                        copy.wait_recv()
                prepare_pairs()
            for copy in pair_copies(k):
                copy.wait_recv()
            halo_part(
                k, own[k], lambda g: tl[p, g, 1], lambda g: th[p, g, 0],
                lambda g, a: sb[p, g, a : a + 1, :],
                lambda g, a: sb[p, g, 4 + a : 5 + a, :],
            )
            wall_step(k + 1)
            beside_cells(k)
            local_part(k + 1)
            if k + 1 == KRYLOV - 1:
                combine(k + 1, k + 1, False)
                gram_rows(k + 1, k + 1)
            for copy in inflow_copies(k):
                copy.wait_recv()
            beside_inflow(k)
            metal_step(k + 1)
            halo_part(
                k + 1, own[k + 1], lambda g: el[g], lambda g: eh[g],
                lambda g, a: es[g, a : a + 1, :],
                lambda g, a: es[g, 4 + a : 5 + a, :],
            )

    last = KRYLOV
    combine(last, last, False)
    gram_rows(last, last)
    ra[1, pl.ds(f, 1), :] = packed(pairs, 0, 32)
    send_rows_flow(ra.at[1], KRYLOV + 2)
    coef_a, coef_b, poly, spread = state["basis"]
    metal_combine(0, last - 1, True)
    metal_gram_rows(0, last - 1)
    rows_flow(wall.at[last - 1], last - 1).wait_recv()
    sink = jnp.dot(
        state["pick"], wall[last - 1], precision=lax.Precision.HIGHEST, preferred_element_type=f32
    )
    for copy in edges(last - 1):
        copy.wait_recv()
    qm[last] = qm[last] + poly[last][last] * (metal_local(last - 1) - sink)
    metal_gram_rows(last, last)
    metal_done = packed(mpairs, 0, 32)
    rows_flow(ra.at[1], KRYLOV + 2).wait_recv()
    rb[1, pl.ds(s, 1), :] = jnp.sum(ra[1], axis=0, keepdims=True) + metal_done
    send_rows_span(rb.at[1], 1)
    for k, width in PLAN:
        for copy in halos(k) if width == 1 else pair_copies(k) + inflow_copies(k):
            copy.wait_send()
    for chunk in range(len(CHUNKS)):
        for copy in once_copies(chunk):
            copy.wait_send()
    for k in range(KRYLOV):
        for copy in edges(k):
            copy.wait_send()
    for k in range(KRYLOV):
        rows_flow(wall.at[k], k).wait_send()
    rows_flow(place, KRYLOV).wait_send()
    rows_flow(ra.at[0], KRYLOV + 1).wait_send()
    rows_flow(ra.at[1], KRYLOV + 2).wait_send()
    rows_span(rb.at[0], 0).wait_send()
    rows_span(rb.at[1], 1).wait()
    unpack(jnp.sum(rb[1], axis=0, keepdims=True))
    gram = {}
    n = 0
    for i in range(KRYLOV + 1):
        for j in range(i + 1):
            m = 24 + j if i == KRYLOV else n
            gram[j, i] = scal[m : m + 1, :]
            n += 1
    r = {}
    low = None
    for i in range(KRYLOV + 1):
        scale = None
        for j in range(i, KRYLOV + 1):
            t = gram[i, j]
            for h in range(i):
                t = t - r[h, i] * r[h, j]
            if i == j:
                rel = t / gram[i, i]
                low = rel if low is None else jnp.minimum(low, rel)
                scale = lax.rsqrt(t)
            r[i, j] = t * scale
    zero = jnp.zeros((1, 128), f32)
    hess = [[zero] * KRYLOV for _ in range(KRYLOV + 1)]
    for j in range(KRYLOV):
        for i in range(j + 2):
            t = r[i, j + 1] * coef_b[j + 1]
            if i <= j:
                t = t + r[i, j] * coef_a[j]
            if i <= j - 1:
                t = t + r[i, j - 1] * coef_b[j]
            hess[i][j] = t
    y = least_squares(hess, r[0, 0] / poly[0][0], zero, KRYLOV)
    top = jnp.abs(y[0])
    total = jnp.abs(y[0]) * spread[0]
    for k in range(1, KRYLOV):
        top = jnp.maximum(top, jnp.abs(y[k]))
        total = total + jnp.abs(y[k]) * spread[k]
    fine = (low > 1e-2) & (total < 1e3 * top)
    ok_ref[...] = jnp.where(fine, 1.0, 0.0)
    for g in range(6):
        t = y[0] * q[0, g]
        for k in range(1, KRYLOV):
            t = t + y[k] * q[k, g]
        xf_ref[g] = t
    out = None
    for j in range(KRYLOV):
        c = y[j] * poly[j][j]
        for k in range(j + 1, KRYLOV):
            c = c + y[k] * poly[k][j]
        out = c * u[j] if out is None else out + c * u[j]
    xs_ref[...] = out


def shards(ns, nf, *args):
    rhs_fluid, rhs_solid = args[0], args[1]
    f32 = jnp.float32
    hbm = pl.BlockSpec(memory_space=pltpu.HBM)
    vmem = pl.BlockSpec(memory_space=pltpu.VMEM)
    smem = pl.BlockSpec(memory_space=pltpu.SMEM)
    dma = pltpu.SemaphoreType.DMA
    x_fluid, x_solid, ok, coef = pl.pallas_call(
        functools.partial(kernel, ns, nf),
        name="gmres",
        out_shape=(
            jax.ShapeDtypeStruct(rhs_fluid.shape, f32),
            jax.ShapeDtypeStruct(rhs_solid.shape, f32),
            jax.ShapeDtypeStruct((1, 128), f32),
            jax.ShapeDtypeStruct(args[-1].shape, f32),
        ),
        in_specs=[hbm] * 5 + [smem] * 2 + [hbm],
        out_specs=(vmem,) * 4,
        scratch_shapes=[
            pltpu.VMEM((KRYLOV + 1, 6, 2, 8, 128), f32),
            pltpu.VMEM((KRYLOV, 32, 128), f32),
            pltpu.VMEM((KRYLOV + 1, 6, 2, 8, 128), f32),
            pltpu.VMEM((KRYLOV + 1, 32, 128), f32),
            pltpu.VMEM((6, 6, 2, 8, 128), f32),
            pltpu.VMEM((6, 2, 8, 128), f32),
            pltpu.VMEM((5, 2, 8, 128), f32),
            pltpu.VMEM((32, 128), f32),
            pltpu.VMEM((KRYLOV, 2, 6, 8, 128), f32),
            pltpu.VMEM((KRYLOV, 2, 16, 128), f32),
            pltpu.VMEM((KRYLOV, 2, 16, 128), f32),
            pltpu.VMEM((KRYLOV, 2, 8, 128), f32),
            pltpu.VMEM((KRYLOV, 32, 128), f32),
            pltpu.VMEM((32, 128), f32),
            pltpu.VMEM((32, 128), f32),
            pltpu.VMEM((32, 128), f32),
            pltpu.VMEM((32, 128), f32),
            pltpu.VMEM((2, 32, 128), f32),
            pltpu.VMEM((2, 16, 128), f32),
            pltpu.VMEM((len(PAIRS), 6, 2, 8, 128), f32),
            pltpu.VMEM((len(PAIRS), 6, 2, 8, 128), f32),
            pltpu.VMEM((len(PAIRS), 6, 8, 128), f32),
            pltpu.VMEM((len(PAIRS), 6, 8, 128), f32),
            pltpu.VMEM((len(PAIRS), 6, 8, 128), f32),
            pltpu.VMEM((len(PAIRS), 8, 128), f32),
            pltpu.VMEM((len(PAIRS), 8, 128), f32),
            pltpu.VMEM((6, 6, 8, 128), f32),
            pltpu.VMEM((6, 6, 8, 128), f32),
            pltpu.VMEM((6, 6, 8, 128), f32),
            pltpu.VMEM((6, 6, 8, 128), f32),
            pltpu.VMEM((6, 8, 128), f32),
            pltpu.VMEM((6, 8, 128), f32),
            pltpu.VMEM((6, 8, 128), f32),
            pltpu.VMEM((6, 8, 128), f32),
            pltpu.VMEM((11, 8, 128), f32),
            pltpu.VMEM((8, 128), f32),
            pltpu.VMEM((6, 8, 128), f32),
            pltpu.VMEM((6, 8, 128), f32),
            pltpu.VMEM((6, 8, 128), f32),
            dma((6,)),
            dma((KRYLOV, 4)), dma((KRYLOV, 4)),
            dma((KRYLOV, 2)), dma((KRYLOV, 2)),
            dma((KRYLOV + 3,)), dma((KRYLOV + 3,)),
            dma((2,)), dma((2,)),
            dma((len(PAIRS), 12)), dma((len(PAIRS), 12)),
            dma((2 * len(CHUNKS) + 10,)), dma((2 * len(CHUNKS) + 10,)),
        ],
        compiler_params=pltpu.CompilerParams(
            collective_id=0, has_side_effects=True, vmem_limit_bytes=8 * 1024 * 1024
        ),
    )(*args)
    return lax.cond(
        ok[0, 0] > 0.5, lambda *a: (x_fluid, x_solid), lambda *a: arnoldi(*a), *args[:-1], coef
    )


def solution(mesh):
    in_specs = (
        P(None, "span", "flow", None),
        P("span", None),
        P(None, None, "span", "flow", None),
        P(None, "span", "flow", None),
        P("span", None),
        P("span", "flow"),
        P("span", "flow"),
        P("span", "flow", None),
    )
    out_specs = (P(None, "span", "flow", None), P("span", None))
    return jax.shard_map(
        functools.partial(shards, mesh.shape["span"], mesh.shape["flow"]),
        mesh=mesh, in_specs=in_specs, out_specs=out_specs, check_vma=False,
    )
```

```python
import functools

import jax
import jax.numpy as jnp
from jax import lax
from jax.experimental import pallas as pl
from jax.experimental.pallas import tpu as pltpu
from jax.sharding import PartitionSpec as P

KRYLOV = 6
MESH = pl.DeviceIdType.MESH
EARLY = 2
PLAN = ((0, 1), (1, 1), (2, 1), (3, 1), (4, 2))
PAIRS = tuple(k for k, width in PLAN if width == 2)


def extended(shard, sides, width):
    for axis, dim in sides:
        count, length = (lax.axis_size(axis), shard.shape[dim])
        up = [(i, (i + 1) % count) for i in range(count - 1)]
        down = [(j, i) for i, j in up]
        last = lax.slice_in_dim(shard, length - width, length, axis=dim)
        first = lax.slice_in_dim(shard, 0, width, axis=dim)
        before = lax.ppermute(last, axis, up)
        after = lax.ppermute(first, axis, down)
        shard = jnp.concatenate([before, shard, after], axis=dim)
    return shard


def back_substitute(upper, rhs_g, steps):
    coeffs = [None] * steps
    for j in range(steps - 1, -1, -1):
        total = rhs_g[j]
        for k in range(j + 1, steps):
            total = total - upper[k][j] * coeffs[k]
        coeffs[j] = total / upper[j][j]
    return coeffs


def least_squares(hess, beta, zero, steps):
    cos_list, sin_list, upper = ([], [], [])
    rhs_g = [beta] + [zero for _ in range(steps)]
    for j in range(steps):
        column = [hess[i][j] for i in range(j + 2)]
        for i in range(j):
            top = cos_list[i] * column[i] + sin_list[i] * column[i + 1]
            column[i + 1] = -sin_list[i] * column[i] + cos_list[i] * column[i + 1]
            column[i] = top
        radius = jnp.sqrt(column[j] * column[j] + column[j + 1] * column[j + 1])
        cos_now = column[j] / radius
        sin_now = column[j + 1] / radius
        column[j] = radius
        rhs_g[j + 1] = -sin_now * rhs_g[j]
        rhs_g[j] = cos_now * rhs_g[j]
        cos_list.append(cos_now)
        sin_list.append(sin_now)
        upper.append(column[: j + 1])
    return back_substitute(upper, rhs_g, steps)


def arnoldi(rhs_fluid, rhs_solid, blocks, weights, kdiag, wall_fluid, wall_solid, wall_coef):
    rows_a = rhs_fluid.shape[1]
    rows_b = rhs_fluid.shape[2]
    width = rhs_fluid.shape[3]
    cells = rows_a * rows_b
    band_rows = rhs_solid.shape[0]
    patch_rows = wall_fluid[0]
    patch_metal = wall_solid[0]
    coef = wall_coef[0]
    fluid_pick = (jnp.arange(cells, dtype=jnp.int32)[:, None] == patch_rows[None, :]).astype(
        jnp.float32
    )
    metal_pick = (jnp.arange(band_rows, dtype=jnp.int32)[:, None] == patch_metal[None, :]).astype(
        jnp.float32
    )
    first_flow = (lax.axis_index("flow") == 0).astype(jnp.float32)
    highest = lax.Precision.HIGHEST

    def local_inner(left, right):
        return jnp.sum(left[0] * right[0]) + first_flow * jnp.sum(left[1] * right[1])

    beta = jnp.sqrt(
        lax.psum(local_inner((rhs_fluid, rhs_solid), (rhs_fluid, rhs_solid)), ("span", "flow"))
    )
    basis = [(rhs_fluid / beta, rhs_solid / beta)]
    hess = [[jnp.float32(0.0) for _ in range(KRYLOV)] for _ in range(KRYLOV + 1)]
    for j in range(KRYLOV):
        field = basis[j][0]
        metal_u = basis[j][1]
        padded = extended(field, (("span", 1), ("flow", 2)), 1)
        local = jnp.einsum("fgabc,gabc->fabc", blocks, field, precision=highest)
        beside = weights[0][None] * padded[:, :-2, 1:-1] + weights[1][None] * padded[:, 2:, 1:-1]
        beside = (
            beside
            + weights[2][None] * padded[:, 1:-1, :-2]
            + weights[3][None] * padded[:, 1:-1, 2:]
        )
        beside = (
            beside
            + weights[4][None] * jnp.roll(field, 1, axis=3)
            + weights[5][None] * jnp.roll(field, -1, axis=3)
        )
        metal_at = jnp.dot(metal_pick.T, metal_u, precision=highest)
        inflow = jnp.dot(fluid_pick, coef * metal_at, precision=highest).reshape(
            rows_a, rows_b, width
        )
        image_f = (local - beside).at[5].add(-inflow)
        wall_vals = coef * jnp.dot(fluid_pick.T, field[5].reshape(cells, width), precision=highest)
        sink = lax.psum(jnp.dot(metal_pick, wall_vals, precision=highest), "flow")
        upad = extended(metal_u, (("span", 0),), 1)
        beside_all = (
            upad[:-2] + upad[2:] + jnp.roll(metal_u, 1, axis=1) + jnp.roll(metal_u, -1, axis=1)
        )
        image_s = (4.0 + kdiag) * metal_u - beside_all - sink
        terms = jnp.stack([local_inner(basis[i], (image_f, image_s)) for i in range(j + 1)])
        values = lax.psum(terms, ("span", "flow"))
        for i in range(j + 1):
            image_f = image_f - values[i] * basis[i][0]
            image_s = image_s - values[i] * basis[i][1]
        rest = jnp.sqrt(
            lax.psum(local_inner((image_f, image_s), (image_f, image_s)), ("span", "flow"))
        )
        for i in range(j + 1):
            hess[i][j] = values[i]
        hess[j + 1][j] = rest
        basis.append((image_f / rest, image_s / rest))
    coeffs = least_squares(hess, beta, jnp.float32(0.0), KRYLOV)
    x_fluid = jnp.zeros_like(rhs_fluid)
    x_solid = jnp.zeros_like(rhs_solid)
    for j in range(KRYLOV):
        x_fluid = x_fluid + coeffs[j] * basis[j][0]
        x_solid = x_solid + coeffs[j] * basis[j][1]
    return (x_fluid, x_solid)


def small_solve(hess, beta, zero, steps):
    cos_list, sin_list, upper, inverse = ([], [], [], [])
    rhs_g = [beta] + [zero for _ in range(steps)]
    for j in range(steps):
        column = [hess[i][j] for i in range(j + 2)]
        for i in range(j):
            top = cos_list[i] * column[i] + sin_list[i] * column[i + 1]
            column[i + 1] = -sin_list[i] * column[i] + cos_list[i] * column[i + 1]
            column[i] = top
        scale = lax.rsqrt(column[j] * column[j] + column[j + 1] * column[j + 1])
        cos_now = column[j] * scale
        sin_now = column[j + 1] * scale
        rhs_g[j + 1] = -sin_now * rhs_g[j]
        rhs_g[j] = cos_now * rhs_g[j]
        cos_list.append(cos_now)
        sin_list.append(sin_now)
        upper.append(column[:j])
        inverse.append(scale)
    coeffs = [None] * steps
    for j in range(steps - 1, -1, -1):
        total = rhs_g[j]
        for k in range(j + 1, steps):
            total = total - upper[k][j] * coeffs[k]
        coeffs[j] = total * inverse[j]
    return coeffs


def kernel(
    ns, nf,
    rf_hbm, rs_hbm, bl_hbm, we_hbm, kd_hbm, wf_ref, ws_ref, wc_hbm,
    xf_ref, xs_ref, ok_ref, wc,
    z, u, q, qm, bl, we, wm, kd, hs, hq, sq, he, wall, place, pairs, mpairs, scal, ra, rb,
    tl, th, lp, sb, pk, cb, ir, ib, wl, wh, wsr, pws, wn, pid, el, eh, es,
    in_sem, s_halo, r_halo, s_edge, r_edge, s_wall, r_wall, s_red, r_red, s_pair, r_pair, s_once, r_once,
):
    f32 = jnp.float32
    s = lax.axis_index("span")
    f = lax.axis_index("flow")
    up = (lax.rem(s + 1, ns), f)
    down = (lax.rem(s + ns - 1, ns), f)
    right = (s, lax.rem(f + 1, nf))
    left = (s, lax.rem(f + nf - 1, nf))
    corners = ((up[0], right[1]), (down[0], right[1]), (up[0], left[1]), (down[0], left[1]))

    loads = [
        pltpu.make_async_copy(rf_hbm, z.at[0], in_sem.at[0]),
        pltpu.make_async_copy(rs_hbm, u.at[0], in_sem.at[1]),
        pltpu.make_async_copy(we_hbm, we, in_sem.at[2]),
        pltpu.make_async_copy(bl_hbm, bl, in_sem.at[3]),
        pltpu.make_async_copy(kd_hbm, kd, in_sem.at[4]),
        pltpu.make_async_copy(wc_hbm, wc, in_sem.at[5]),
    ]
    for load in loads:
        load.start()

    cb[...] = jnp.zeros((len(PAIRS), 6, 8, 128), f32)

    barrier = pltpu.get_barrier_semaphore()

    def far_first(n):
        return sorted(range(1, n), key=lambda d: -min(d, n - d))

    flow_peers = [(s, lax.rem(f + d, nf)) for d in far_first(nf)]
    span_peers = [(lax.rem(s + d, ns), f) for d in far_first(ns)]
    for to in span_peers + flow_peers:
        pl.semaphore_signal(barrier, inc=1, device_id=to, device_id_type=MESH)
    for to in corners:
        pl.semaphore_signal(barrier, inc=1, device_id=to, device_id_type=MESH)
    row8 = lax.broadcasted_iota(jnp.int32, (8, 128), 0)
    row16 = lax.broadcasted_iota(jnp.int32, (2, 8, 128), 0) * 8 + lax.broadcasted_iota(
        jnp.int32, (2, 8, 128), 1
    )
    row32 = lax.broadcasted_iota(jnp.int32, (32, 128), 0)
    lane32 = lax.broadcasted_iota(jnp.int32, (32, 128), 1)
    lane1 = lax.broadcasted_iota(jnp.int32, (1, 128), 1)
    eye = row32 == lane32
    loads[5].wait()
    patch = wf_ref[0, 0]
    metal_row = ws_ref[0, 0]
    coef = wc[0]
    wall_mask = jnp.where(row16 == patch, 1.0, 0.0).astype(f32)
    metal_mask = jnp.where(row32 == metal_row, 1.0, 0.0).astype(f32)
    place[pl.ds(f, 1), :] = jnp.where(lane1 == f, metal_row.astype(f32), 0.0)
    has_down = jnp.where(s > 0, 1.0, 0.0).astype(f32)
    has_up = jnp.where(s < ns - 1, 1.0, 0.0).astype(f32)
    has_left = jnp.where(f > 0, 1.0, 0.0).astype(f32)
    has_right = jnp.where(f < nf - 1, 1.0, 0.0).astype(f32)

    def send_rows_flow(buf, k):
        for to in flow_peers:
            pltpu.make_async_remote_copy(
                src_ref=buf.at[pl.ds(f, 1)], dst_ref=buf.at[pl.ds(f, 1)],
                send_sem=s_wall.at[k], recv_sem=r_wall.at[k], device_id=to, device_id_type=MESH,
            ).start()

    def rows_flow(buf, k):
        return pltpu.make_async_remote_copy(
            src_ref=buf.at[pl.ds(0, nf - 1)], dst_ref=buf.at[pl.ds(0, nf - 1)],
            send_sem=s_wall.at[k], recv_sem=r_wall.at[k], device_id=right, device_id_type=MESH,
        )

    def send_rows_span(buf, k):
        for to in span_peers:
            pltpu.make_async_remote_copy(
                src_ref=buf.at[pl.ds(s, 1)], dst_ref=buf.at[pl.ds(s, 1)],
                send_sem=s_red.at[k], recv_sem=r_red.at[k], device_id=to, device_id_type=MESH,
            ).start()

    def rows_span(buf, k):
        return pltpu.make_async_remote_copy(
            src_ref=buf.at[pl.ds(0, ns - 1)], dst_ref=buf.at[pl.ds(0, ns - 1)],
            send_sem=s_red.at[k], recv_sem=r_red.at[k], device_id=up, device_id_type=MESH,
        )

    def halos(k):
        def copy(n, src, dst, to):
            return pltpu.make_async_remote_copy(
                src_ref=src, dst_ref=dst, send_sem=s_halo.at[k, n], recv_sem=r_halo.at[k, n],
                device_id=to, device_id_type=MESH,
            )

        return [
            copy(0, z.at[k, :, 1], hs.at[k, 0], up),
            copy(1, z.at[k, :, 0], hs.at[k, 1], down),
            copy(2, sq.at[k, 0], hq.at[k, 0], right),
            copy(3, sq.at[k, 1], hq.at[k, 1], left),
        ]

    def edges(k):
        def copy(n, src, dst, to):
            return pltpu.make_async_remote_copy(
                src_ref=src, dst_ref=dst, send_sem=s_edge.at[k, n], recv_sem=r_edge.at[k, n],
                device_id=to, device_id_type=MESH,
            )

        return [
            copy(0, u.at[k, pl.ds(31, 1)], he.at[k, 0, pl.ds(0, 1)], up),
            copy(1, u.at[k, pl.ds(0, 1)], he.at[k, 1, pl.ds(0, 1)], down),
        ]

    def send_halos(k):
        out = halos(k)
        out[0].start()
        out[1].start()
        for g in range(6):
            for a in range(2):
                i = 2 * g + a
                sq[k, 0, i : i + 1, :] = z[k, g, a, 7:8, :]
                sq[k, 1, i : i + 1, :] = z[k, g, a, 0:1, :]
        out[2].start()
        out[3].start()

    def remote(src, dst, send, recv, to):
        return pltpu.make_async_remote_copy(
            src_ref=src, dst_ref=dst, send_sem=send, recv_sem=recv, device_id=to, device_id_type=MESH
        )

    def pair_copies(k):
        p = PAIRS.index(k)

        def copy(n, src, dst, to):
            return remote(src, dst, s_pair.at[p, n], r_pair.at[p, n], to)

        return [
            copy(0, z.at[k, :, 1], tl.at[p, :, 1], up),
            copy(1, z.at[k, :, 0], th.at[p, :, 0], down),
            copy(4, pk.at[p, :, pl.ds(5, 1)], cb.at[p, :, pl.ds(0, 1)], corners[0]),
            copy(5, pk.at[p, :, pl.ds(4, 1)], cb.at[p, :, pl.ds(1, 1)], corners[1]),
            copy(6, pk.at[p, :, pl.ds(1, 1)], cb.at[p, :, pl.ds(4, 1)], corners[2]),
            copy(7, pk.at[p, :, pl.ds(0, 1)], cb.at[p, :, pl.ds(5, 1)], corners[3]),
            copy(12, lp.at[p, :, 1], tl.at[p, :, 0], up),
            copy(13, lp.at[p, :, 0], th.at[p, :, 1], down),
            copy(2, pk.at[p, :, pl.ds(4, 4)], sb.at[p, :, pl.ds(0, 4)], right),
            copy(3, pk.at[p, :, pl.ds(0, 4)], sb.at[p, :, pl.ds(4, 4)], left),
        ]

    def inflow_copies(k):
        p = PAIRS.index(k)
        return [
            remote(
                ir.at[p, pl.ds(0, 1)], ib.at[p, pl.ds(n, 1)],
                s_pair.at[p, 8 + n], r_pair.at[p, 8 + n], to,
            )
            for n, to in enumerate((up, down, right, left))
        ]

    def once_copies():
        def copy(n, src, dst, to):
            return remote(src, dst, s_once.at[n], r_once.at[n], to)

        out = [
            copy(0, we.at[:, 1], wl, up),
            copy(1, we.at[:, 0], wh, down),
            copy(2, pws.at[:, pl.ds(4, 4)], wsr.at[:, pl.ds(0, 4)], right),
            copy(3, pws.at[:, pl.ds(0, 4)], wsr.at[:, pl.ds(4, 4)], left),
        ]
        return out + [
            copy(4 + m, pid.at[pl.ds(4, 1)], pid.at[pl.ds(m, 1)], to)
            for m, to in enumerate((up, down, right, left))
        ]

    PACK = ((0, 0, 0), (1, 0, 1), (4, 7, 0), (5, 7, 1))

    def pack_once():
        for i in range(6):
            for m, b, a in PACK:
                pws[i, m : m + 1, :] = we[i, a, b : b + 1, :]
                pws[i, m + 2 : m + 3, :] = we[i, a, b : b + 1, :]
        pid[4:5, :] = jnp.broadcast_to(patch.astype(f32), (1, 128))

    def prepare_pairs():
        wn[0] = jnp.where(row8 == 0, has_left * wl[2], 0.0)
        wn[1] = jnp.where(row8 == 7, has_right * wl[3], 0.0)
        wn[2] = jnp.where(row8 == 0, has_left * wh[2], 0.0)
        wn[3] = jnp.where(row8 == 7, has_right * wh[3], 0.0)
        first = (row8 == 0) | (row8 == 4)
        wn[4] = jnp.where(first, has_down * wsr[0], has_up * wsr[1])
        wn[7] = jnp.where(row8 < 4, wsr[3], wsr[2])
        here = row8.astype(f32)
        wn[8] = jnp.where(here + 8.0 == pid[0:1, :], 1.0, 0.0)
        wn[9] = jnp.where(here == pid[1:2, :], 1.0, 0.0)
        side = jnp.where((row8 == 0) & (pid[2:3, :] == 7.0), 1.0, 0.0)
        side = side + jnp.where((row8 == 1) & (pid[2:3, :] == 15.0), 1.0, 0.0)
        side = side + jnp.where((row8 == 4) & (pid[3:4, :] == 0.0), 1.0, 0.0)
        wn[10] = side + jnp.where((row8 == 5) & (pid[3:4, :] == 8.0), 1.0, 0.0)

    def beside_cells(k):
        p = PAIRS.index(k)
        for g in range(6):
            el[g] = (
                tl[p, g, 0] - wl[1] * z[k, g, 0]
                - wn[0] * cb[p, g, 0:1, :] - wn[1] * cb[p, g, 4:5, :]
            )
            eh[g] = (
                th[p, g, 1] - wh[0] * z[k, g, 1]
                - wn[2] * cb[p, g, 1:2, :] - wn[3] * cb[p, g, 5:6, :]
            )
            es[g] = pltpu.roll(sb[p, g], 6, 0) - wn[4] * cb[p, g] - wn[7] * pk[p, g]

    def beside_inflow(k):
        p = PAIRS.index(k)
        el[5] = el[5] - wn[8] * ib[p, 0:1, :]
        eh[5] = eh[5] - wn[9] * ib[p, 1:2, :]
        es[5] = es[5] - wn[10] * jnp.where(row8 < 4, ib[p, 2:3, :], ib[p, 3:4, :])

    def local_part(k):
        field = [z[k, g] for g in range(6)]
        for g in range(6):
            v = field[g]
            total = bl[g, 0] * field[0]
            for h in range(1, 6):
                total = total + bl[g, h] * field[h]
            total = total - we[4] * pltpu.roll(v, 1, 2) - we[5] * pltpu.roll(v, 127, 2)
            total = total - wm[0] * pltpu.roll(v, 1, 1) - wm[1] * pltpu.roll(v, 7, 1)
            z[k + 1, g, 0] = total[0] - we[1, 0] * v[1]
            z[k + 1, g, 1] = total[1] - we[0, 1] * v[0]

    def halo_part(k, metal_here, low, high, west, east):
        inflow = coef * metal_here
        for g in range(6):
            for a in range(2):
                total = z[k + 1, g, a]
                if a == 0:
                    total = total - wm[4, 0] * low(g)
                else:
                    total = total - wm[4, 1] * high(g)
                total = total - wm[2, a] * west(g, a) - wm[3, a] * east(g, a)
                if g == 5:
                    total = total - wall_mask[a] * inflow
                z[k + 1, g, a] = total

    def own_metal(values):
        return jnp.sum(metal_mask * values, axis=0, keepdims=True)

    def wall_value(k):
        picked = wall_mask[0] * z[k, 5, 0] + wall_mask[1] * z[k, 5, 1]
        return coef * jnp.sum(picked, axis=0, keepdims=True)

    def metal_local(k):
        v = u[k]
        total = (4.0 + kd[...]) * v - pltpu.roll(v, 1, 1) - pltpu.roll(v, 127, 1)
        below = jnp.where(row32 == 0, has_down * he[k, 0, 0:1, :], pltpu.roll(v, 1, 0))
        above = jnp.where(row32 == 31, has_up * he[k, 1, 0:1, :], pltpu.roll(v, 31, 0))
        return total - below - above

    def dot_row(store, i, j):
        total = store[i, 0, 0] * store[j, 0, 0] + store[i, 0, 1] * store[j, 0, 1]
        for g in range(1, 6):
            total = total + store[i, g, 0] * store[j, g, 0] + store[i, g, 1] * store[j, g, 1]
        return jnp.sum(total, axis=0, keepdims=True)

    def metal_dot_row(i, j):
        t = qm[i] * qm[j]
        t = (t[0:8] + t[8:16]) + (t[16:24] + t[24:32])
        return jnp.sum(t, axis=0, keepdims=True)

    def packed(rows, low, high):
        sums = jnp.sum(rows[low:high, :], axis=1, keepdims=True)
        return jnp.sum(jnp.where(eye[low:high], sums, 0.0), axis=0, keepdims=True)

    def unpack(total):
        sums = jnp.sum(jnp.where(eye, total, 0.0), axis=1, keepdims=True)
        scal[...] = jnp.broadcast_to(sums, (32, 128))

    loads[0].wait()
    for g in range(6):
        for a in range(2):
            i = 2 * g + a
            sq[0, 0, i : i + 1, :] = z[0, g, a, 7:8, :]
            sq[0, 1, i : i + 1, :] = z[0, g, a, 0:1, :]
    sq[:, :, 12:16, :] = jnp.zeros((KRYLOV, 2, 4, 128), f32)
    pl.semaphore_wait(barrier, ns + nf + 2)
    for copy in halos(0):
        copy.start()
    loads[1].wait()
    for copy in edges(0):
        copy.start()
    pairs[...] = jnp.zeros((32, 128), f32)
    mpairs[...] = jnp.zeros((32, 128), f32)
    loads[2].wait()
    wm[0] = jnp.where(row8 == 0, 0.0, we[2])
    wm[1] = jnp.where(row8 == 7, 0.0, we[3])
    wm[2] = jnp.where(row8 == 0, has_left * we[2], 0.0)
    wm[3] = jnp.where(row8 == 7, has_right * we[3], 0.0)
    wm[4, 0] = has_down * we[0, 0]
    wm[4, 1] = has_up * we[1, 1]
    loads[3].wait()
    loads[4].wait()

    own = []
    state = {}

    def wall_step(k):
        wall[k, pl.ds(f, 1), :] = wall_value(k)
        send_rows_flow(wall.at[k], k)

    def metal_step(k):
        if k == 1:
            rows_flow(place, KRYLOV).wait_recv()
            places = jnp.sum(place[...], axis=0, keepdims=True)
            state["pick"] = jnp.where((row32.astype(f32) == places) & (lane32 < 32), 1.0, 0.0)[:, 0:32]
        if k > 0:
            rows_flow(wall.at[k - 1], k - 1).wait_recv()
            sink = jnp.dot(
                state["pick"], wall[k - 1],
                precision=lax.Precision.HIGHEST, preferred_element_type=f32,
            )
            for copy in edges(k - 1):
                copy.wait_recv()
            u[k] = metal_local(k - 1) - sink
            for copy in edges(k):
                copy.start()
        own.append(own_metal(u[k]))

    def early_gram():
        n = 0
        for i in range(EARLY):
            for j in range(i, EARLY):
                pairs[n : n + 1, :] = dot_row(z, i, j)
                n += 1
        ra[0, pl.ds(f, 1), :] = packed(pairs, 0, 32)
        send_rows_flow(ra.at[0], KRYLOV + 1)

    def early_span():
        rows_flow(ra.at[0], KRYLOV + 1).wait_recv()
        rb[0, pl.ds(s, 1), :] = jnp.sum(ra[0], axis=0, keepdims=True)
        send_rows_span(rb.at[0], 0)

    def basis():
        rows_span(rb.at[0], 0).wait_recv()
        unpack(jnp.sum(rb[0], axis=0, keepdims=True))
        gram = {}
        n = 0
        for i in range(EARLY):
            for j in range(i, EARLY):
                gram[i, j] = scal[n : n + 1, :]
                n += 1
        r = {}
        inv = []
        trust = []
        for i in range(EARLY):
            for j in range(i, EARLY):
                t = gram[i, j]
                for h in range(i):
                    t = t - r[h, i] * r[h, j]
                if i == j:
                    floor = gram[i, i] * 1e-5
                    trust.append(t > floor)
                    t = jnp.maximum(t, floor)
                    inv.append(lax.rsqrt(t))
                r[i, j] = t * inv[i]
        ratio = [r[i, i + 1] * inv[i] for i in range(EARLY - 1)]
        coef_a = [ratio[0]]
        coef_b = [None, r[1, 1] * inv[0]]
        good = trust[1]
        for i in range(1, EARLY - 1):
            good = good & trust[i + 1]
            coef_a.append(jnp.where(good, ratio[i] - ratio[i - 1], coef_a[i - 1]))
            guess = coef_b[1] * 1.22
            coef_b.append(jnp.where(good, r[i + 1, i + 1] * inv[i], guess))
        while len(coef_a) < KRYLOV:
            coef_a.append(coef_a[-1])
        while len(coef_b) < KRYLOV + 1:
            coef_b.append(coef_b[-1])
        poly = [[inv[0]]]
        for i in range(KRYLOV):
            back = 1.0 / coef_b[i + 1]
            new = []
            for j in range(i + 2):
                t = None
                if j >= 1:
                    t = poly[i][j - 1]
                if j <= i:
                    t = -coef_a[i] * poly[i][j] if t is None else t - coef_a[i] * poly[i][j]
                if i >= 1 and j <= i - 1:
                    t = t - coef_b[i] * poly[i - 1][j]
                new.append(t * back)
            poly.append(new)
        size = [jnp.sqrt(gram[i, i]) for i in range(EARLY)]
        growth = size[-1] / size[-2]
        while len(size) < KRYLOV:
            size.append(size[-1] * growth)
        spread = []
        for i in range(KRYLOV):
            t = jnp.abs(poly[i][0]) * size[0]
            for j in range(1, i + 1):
                t = t + jnp.abs(poly[i][j]) * size[j]
            spread.append(t)
        return coef_a, coef_b, poly, spread

    def combine(low, high, first):
        poly = state["basis"][2]
        for i in range(low, KRYLOV + 1):
            terms = range(low, min(i, high) + 1)
            if not terms:
                continue
            for g in range(6):
                t = None if first else q[i, g]
                for j in terms:
                    t = poly[i][j] * z[j, g] if t is None else t + poly[i][j] * z[j, g]
                q[i, g] = t

    def metal_combine(low, high, first):
        poly = state["basis"][2]
        for i in range(low, KRYLOV + 1):
            t = None if first else qm[i]
            for j in range(low, min(i, high) + 1):
                t = poly[i][j] * u[j] if t is None else t + poly[i][j] * u[j]
            qm[i] = t

    def place_of(j, i):
        return 24 + j if i == KRYLOV else i * (i + 1) // 2 + j

    def gram_rows(low, high):
        for i in range(low, high + 1):
            for j in range(i + 1):
                n = place_of(j, i)
                pairs[n : n + 1, :] = dot_row(q, j, i)

    def metal_gram_rows(low, high):
        for i in range(low, high + 1):
            for j in range(i + 1):
                n = place_of(j, i)
                mpairs[n : n + 1, :] = metal_dot_row(j, i)

    early = [k for k, _ in PLAN if k >= EARLY - 1][0]
    when = [k for k, _ in PLAN].index(early)
    for step, (k, width) in enumerate(PLAN):
        if k > 0:
            if width == 1:
                send_halos(k)
            else:
                p = PAIRS.index(k)
                copies = pair_copies(k)
                for copy in copies[:2]:
                    copy.start()
                for g in range(6):
                    for m, b, a in PACK:
                        pk[p, g, m : m + 1, :] = z[k, g, a, b : b + 1, :]
                for copy in copies[2:6]:
                    copy.start()
        if step == when:
            early_gram()
        wall_step(k)
        if k == 0:
            send_rows_flow(place, KRYLOV)
            pack_once()
            for copy in once_copies():
                copy.start()
        local_part(k)
        if width == 2:
            for g in range(6):
                for a in range(2):
                    lp[p, g, a] = z[k + 1, g, a]
                for m, b, a in PACK:
                    pk[p, g, m + 2 : m + 3, :] = z[k + 1, g, a, b : b + 1, :]
            for copy in copies[6:]:
                copy.start()
        metal_step(k)
        if width == 2:
            p = PAIRS.index(k)
            ir[p, 0:1, :] = coef * own[k]
            for copy in inflow_copies(k):
                copy.start()
        if step == when + 1:
            early_span()
        if step == when + 3:
            state["basis"] = basis()
            combine(0, k, True)
            gram_rows(0, k)
        if width == 1:
            for copy in halos(k):
                copy.wait_recv()
            halo_part(
                k, own[k], lambda g: hs[k, 0, g], lambda g: hs[k, 1, g],
                lambda g, a: hq[k, 0, 2 * g + a : 2 * g + a + 1, :],
                lambda g, a: hq[k, 1, 2 * g + a : 2 * g + a + 1, :],
            )
        else:
            if k == PAIRS[0]:
                for copy in once_copies():
                    copy.wait_recv()
                prepare_pairs()
            for copy in pair_copies(k):
                copy.wait_recv()
            halo_part(
                k, own[k], lambda g: tl[p, g, 1], lambda g: th[p, g, 0],
                lambda g, a: sb[p, g, a : a + 1, :],
                lambda g, a: sb[p, g, 4 + a : 5 + a, :],
            )
            wall_step(k + 1)
            beside_cells(k)
            local_part(k + 1)
            if k + 1 == KRYLOV - 1:
                combine(k + 1, k + 1, False)
                gram_rows(k + 1, k + 1)
            for copy in inflow_copies(k):
                copy.wait_recv()
            beside_inflow(k)
            metal_step(k + 1)
            halo_part(
                k + 1, own[k + 1], lambda g: el[g], lambda g: eh[g],
                lambda g, a: es[g, a : a + 1, :],
                lambda g, a: es[g, 4 + a : 5 + a, :],
            )

    last = KRYLOV
    combine(last, last, False)
    gram_rows(last, last)
    ra[1, pl.ds(f, 1), :] = packed(pairs, 0, 32)
    send_rows_flow(ra.at[1], KRYLOV + 2)
    coef_a, coef_b, poly, spread = state["basis"]
    metal_combine(0, last - 1, True)
    metal_gram_rows(0, last - 1)
    rows_flow(wall.at[last - 1], last - 1).wait_recv()
    sink = jnp.dot(
        state["pick"], wall[last - 1], precision=lax.Precision.HIGHEST, preferred_element_type=f32
    )
    for copy in edges(last - 1):
        copy.wait_recv()
    qm[last] = qm[last] + poly[last][last] * (metal_local(last - 1) - sink)
    metal_gram_rows(last, last)
    metal_done = packed(mpairs, 0, 32)
    rows_flow(ra.at[1], KRYLOV + 2).wait_recv()
    rb[1, pl.ds(s, 1), :] = jnp.sum(ra[1], axis=0, keepdims=True) + metal_done
    send_rows_span(rb.at[1], 1)
    for k, width in PLAN:
        for copy in halos(k) if width == 1 else pair_copies(k) + inflow_copies(k):
            copy.wait_send()
    for copy in once_copies():
        copy.wait_send()
    for k in range(KRYLOV):
        for copy in edges(k):
            copy.wait_send()
    for k in range(KRYLOV):
        rows_flow(wall.at[k], k).wait_send()
    rows_flow(place, KRYLOV).wait_send()
    rows_flow(ra.at[0], KRYLOV + 1).wait_send()
    rows_flow(ra.at[1], KRYLOV + 2).wait_send()
    rows_span(rb.at[0], 0).wait_send()
    rows_span(rb.at[1], 1).wait()
    unpack(jnp.sum(rb[1], axis=0, keepdims=True))
    gram = {}
    n = 0
    for i in range(KRYLOV + 1):
        for j in range(i + 1):
            m = 24 + j if i == KRYLOV else n
            gram[j, i] = scal[m : m + 1, :]
            n += 1
    r = {}
    low = None
    for i in range(KRYLOV + 1):
        scale = None
        for j in range(i, KRYLOV + 1):
            t = gram[i, j]
            for h in range(i):
                t = t - r[h, i] * r[h, j]
            if i == j:
                rel = t / gram[i, i]
                low = rel if low is None else jnp.minimum(low, rel)
                scale = lax.rsqrt(t)
            r[i, j] = t * scale
    zero = jnp.zeros((1, 128), f32)
    hess = [[zero] * KRYLOV for _ in range(KRYLOV + 1)]
    for j in range(KRYLOV):
        for i in range(j + 2):
            t = r[i, j + 1] * coef_b[j + 1]
            if i <= j:
                t = t + r[i, j] * coef_a[j]
            if i <= j - 1:
                t = t + r[i, j - 1] * coef_b[j]
            hess[i][j] = t
    y = small_solve(hess, r[0, 0] / poly[0][0], zero, KRYLOV)
    top = jnp.abs(y[0])
    total = jnp.abs(y[0]) * spread[0]
    for k in range(1, KRYLOV):
        top = jnp.maximum(top, jnp.abs(y[k]))
        total = total + jnp.abs(y[k]) * spread[k]
    fine = (low > 1e-2) & (total < 1e3 * top)
    ok_ref[...] = jnp.where(fine, 1.0, 0.0)
    for g in range(6):
        t = y[0] * q[0, g]
        for k in range(1, KRYLOV):
            t = t + y[k] * q[k, g]
        xf_ref[g] = t
    out = None
    for j in range(KRYLOV):
        c = y[j] * poly[j][j]
        for k in range(j + 1, KRYLOV):
            c = c + y[k] * poly[k][j]
        out = c * u[j] if out is None else out + c * u[j]
    xs_ref[...] = out


def store(a_ref, b_ref, a_out, b_out, sem):
    copies = [
        pltpu.make_async_copy(a_ref, a_out, sem.at[0]),
        pltpu.make_async_copy(b_ref, b_out, sem.at[1]),
    ]
    for copy in copies:
        copy.start()
    for copy in copies:
        copy.wait()


def shards(ns, nf, *args):
    rhs_fluid, rhs_solid = args[0], args[1]
    f32 = jnp.float32
    hbm = pl.BlockSpec(memory_space=pltpu.HBM)
    vmem = pl.BlockSpec(memory_space=pltpu.VMEM)
    smem = pl.BlockSpec(memory_space=pltpu.SMEM)
    dma = pltpu.SemaphoreType.DMA
    x_fluid, x_solid, ok, coef = pl.pallas_call(
        functools.partial(kernel, ns, nf),
        name="gmres",
        out_shape=(
            jax.ShapeDtypeStruct(rhs_fluid.shape, f32),
            jax.ShapeDtypeStruct(rhs_solid.shape, f32),
            jax.ShapeDtypeStruct((1, 128), f32),
            jax.ShapeDtypeStruct(args[-1].shape, f32),
        ),
        in_specs=[hbm] * 5 + [smem] * 2 + [hbm],
        out_specs=(vmem,) * 4,
        scratch_shapes=[
            pltpu.VMEM((KRYLOV + 1, 6, 2, 8, 128), f32),
            pltpu.VMEM((KRYLOV, 32, 128), f32),
            pltpu.VMEM((KRYLOV + 1, 6, 2, 8, 128), f32),
            pltpu.VMEM((KRYLOV + 1, 32, 128), f32),
            pltpu.VMEM((6, 6, 2, 8, 128), f32),
            pltpu.VMEM((6, 2, 8, 128), f32),
            pltpu.VMEM((5, 2, 8, 128), f32),
            pltpu.VMEM((32, 128), f32),
            pltpu.VMEM((KRYLOV, 2, 6, 8, 128), f32),
            pltpu.VMEM((KRYLOV, 2, 16, 128), f32),
            pltpu.VMEM((KRYLOV, 2, 16, 128), f32),
            pltpu.VMEM((KRYLOV, 2, 8, 128), f32),
            pltpu.VMEM((KRYLOV, 32, 128), f32),
            pltpu.VMEM((32, 128), f32),
            pltpu.VMEM((32, 128), f32),
            pltpu.VMEM((32, 128), f32),
            pltpu.VMEM((32, 128), f32),
            pltpu.VMEM((2, 32, 128), f32),
            pltpu.VMEM((2, 16, 128), f32),
            pltpu.VMEM((len(PAIRS), 6, 2, 8, 128), f32),
            pltpu.VMEM((len(PAIRS), 6, 2, 8, 128), f32),
            pltpu.VMEM((len(PAIRS), 6, 2, 8, 128), f32),
            pltpu.VMEM((len(PAIRS), 6, 8, 128), f32),
            pltpu.VMEM((len(PAIRS), 6, 8, 128), f32),
            pltpu.VMEM((len(PAIRS), 6, 8, 128), f32),
            pltpu.VMEM((len(PAIRS), 8, 128), f32),
            pltpu.VMEM((len(PAIRS), 8, 128), f32),
            pltpu.VMEM((6, 8, 128), f32),
            pltpu.VMEM((6, 8, 128), f32),
            pltpu.VMEM((6, 8, 128), f32),
            pltpu.VMEM((6, 8, 128), f32),
            pltpu.VMEM((11, 8, 128), f32),
            pltpu.VMEM((8, 128), f32),
            pltpu.VMEM((6, 8, 128), f32),
            pltpu.VMEM((6, 8, 128), f32),
            pltpu.VMEM((6, 8, 128), f32),
            dma((6,)),
            dma((KRYLOV, 4)), dma((KRYLOV, 4)),
            dma((KRYLOV, 2)), dma((KRYLOV, 2)),
            dma((KRYLOV + 3,)), dma((KRYLOV + 3,)),
            dma((2,)), dma((2,)),
            dma((len(PAIRS), 14)), dma((len(PAIRS), 14)),
            dma((8,)), dma((8,)),
        ],
        compiler_params=pltpu.CompilerParams(
            collective_id=0, has_side_effects=True, vmem_limit_bytes=8 * 1024 * 1024
        ),
    )(*args)
    def place_out(*a):
        return pl.pallas_call(
            store,
            name="place_out",
            out_shape=(
                jax.ShapeDtypeStruct(rhs_fluid.shape, f32),
                jax.ShapeDtypeStruct(rhs_solid.shape, f32),
            ),
            in_specs=[vmem, vmem],
            out_specs=(hbm, hbm),
            scratch_shapes=[dma((2,))],
        )(x_fluid, x_solid)

    return lax.cond(ok[0, 0] > 0.5, place_out, lambda *a: arnoldi(*a), *args[:-1], coef)


def solution(mesh):
    in_specs = (
        P(None, "span", "flow", None),
        P("span", None),
        P(None, None, "span", "flow", None),
        P(None, "span", "flow", None),
        P("span", None),
        P("span", "flow"),
        P("span", "flow"),
        P("span", "flow", None),
    )
    out_specs = (P(None, "span", "flow", None), P("span", None))
    return jax.shard_map(
        functools.partial(shards, mesh.shape["span"], mesh.shape["flow"]),
        mesh=mesh, in_specs=in_specs, out_specs=out_specs, check_vma=False,
    )
```

```python
import functools

import jax
import jax.numpy as jnp
from jax import lax
from jax.experimental import pallas as pl
from jax.experimental.pallas import tpu as pltpu
from jax.sharding import PartitionSpec as P

KRYLOV = 6
MESH = pl.DeviceIdType.MESH
EARLY = 2
PLAN = ((0, 1), (1, 1), (2, 1), (3, 1), (4, 2))
PAIRS = tuple(k for k, width in PLAN if width == 2)


def extended(shard, sides, width):
    for axis, dim in sides:
        count, length = (lax.axis_size(axis), shard.shape[dim])
        up = [(i, (i + 1) % count) for i in range(count - 1)]
        down = [(j, i) for i, j in up]
        last = lax.slice_in_dim(shard, length - width, length, axis=dim)
        first = lax.slice_in_dim(shard, 0, width, axis=dim)
        before = lax.ppermute(last, axis, up)
        after = lax.ppermute(first, axis, down)
        shard = jnp.concatenate([before, shard, after], axis=dim)
    return shard


def back_substitute(upper, rhs_g, steps):
    coeffs = [None] * steps
    for j in range(steps - 1, -1, -1):
        total = rhs_g[j]
        for k in range(j + 1, steps):
            total = total - upper[k][j] * coeffs[k]
        coeffs[j] = total / upper[j][j]
    return coeffs


def least_squares(hess, beta, zero, steps):
    cos_list, sin_list, upper = ([], [], [])
    rhs_g = [beta] + [zero for _ in range(steps)]
    for j in range(steps):
        column = [hess[i][j] for i in range(j + 2)]
        for i in range(j):
            top = cos_list[i] * column[i] + sin_list[i] * column[i + 1]
            column[i + 1] = -sin_list[i] * column[i] + cos_list[i] * column[i + 1]
            column[i] = top
        radius = jnp.sqrt(column[j] * column[j] + column[j + 1] * column[j + 1])
        cos_now = column[j] / radius
        sin_now = column[j + 1] / radius
        column[j] = radius
        rhs_g[j + 1] = -sin_now * rhs_g[j]
        rhs_g[j] = cos_now * rhs_g[j]
        cos_list.append(cos_now)
        sin_list.append(sin_now)
        upper.append(column[: j + 1])
    return back_substitute(upper, rhs_g, steps)


def arnoldi(rhs_fluid, rhs_solid, blocks, weights, kdiag, wall_fluid, wall_solid, wall_coef):
    rows_a = rhs_fluid.shape[1]
    rows_b = rhs_fluid.shape[2]
    width = rhs_fluid.shape[3]
    cells = rows_a * rows_b
    band_rows = rhs_solid.shape[0]
    patch_rows = wall_fluid[0]
    patch_metal = wall_solid[0]
    coef = wall_coef[0]
    fluid_pick = (jnp.arange(cells, dtype=jnp.int32)[:, None] == patch_rows[None, :]).astype(
        jnp.float32
    )
    metal_pick = (jnp.arange(band_rows, dtype=jnp.int32)[:, None] == patch_metal[None, :]).astype(
        jnp.float32
    )
    first_flow = (lax.axis_index("flow") == 0).astype(jnp.float32)
    highest = lax.Precision.HIGHEST

    def local_inner(left, right):
        return jnp.sum(left[0] * right[0]) + first_flow * jnp.sum(left[1] * right[1])

    beta = jnp.sqrt(
        lax.psum(local_inner((rhs_fluid, rhs_solid), (rhs_fluid, rhs_solid)), ("span", "flow"))
    )
    basis = [(rhs_fluid / beta, rhs_solid / beta)]
    hess = [[jnp.float32(0.0) for _ in range(KRYLOV)] for _ in range(KRYLOV + 1)]
    for j in range(KRYLOV):
        field = basis[j][0]
        metal_u = basis[j][1]
        padded = extended(field, (("span", 1), ("flow", 2)), 1)
        local = jnp.einsum("fgabc,gabc->fabc", blocks, field, precision=highest)
        beside = weights[0][None] * padded[:, :-2, 1:-1] + weights[1][None] * padded[:, 2:, 1:-1]
        beside = (
            beside
            + weights[2][None] * padded[:, 1:-1, :-2]
            + weights[3][None] * padded[:, 1:-1, 2:]
        )
        beside = (
            beside
            + weights[4][None] * jnp.roll(field, 1, axis=3)
            + weights[5][None] * jnp.roll(field, -1, axis=3)
        )
        metal_at = jnp.dot(metal_pick.T, metal_u, precision=highest)
        inflow = jnp.dot(fluid_pick, coef * metal_at, precision=highest).reshape(
            rows_a, rows_b, width
        )
        image_f = (local - beside).at[5].add(-inflow)
        wall_vals = coef * jnp.dot(fluid_pick.T, field[5].reshape(cells, width), precision=highest)
        sink = lax.psum(jnp.dot(metal_pick, wall_vals, precision=highest), "flow")
        upad = extended(metal_u, (("span", 0),), 1)
        beside_all = (
            upad[:-2] + upad[2:] + jnp.roll(metal_u, 1, axis=1) + jnp.roll(metal_u, -1, axis=1)
        )
        image_s = (4.0 + kdiag) * metal_u - beside_all - sink
        terms = jnp.stack([local_inner(basis[i], (image_f, image_s)) for i in range(j + 1)])
        values = lax.psum(terms, ("span", "flow"))
        for i in range(j + 1):
            image_f = image_f - values[i] * basis[i][0]
            image_s = image_s - values[i] * basis[i][1]
        rest = jnp.sqrt(
            lax.psum(local_inner((image_f, image_s), (image_f, image_s)), ("span", "flow"))
        )
        for i in range(j + 1):
            hess[i][j] = values[i]
        hess[j + 1][j] = rest
        basis.append((image_f / rest, image_s / rest))
    coeffs = least_squares(hess, beta, jnp.float32(0.0), KRYLOV)
    x_fluid = jnp.zeros_like(rhs_fluid)
    x_solid = jnp.zeros_like(rhs_solid)
    for j in range(KRYLOV):
        x_fluid = x_fluid + coeffs[j] * basis[j][0]
        x_solid = x_solid + coeffs[j] * basis[j][1]
    return (x_fluid, x_solid)


def small_solve(hess, beta, zero, steps):
    cos_list, sin_list, upper, inverse = ([], [], [], [])
    rhs_g = [beta] + [zero for _ in range(steps)]
    for j in range(steps):
        column = [hess[i][j] for i in range(j + 2)]
        for i in range(j):
            top = cos_list[i] * column[i] + sin_list[i] * column[i + 1]
            column[i + 1] = -sin_list[i] * column[i] + cos_list[i] * column[i + 1]
            column[i] = top
        scale = lax.rsqrt(column[j] * column[j] + column[j + 1] * column[j + 1])
        cos_now = column[j] * scale
        sin_now = column[j + 1] * scale
        rhs_g[j + 1] = -sin_now * rhs_g[j]
        rhs_g[j] = cos_now * rhs_g[j]
        cos_list.append(cos_now)
        sin_list.append(sin_now)
        upper.append(column[:j])
        inverse.append(scale)
    coeffs = [None] * steps
    for j in range(steps - 1, -1, -1):
        total = rhs_g[j]
        for k in range(j + 1, steps):
            total = total - upper[k][j] * coeffs[k]
        coeffs[j] = total * inverse[j]
    return coeffs


def kernel(
    ns, nf,
    rf_hbm, rs_hbm, bl_hbm, we_hbm, kd_hbm, wf_ref, ws_ref, wc_hbm,
    xf_ref, xs_ref, ok_ref, wc,
    z, u, q, qm, bl, we, wm, kd, hs, hq, sq, sinks, wall, place, pairs, mpairs, scal, ra, rb,
    tl, th, lp, sb, pk, cb, ir, ib, wl, wh, wsr, pws, wn, pid, el, eh, es,
    in_sem, s_halo, r_halo, s_edge, r_edge, s_wall, r_wall, s_red, r_red, s_pair, r_pair, s_once, r_once,
):
    f32 = jnp.float32
    s = lax.axis_index("span")
    f = lax.axis_index("flow")
    up = (lax.rem(s + 1, ns), f)
    down = (lax.rem(s + ns - 1, ns), f)
    right = (s, lax.rem(f + 1, nf))
    left = (s, lax.rem(f + nf - 1, nf))
    corners = ((up[0], right[1]), (down[0], right[1]), (up[0], left[1]), (down[0], left[1]))

    loads = [
        pltpu.make_async_copy(rf_hbm, z.at[0], in_sem.at[0]),
        pltpu.make_async_copy(rs_hbm, u.at[0, pl.ds(8, 32)], in_sem.at[1]),
        pltpu.make_async_copy(we_hbm, we, in_sem.at[2]),
        pltpu.make_async_copy(bl_hbm, bl, in_sem.at[3]),
        pltpu.make_async_copy(kd_hbm, kd.at[pl.ds(8, 32)], in_sem.at[4]),
        pltpu.make_async_copy(wc_hbm, wc, in_sem.at[5]),
    ]
    for load in loads:
        load.start()

    cb[...] = jnp.zeros((len(PAIRS), 6, 8, 128), f32)

    barrier = pltpu.get_barrier_semaphore()

    def far_first(n):
        return sorted(range(1, n), key=lambda d: -min(d, n - d))

    flow_peers = [(s, lax.rem(f + d, nf)) for d in far_first(nf)]
    span_peers = [(lax.rem(s + d, ns), f) for d in far_first(ns)]
    for to in span_peers + flow_peers:
        pl.semaphore_signal(barrier, inc=1, device_id=to, device_id_type=MESH)
    for to in corners:
        pl.semaphore_signal(barrier, inc=1, device_id=to, device_id_type=MESH)
    row8 = lax.broadcasted_iota(jnp.int32, (8, 128), 0)
    row16 = lax.broadcasted_iota(jnp.int32, (2, 8, 128), 0) * 8 + lax.broadcasted_iota(
        jnp.int32, (2, 8, 128), 1
    )
    row32 = lax.broadcasted_iota(jnp.int32, (32, 128), 0)
    lane32 = lax.broadcasted_iota(jnp.int32, (32, 128), 1)
    lane1 = lax.broadcasted_iota(jnp.int32, (1, 128), 1)
    eye = row32 == lane32
    loads[5].wait()
    patch = wf_ref[0, 0]
    metal_row = ws_ref[0, 0]
    coef = wc[0]
    wall_mask = jnp.where(row16 == patch, 1.0, 0.0).astype(f32)
    metal_mask = jnp.where(row32 == metal_row, 1.0, 0.0).astype(f32)
    place[pl.ds(f, 1), :] = jnp.where(lane1 == f, metal_row.astype(f32), 0.0)
    has_down = jnp.where(s > 0, 1.0, 0.0).astype(f32)
    has_up = jnp.where(s < ns - 1, 1.0, 0.0).astype(f32)
    has_left = jnp.where(f > 0, 1.0, 0.0).astype(f32)
    has_right = jnp.where(f < nf - 1, 1.0, 0.0).astype(f32)
    row48 = lax.broadcasted_iota(jnp.int32, (48, 128), 0)
    inside = jnp.where(row48 < 8, has_down, jnp.where(row48 < 40, 1.0, has_up))

    def send_rows_flow(buf, k):
        for to in flow_peers:
            pltpu.make_async_remote_copy(
                src_ref=buf.at[pl.ds(f, 1)], dst_ref=buf.at[pl.ds(f, 1)],
                send_sem=s_wall.at[k], recv_sem=r_wall.at[k], device_id=to, device_id_type=MESH,
            ).start()

    def rows_flow(buf, k):
        return pltpu.make_async_remote_copy(
            src_ref=buf.at[pl.ds(0, nf - 1)], dst_ref=buf.at[pl.ds(0, nf - 1)],
            send_sem=s_wall.at[k], recv_sem=r_wall.at[k], device_id=right, device_id_type=MESH,
        )

    def send_rows_span(buf, k):
        for to in span_peers:
            pltpu.make_async_remote_copy(
                src_ref=buf.at[pl.ds(s, 1)], dst_ref=buf.at[pl.ds(s, 1)],
                send_sem=s_red.at[k], recv_sem=r_red.at[k], device_id=to, device_id_type=MESH,
            ).start()

    def rows_span(buf, k):
        return pltpu.make_async_remote_copy(
            src_ref=buf.at[pl.ds(0, ns - 1)], dst_ref=buf.at[pl.ds(0, ns - 1)],
            send_sem=s_red.at[k], recv_sem=r_red.at[k], device_id=up, device_id_type=MESH,
        )

    def halos(k):
        def copy(n, src, dst, to):
            return pltpu.make_async_remote_copy(
                src_ref=src, dst_ref=dst, send_sem=s_halo.at[k, n], recv_sem=r_halo.at[k, n],
                device_id=to, device_id_type=MESH,
            )

        return [
            copy(0, z.at[k, :, 1], hs.at[k, 0], up),
            copy(1, z.at[k, :, 0], hs.at[k, 1], down),
            copy(2, sq.at[k, 0], hq.at[k, 0], right),
            copy(3, sq.at[k, 1], hq.at[k, 1], left),
        ]

    def rows_to_bands(buf, n):
        def copy(m, src, dst, to):
            return pltpu.make_async_remote_copy(
                src_ref=buf.at[pl.ds(src, 8)], dst_ref=buf.at[pl.ds(dst, 8)],
                send_sem=s_edge.at[n, m], recv_sem=r_edge.at[n, m],
                device_id=to, device_id_type=MESH,
            )

        return [copy(0, 32, 0, up), copy(1, 8, 40, down)]

    def edges(k):
        return rows_to_bands(sinks.at[k], k)

    def first_edges():
        return rows_to_bands(u.at[0], KRYLOV) + rows_to_bands(kd, KRYLOV + 1)

    def send_halos(k):
        out = halos(k)
        out[0].start()
        out[1].start()
        for g in range(6):
            for a in range(2):
                i = 2 * g + a
                sq[k, 0, i : i + 1, :] = z[k, g, a, 7:8, :]
                sq[k, 1, i : i + 1, :] = z[k, g, a, 0:1, :]
        out[2].start()
        out[3].start()

    def remote(src, dst, send, recv, to):
        return pltpu.make_async_remote_copy(
            src_ref=src, dst_ref=dst, send_sem=send, recv_sem=recv, device_id=to, device_id_type=MESH
        )

    def pair_copies(k):
        p = PAIRS.index(k)

        def copy(n, src, dst, to):
            return remote(src, dst, s_pair.at[p, n], r_pair.at[p, n], to)

        return [
            copy(0, z.at[k, :, 1], tl.at[p, :, 1], up),
            copy(1, z.at[k, :, 0], th.at[p, :, 0], down),
            copy(4, pk.at[p, :, pl.ds(5, 1)], cb.at[p, :, pl.ds(0, 1)], corners[0]),
            copy(5, pk.at[p, :, pl.ds(4, 1)], cb.at[p, :, pl.ds(1, 1)], corners[1]),
            copy(6, pk.at[p, :, pl.ds(1, 1)], cb.at[p, :, pl.ds(4, 1)], corners[2]),
            copy(7, pk.at[p, :, pl.ds(0, 1)], cb.at[p, :, pl.ds(5, 1)], corners[3]),
            copy(12, lp.at[p, :, 1], tl.at[p, :, 0], up),
            copy(13, lp.at[p, :, 0], th.at[p, :, 1], down),
            copy(2, pk.at[p, :, pl.ds(4, 4)], sb.at[p, :, pl.ds(0, 4)], right),
            copy(3, pk.at[p, :, pl.ds(0, 4)], sb.at[p, :, pl.ds(4, 4)], left),
        ]

    def inflow_copies(k):
        p = PAIRS.index(k)
        return [
            remote(
                ir.at[p, pl.ds(0, 1)], ib.at[p, pl.ds(n, 1)],
                s_pair.at[p, 8 + n], r_pair.at[p, 8 + n], to,
            )
            for n, to in enumerate((up, down, right, left))
        ]

    def once_copies():
        def copy(n, src, dst, to):
            return remote(src, dst, s_once.at[n], r_once.at[n], to)

        out = [
            copy(0, we.at[:, 1], wl, up),
            copy(1, we.at[:, 0], wh, down),
            copy(2, pws.at[:, pl.ds(4, 4)], wsr.at[:, pl.ds(0, 4)], right),
            copy(3, pws.at[:, pl.ds(0, 4)], wsr.at[:, pl.ds(4, 4)], left),
        ]
        return out + [
            copy(4 + m, pid.at[pl.ds(4, 1)], pid.at[pl.ds(m, 1)], to)
            for m, to in enumerate((up, down, right, left))
        ]

    PACK = ((0, 0, 0), (1, 0, 1), (4, 7, 0), (5, 7, 1))

    def pack_once():
        for i in range(6):
            for m, b, a in PACK:
                pws[i, m : m + 1, :] = we[i, a, b : b + 1, :]
                pws[i, m + 2 : m + 3, :] = we[i, a, b : b + 1, :]
        pid[4:5, :] = jnp.broadcast_to(patch.astype(f32), (1, 128))

    def prepare_pairs():
        wn[0] = jnp.where(row8 == 0, has_left * wl[2], 0.0)
        wn[1] = jnp.where(row8 == 7, has_right * wl[3], 0.0)
        wn[2] = jnp.where(row8 == 0, has_left * wh[2], 0.0)
        wn[3] = jnp.where(row8 == 7, has_right * wh[3], 0.0)
        first = (row8 == 0) | (row8 == 4)
        wn[4] = jnp.where(first, has_down * wsr[0], has_up * wsr[1])
        wn[7] = jnp.where(row8 < 4, wsr[3], wsr[2])
        here = row8.astype(f32)
        wn[8] = jnp.where(here + 8.0 == pid[0:1, :], 1.0, 0.0)
        wn[9] = jnp.where(here == pid[1:2, :], 1.0, 0.0)
        side = jnp.where((row8 == 0) & (pid[2:3, :] == 7.0), 1.0, 0.0)
        side = side + jnp.where((row8 == 1) & (pid[2:3, :] == 15.0), 1.0, 0.0)
        side = side + jnp.where((row8 == 4) & (pid[3:4, :] == 0.0), 1.0, 0.0)
        wn[10] = side + jnp.where((row8 == 5) & (pid[3:4, :] == 8.0), 1.0, 0.0)

    def beside_cells(k):
        p = PAIRS.index(k)
        for g in range(6):
            el[g] = (
                tl[p, g, 0] - wl[1] * z[k, g, 0]
                - wn[0] * cb[p, g, 0:1, :] - wn[1] * cb[p, g, 4:5, :]
            )
            eh[g] = (
                th[p, g, 1] - wh[0] * z[k, g, 1]
                - wn[2] * cb[p, g, 1:2, :] - wn[3] * cb[p, g, 5:6, :]
            )
            es[g] = pltpu.roll(sb[p, g], 6, 0) - wn[4] * cb[p, g] - wn[7] * pk[p, g]

    def beside_inflow(k):
        p = PAIRS.index(k)
        el[5] = el[5] - wn[8] * ib[p, 0:1, :]
        eh[5] = eh[5] - wn[9] * ib[p, 1:2, :]
        es[5] = es[5] - wn[10] * jnp.where(row8 < 4, ib[p, 2:3, :], ib[p, 3:4, :])

    def local_part(k):
        field = [z[k, g] for g in range(6)]
        for g in range(6):
            v = field[g]
            total = bl[g, 0] * field[0]
            for h in range(1, 6):
                total = total + bl[g, h] * field[h]
            total = total - we[4] * pltpu.roll(v, 1, 2) - we[5] * pltpu.roll(v, 127, 2)
            total = total - wm[0] * pltpu.roll(v, 1, 1) - wm[1] * pltpu.roll(v, 7, 1)
            z[k + 1, g, 0] = total[0] - we[1, 0] * v[1]
            z[k + 1, g, 1] = total[1] - we[0, 1] * v[0]

    def halo_part(k, metal_here, low, high, west, east):
        inflow = coef * metal_here
        for g in range(6):
            for a in range(2):
                total = z[k + 1, g, a]
                if a == 0:
                    total = total - wm[4, 0] * low(g)
                else:
                    total = total - wm[4, 1] * high(g)
                total = total - wm[2, a] * west(g, a) - wm[3, a] * east(g, a)
                if g == 5:
                    total = total - wall_mask[a] * inflow
                z[k + 1, g, a] = total

    def own_metal(values):
        return jnp.sum(metal_mask * values, axis=0, keepdims=True)

    def wall_value(k):
        picked = wall_mask[0] * z[k, 5, 0] + wall_mask[1] * z[k, 5, 1]
        return coef * jnp.sum(picked, axis=0, keepdims=True)

    def metal_local(k):
        v = u[k]
        total = (4.0 + kd[...]) * v - pltpu.roll(v, 1, 1) - pltpu.roll(v, 127, 1)
        return (total - pltpu.roll(v, 1, 0) - pltpu.roll(v, 47, 0)) * inside

    def metal_halo(k):
        if k == 0:
            for copy in first_edges():
                copy.wait_recv()
            u[0, 0:8, :] = u[0, 0:8, :] * has_down
            u[0, 40:48, :] = u[0, 40:48, :] * has_up
        else:
            for copy in edges(k - 1):
                copy.wait_recv()
            u[k, 0:8, :] = u[k, 0:8, :] - has_down * sinks[k - 1, 0:8, :]
            u[k, 40:48, :] = u[k, 40:48, :] - has_up * sinks[k - 1, 40:48, :]

    def sink_of(k):
        rows_flow(wall.at[k], k).wait_recv()
        return jnp.dot(
            state["pick"], wall[k], precision=lax.Precision.HIGHEST, preferred_element_type=f32
        )

    def dot_row(store, i, j):
        total = store[i, 0, 0] * store[j, 0, 0] + store[i, 0, 1] * store[j, 0, 1]
        for g in range(1, 6):
            total = total + store[i, g, 0] * store[j, g, 0] + store[i, g, 1] * store[j, g, 1]
        return jnp.sum(total, axis=0, keepdims=True)

    def metal_dot_row(i, j):
        t = qm[i] * qm[j]
        t = (t[0:8] + t[8:16]) + (t[16:24] + t[24:32])
        return jnp.sum(t, axis=0, keepdims=True)

    def packed(rows, low, high):
        sums = jnp.sum(rows[low:high, :], axis=1, keepdims=True)
        return jnp.sum(jnp.where(eye[low:high], sums, 0.0), axis=0, keepdims=True)

    def unpack(total):
        sums = jnp.sum(jnp.where(eye, total, 0.0), axis=1, keepdims=True)
        scal[...] = jnp.broadcast_to(sums, (32, 128))

    loads[0].wait()
    for g in range(6):
        for a in range(2):
            i = 2 * g + a
            sq[0, 0, i : i + 1, :] = z[0, g, a, 7:8, :]
            sq[0, 1, i : i + 1, :] = z[0, g, a, 0:1, :]
    sq[:, :, 12:16, :] = jnp.zeros((KRYLOV, 2, 4, 128), f32)
    pl.semaphore_wait(barrier, ns + nf + 2)
    for copy in halos(0):
        copy.start()
    loads[1].wait()
    pairs[...] = jnp.zeros((32, 128), f32)
    mpairs[...] = jnp.zeros((32, 128), f32)
    loads[2].wait()
    wm[0] = jnp.where(row8 == 0, 0.0, we[2])
    wm[1] = jnp.where(row8 == 7, 0.0, we[3])
    wm[2] = jnp.where(row8 == 0, has_left * we[2], 0.0)
    wm[3] = jnp.where(row8 == 7, has_right * we[3], 0.0)
    wm[4, 0] = has_down * we[0, 0]
    wm[4, 1] = has_up * we[1, 1]
    loads[3].wait()
    loads[4].wait()
    for copy in first_edges():
        copy.start()

    own = []
    state = {}

    def wall_step(k):
        wall[k, pl.ds(f, 1), :] = wall_value(k)
        send_rows_flow(wall.at[k], k)

    def metal_step(k):
        if k == 1:
            rows_flow(place, KRYLOV).wait_recv()
            places = jnp.sum(place[...], axis=0, keepdims=True)
            state["pick"] = jnp.where((row32.astype(f32) == places) & (lane32 < 32), 1.0, 0.0)[:, 0:32]
        if k > 0:
            metal_halo(k - 1)
            u[k] = metal_local(k - 1)
            sinks[k - 1, 8:40, :] = sink_of(k - 1)
            for copy in edges(k - 1):
                copy.start()
            u[k, 8:40, :] = u[k, 8:40, :] - sinks[k - 1, 8:40, :]
        own.append(own_metal(u[k, 8:40, :]))

    def early_gram():
        n = 0
        for i in range(EARLY):
            for j in range(i, EARLY):
                pairs[n : n + 1, :] = dot_row(z, i, j)
                n += 1
        ra[0, pl.ds(f, 1), :] = packed(pairs, 0, 32)
        send_rows_flow(ra.at[0], KRYLOV + 1)

    def early_span():
        rows_flow(ra.at[0], KRYLOV + 1).wait_recv()
        rb[0, pl.ds(s, 1), :] = jnp.sum(ra[0], axis=0, keepdims=True)
        send_rows_span(rb.at[0], 0)

    def basis():
        rows_span(rb.at[0], 0).wait_recv()
        unpack(jnp.sum(rb[0], axis=0, keepdims=True))
        gram = {}
        n = 0
        for i in range(EARLY):
            for j in range(i, EARLY):
                gram[i, j] = scal[n : n + 1, :]
                n += 1
        r = {}
        inv = []
        trust = []
        for i in range(EARLY):
            for j in range(i, EARLY):
                t = gram[i, j]
                for h in range(i):
                    t = t - r[h, i] * r[h, j]
                if i == j:
                    floor = gram[i, i] * 1e-5
                    trust.append(t > floor)
                    t = jnp.maximum(t, floor)
                    inv.append(lax.rsqrt(t))
                r[i, j] = t * inv[i]
        ratio = [r[i, i + 1] * inv[i] for i in range(EARLY - 1)]
        coef_a = [ratio[0]]
        coef_b = [None, r[1, 1] * inv[0]]
        good = trust[1]
        for i in range(1, EARLY - 1):
            good = good & trust[i + 1]
            coef_a.append(jnp.where(good, ratio[i] - ratio[i - 1], coef_a[i - 1]))
            guess = coef_b[1] * 1.22
            coef_b.append(jnp.where(good, r[i + 1, i + 1] * inv[i], guess))
        while len(coef_a) < KRYLOV:
            coef_a.append(coef_a[-1])
        while len(coef_b) < KRYLOV + 1:
            coef_b.append(coef_b[-1])
        poly = [[inv[0]]]
        for i in range(KRYLOV):
            back = 1.0 / coef_b[i + 1]
            new = []
            for j in range(i + 2):
                t = None
                if j >= 1:
                    t = poly[i][j - 1]
                if j <= i:
                    t = -coef_a[i] * poly[i][j] if t is None else t - coef_a[i] * poly[i][j]
                if i >= 1 and j <= i - 1:
                    t = t - coef_b[i] * poly[i - 1][j]
                new.append(t * back)
            poly.append(new)
        size = [jnp.sqrt(gram[i, i]) for i in range(EARLY)]
        growth = size[-1] / size[-2]
        while len(size) < KRYLOV:
            size.append(size[-1] * growth)
        spread = []
        for i in range(KRYLOV):
            t = jnp.abs(poly[i][0]) * size[0]
            for j in range(1, i + 1):
                t = t + jnp.abs(poly[i][j]) * size[j]
            spread.append(t)
        return coef_a, coef_b, poly, spread

    def combine(low, high, first):
        poly = state["basis"][2]
        for i in range(low, KRYLOV + 1):
            terms = range(low, min(i, high) + 1)
            if not terms:
                continue
            for g in range(6):
                t = None if first else q[i, g]
                for j in terms:
                    t = poly[i][j] * z[j, g] if t is None else t + poly[i][j] * z[j, g]
                q[i, g] = t

    def metal_combine(low, high, first):
        poly = state["basis"][2]
        for i in range(low, KRYLOV + 1):
            t = None if first else qm[i]
            for j in range(low, min(i, high) + 1):
                rows = u[j, 8:40, :]
                t = poly[i][j] * rows if t is None else t + poly[i][j] * rows
            qm[i] = t

    def place_of(j, i):
        return 24 + j if i == KRYLOV else i * (i + 1) // 2 + j

    def gram_rows(low, high):
        for i in range(low, high + 1):
            for j in range(i + 1):
                n = place_of(j, i)
                pairs[n : n + 1, :] = dot_row(q, j, i)

    def metal_gram_rows(low, high):
        for i in range(low, high + 1):
            for j in range(i + 1):
                n = place_of(j, i)
                mpairs[n : n + 1, :] = metal_dot_row(j, i)

    early = [k for k, _ in PLAN if k >= EARLY - 1][0]
    when = [k for k, _ in PLAN].index(early)
    for step, (k, width) in enumerate(PLAN):
        if k > 0:
            if width == 1:
                send_halos(k)
            else:
                p = PAIRS.index(k)
                copies = pair_copies(k)
                for copy in copies[:2]:
                    copy.start()
                for g in range(6):
                    for m, b, a in PACK:
                        pk[p, g, m : m + 1, :] = z[k, g, a, b : b + 1, :]
                for copy in copies[2:6]:
                    copy.start()
        if step == when:
            early_gram()
        wall_step(k)
        if k == 0:
            send_rows_flow(place, KRYLOV)
            pack_once()
            for copy in once_copies():
                copy.start()
        local_part(k)
        if width == 2:
            for g in range(6):
                for a in range(2):
                    lp[p, g, a] = z[k + 1, g, a]
                for m, b, a in PACK:
                    pk[p, g, m + 2 : m + 3, :] = z[k + 1, g, a, b : b + 1, :]
            for copy in copies[6:]:
                copy.start()
        metal_step(k)
        if width == 2:
            p = PAIRS.index(k)
            ir[p, 0:1, :] = coef * own[k]
            for copy in inflow_copies(k):
                copy.start()
        if step == when + 1:
            early_span()
        if step == when + 3:
            state["basis"] = basis()
            combine(0, k, True)
            gram_rows(0, k)
        if width == 1:
            for copy in halos(k):
                copy.wait_recv()
            halo_part(
                k, own[k], lambda g: hs[k, 0, g], lambda g: hs[k, 1, g],
                lambda g, a: hq[k, 0, 2 * g + a : 2 * g + a + 1, :],
                lambda g, a: hq[k, 1, 2 * g + a : 2 * g + a + 1, :],
            )
        else:
            if k == PAIRS[0]:
                for copy in once_copies():
                    copy.wait_recv()
                prepare_pairs()
            for copy in pair_copies(k):
                copy.wait_recv()
            halo_part(
                k, own[k], lambda g: tl[p, g, 1], lambda g: th[p, g, 0],
                lambda g, a: sb[p, g, a : a + 1, :],
                lambda g, a: sb[p, g, 4 + a : 5 + a, :],
            )
            wall_step(k + 1)
            beside_cells(k)
            local_part(k + 1)
            if k + 1 == KRYLOV - 1:
                combine(k + 1, k + 1, False)
                gram_rows(k + 1, k + 1)
            for copy in inflow_copies(k):
                copy.wait_recv()
            beside_inflow(k)
            metal_step(k + 1)
            halo_part(
                k + 1, own[k + 1], lambda g: el[g], lambda g: eh[g],
                lambda g, a: es[g, a : a + 1, :],
                lambda g, a: es[g, 4 + a : 5 + a, :],
            )

    last = KRYLOV
    combine(last, last, False)
    gram_rows(last, last)
    ra[1, pl.ds(f, 1), :] = packed(pairs, 0, 32)
    send_rows_flow(ra.at[1], KRYLOV + 2)
    coef_a, coef_b, poly, spread = state["basis"]
    metal_combine(0, last - 1, True)
    metal_gram_rows(0, last - 1)
    metal_halo(last - 1)
    rows = metal_local(last - 1)[8:40, :] - sink_of(last - 1)
    qm[last] = qm[last] + poly[last][last] * rows
    metal_gram_rows(last, last)
    metal_done = packed(mpairs, 0, 32)
    rows_flow(ra.at[1], KRYLOV + 2).wait_recv()
    rb[1, pl.ds(s, 1), :] = jnp.sum(ra[1], axis=0, keepdims=True) + metal_done
    send_rows_span(rb.at[1], 1)
    for k, width in PLAN:
        for copy in halos(k) if width == 1 else pair_copies(k) + inflow_copies(k):
            copy.wait_send()
    for copy in once_copies():
        copy.wait_send()
    for copy in first_edges():
        copy.wait_send()
    for k in range(KRYLOV - 1):
        for copy in edges(k):
            copy.wait_send()
    for k in range(KRYLOV):
        rows_flow(wall.at[k], k).wait_send()
    rows_flow(place, KRYLOV).wait_send()
    rows_flow(ra.at[0], KRYLOV + 1).wait_send()
    rows_flow(ra.at[1], KRYLOV + 2).wait_send()
    rows_span(rb.at[0], 0).wait_send()
    rows_span(rb.at[1], 1).wait()
    unpack(jnp.sum(rb[1], axis=0, keepdims=True))
    gram = {}
    n = 0
    for i in range(KRYLOV + 1):
        for j in range(i + 1):
            m = 24 + j if i == KRYLOV else n
            gram[j, i] = scal[m : m + 1, :]
            n += 1
    r = {}
    low = None
    for i in range(KRYLOV + 1):
        scale = None
        for j in range(i, KRYLOV + 1):
            t = gram[i, j]
            for h in range(i):
                t = t - r[h, i] * r[h, j]
            if i == j:
                rel = t / gram[i, i]
                low = rel if low is None else jnp.minimum(low, rel)
                scale = lax.rsqrt(t)
            r[i, j] = t * scale
    zero = jnp.zeros((1, 128), f32)
    hess = [[zero] * KRYLOV for _ in range(KRYLOV + 1)]
    for j in range(KRYLOV):
        for i in range(j + 2):
            t = r[i, j + 1] * coef_b[j + 1]
            if i <= j:
                t = t + r[i, j] * coef_a[j]
            if i <= j - 1:
                t = t + r[i, j - 1] * coef_b[j]
            hess[i][j] = t
    y = small_solve(hess, r[0, 0] / poly[0][0], zero, KRYLOV)
    top = jnp.abs(y[0])
    total = jnp.abs(y[0]) * spread[0]
    for k in range(1, KRYLOV):
        top = jnp.maximum(top, jnp.abs(y[k]))
        total = total + jnp.abs(y[k]) * spread[k]
    fine = (low > 1e-2) & (total < 1e3 * top)
    ok_ref[...] = jnp.where(fine, 1.0, 0.0)
    for g in range(6):
        t = y[0] * q[0, g]
        for k in range(1, KRYLOV):
            t = t + y[k] * q[k, g]
        xf_ref[g] = t
    out = None
    for j in range(KRYLOV):
        c = y[j] * poly[j][j]
        for k in range(j + 1, KRYLOV):
            c = c + y[k] * poly[k][j]
        out = c * u[j, 8:40, :] if out is None else out + c * u[j, 8:40, :]
    xs_ref[...] = out


def store(a_ref, b_ref, a_out, b_out, sem):
    copies = [
        pltpu.make_async_copy(a_ref, a_out, sem.at[0]),
        pltpu.make_async_copy(b_ref, b_out, sem.at[1]),
    ]
    for copy in copies:
        copy.start()
    for copy in copies:
        copy.wait()


def shards(ns, nf, *args):
    rhs_fluid, rhs_solid = args[0], args[1]
    f32 = jnp.float32
    hbm = pl.BlockSpec(memory_space=pltpu.HBM)
    vmem = pl.BlockSpec(memory_space=pltpu.VMEM)
    smem = pl.BlockSpec(memory_space=pltpu.SMEM)
    dma = pltpu.SemaphoreType.DMA
    x_fluid, x_solid, ok, coef = pl.pallas_call(
        functools.partial(kernel, ns, nf),
        name="gmres",
        out_shape=(
            jax.ShapeDtypeStruct(rhs_fluid.shape, f32),
            jax.ShapeDtypeStruct(rhs_solid.shape, f32),
            jax.ShapeDtypeStruct((1, 128), f32),
            jax.ShapeDtypeStruct(args[-1].shape, f32),
        ),
        in_specs=[hbm] * 5 + [smem] * 2 + [hbm],
        out_specs=(vmem,) * 4,
        scratch_shapes=[
            pltpu.VMEM((KRYLOV + 1, 6, 2, 8, 128), f32),
            pltpu.VMEM((KRYLOV, 48, 128), f32),
            pltpu.VMEM((KRYLOV + 1, 6, 2, 8, 128), f32),
            pltpu.VMEM((KRYLOV + 1, 32, 128), f32),
            pltpu.VMEM((6, 6, 2, 8, 128), f32),
            pltpu.VMEM((6, 2, 8, 128), f32),
            pltpu.VMEM((5, 2, 8, 128), f32),
            pltpu.VMEM((48, 128), f32),
            pltpu.VMEM((KRYLOV, 2, 6, 8, 128), f32),
            pltpu.VMEM((KRYLOV, 2, 16, 128), f32),
            pltpu.VMEM((KRYLOV, 2, 16, 128), f32),
            pltpu.VMEM((KRYLOV - 1, 48, 128), f32),
            pltpu.VMEM((KRYLOV, 32, 128), f32),
            pltpu.VMEM((32, 128), f32),
            pltpu.VMEM((32, 128), f32),
            pltpu.VMEM((32, 128), f32),
            pltpu.VMEM((32, 128), f32),
            pltpu.VMEM((2, 32, 128), f32),
            pltpu.VMEM((2, 16, 128), f32),
            pltpu.VMEM((len(PAIRS), 6, 2, 8, 128), f32),
            pltpu.VMEM((len(PAIRS), 6, 2, 8, 128), f32),
            pltpu.VMEM((len(PAIRS), 6, 2, 8, 128), f32),
            pltpu.VMEM((len(PAIRS), 6, 8, 128), f32),
            pltpu.VMEM((len(PAIRS), 6, 8, 128), f32),
            pltpu.VMEM((len(PAIRS), 6, 8, 128), f32),
            pltpu.VMEM((len(PAIRS), 8, 128), f32),
            pltpu.VMEM((len(PAIRS), 8, 128), f32),
            pltpu.VMEM((6, 8, 128), f32),
            pltpu.VMEM((6, 8, 128), f32),
            pltpu.VMEM((6, 8, 128), f32),
            pltpu.VMEM((6, 8, 128), f32),
            pltpu.VMEM((11, 8, 128), f32),
            pltpu.VMEM((8, 128), f32),
            pltpu.VMEM((6, 8, 128), f32),
            pltpu.VMEM((6, 8, 128), f32),
            pltpu.VMEM((6, 8, 128), f32),
            dma((6,)),
            dma((KRYLOV, 4)), dma((KRYLOV, 4)),
            dma((KRYLOV + 2, 2)), dma((KRYLOV + 2, 2)),
            dma((KRYLOV + 3,)), dma((KRYLOV + 3,)),
            dma((2,)), dma((2,)),
            dma((len(PAIRS), 14)), dma((len(PAIRS), 14)),
            dma((8,)), dma((8,)),
        ],
        compiler_params=pltpu.CompilerParams(
            collective_id=0, has_side_effects=True, vmem_limit_bytes=8 * 1024 * 1024
        ),
    )(*args)
    def place_out(*a):
        return pl.pallas_call(
            store,
            name="place_out",
            out_shape=(
                jax.ShapeDtypeStruct(rhs_fluid.shape, f32),
                jax.ShapeDtypeStruct(rhs_solid.shape, f32),
            ),
            in_specs=[vmem, vmem],
            out_specs=(hbm, hbm),
            scratch_shapes=[dma((2,))],
        )(x_fluid, x_solid)

    return lax.cond(ok[0, 0] > 0.5, place_out, lambda *a: arnoldi(*a), *args[:-1], coef)


def solution(mesh):
    in_specs = (
        P(None, "span", "flow", None),
        P("span", None),
        P(None, None, "span", "flow", None),
        P(None, "span", "flow", None),
        P("span", None),
        P("span", "flow"),
        P("span", "flow"),
        P("span", "flow", None),
    )
    out_specs = (P(None, "span", "flow", None), P("span", None))
    return jax.shard_map(
        functools.partial(shards, mesh.shape["span"], mesh.shape["flow"]),
        mesh=mesh, in_specs=in_specs, out_specs=out_specs, check_vma=False,
    )
```

```python
import functools

import jax
import jax.numpy as jnp
from jax import lax
from jax.experimental import pallas as pl
from jax.experimental.pallas import tpu as pltpu
from jax.sharding import PartitionSpec as P

KRYLOV = 6
MESH = pl.DeviceIdType.MESH
EARLY = 2
PLAN = ((0, 2), (2, 1), (3, 1), (4, 2))
PAIRS = tuple(k for k, width in PLAN if width == 2)


def extended(shard, sides, width):
    for axis, dim in sides:
        count, length = (lax.axis_size(axis), shard.shape[dim])
        up = [(i, (i + 1) % count) for i in range(count - 1)]
        down = [(j, i) for i, j in up]
        last = lax.slice_in_dim(shard, length - width, length, axis=dim)
        first = lax.slice_in_dim(shard, 0, width, axis=dim)
        before = lax.ppermute(last, axis, up)
        after = lax.ppermute(first, axis, down)
        shard = jnp.concatenate([before, shard, after], axis=dim)
    return shard


def back_substitute(upper, rhs_g, steps):
    coeffs = [None] * steps
    for j in range(steps - 1, -1, -1):
        total = rhs_g[j]
        for k in range(j + 1, steps):
            total = total - upper[k][j] * coeffs[k]
        coeffs[j] = total / upper[j][j]
    return coeffs


def least_squares(hess, beta, zero, steps):
    cos_list, sin_list, upper = ([], [], [])
    rhs_g = [beta] + [zero for _ in range(steps)]
    for j in range(steps):
        column = [hess[i][j] for i in range(j + 2)]
        for i in range(j):
            top = cos_list[i] * column[i] + sin_list[i] * column[i + 1]
            column[i + 1] = -sin_list[i] * column[i] + cos_list[i] * column[i + 1]
            column[i] = top
        radius = jnp.sqrt(column[j] * column[j] + column[j + 1] * column[j + 1])
        cos_now = column[j] / radius
        sin_now = column[j + 1] / radius
        column[j] = radius
        rhs_g[j + 1] = -sin_now * rhs_g[j]
        rhs_g[j] = cos_now * rhs_g[j]
        cos_list.append(cos_now)
        sin_list.append(sin_now)
        upper.append(column[: j + 1])
    return back_substitute(upper, rhs_g, steps)


def arnoldi(rhs_fluid, rhs_solid, blocks, weights, kdiag, wall_fluid, wall_solid, wall_coef):
    rows_a = rhs_fluid.shape[1]
    rows_b = rhs_fluid.shape[2]
    width = rhs_fluid.shape[3]
    cells = rows_a * rows_b
    band_rows = rhs_solid.shape[0]
    patch_rows = wall_fluid[0]
    patch_metal = wall_solid[0]
    coef = wall_coef[0]
    fluid_pick = (jnp.arange(cells, dtype=jnp.int32)[:, None] == patch_rows[None, :]).astype(
        jnp.float32
    )
    metal_pick = (jnp.arange(band_rows, dtype=jnp.int32)[:, None] == patch_metal[None, :]).astype(
        jnp.float32
    )
    first_flow = (lax.axis_index("flow") == 0).astype(jnp.float32)
    highest = lax.Precision.HIGHEST

    def local_inner(left, right):
        return jnp.sum(left[0] * right[0]) + first_flow * jnp.sum(left[1] * right[1])

    beta = jnp.sqrt(
        lax.psum(local_inner((rhs_fluid, rhs_solid), (rhs_fluid, rhs_solid)), ("span", "flow"))
    )
    basis = [(rhs_fluid / beta, rhs_solid / beta)]
    hess = [[jnp.float32(0.0) for _ in range(KRYLOV)] for _ in range(KRYLOV + 1)]
    for j in range(KRYLOV):
        field = basis[j][0]
        metal_u = basis[j][1]
        padded = extended(field, (("span", 1), ("flow", 2)), 1)
        local = jnp.einsum("fgabc,gabc->fabc", blocks, field, precision=highest)
        beside = weights[0][None] * padded[:, :-2, 1:-1] + weights[1][None] * padded[:, 2:, 1:-1]
        beside = (
            beside
            + weights[2][None] * padded[:, 1:-1, :-2]
            + weights[3][None] * padded[:, 1:-1, 2:]
        )
        beside = (
            beside
            + weights[4][None] * jnp.roll(field, 1, axis=3)
            + weights[5][None] * jnp.roll(field, -1, axis=3)
        )
        metal_at = jnp.dot(metal_pick.T, metal_u, precision=highest)
        inflow = jnp.dot(fluid_pick, coef * metal_at, precision=highest).reshape(
            rows_a, rows_b, width
        )
        image_f = (local - beside).at[5].add(-inflow)
        wall_vals = coef * jnp.dot(fluid_pick.T, field[5].reshape(cells, width), precision=highest)
        sink = lax.psum(jnp.dot(metal_pick, wall_vals, precision=highest), "flow")
        upad = extended(metal_u, (("span", 0),), 1)
        beside_all = (
            upad[:-2] + upad[2:] + jnp.roll(metal_u, 1, axis=1) + jnp.roll(metal_u, -1, axis=1)
        )
        image_s = (4.0 + kdiag) * metal_u - beside_all - sink
        terms = jnp.stack([local_inner(basis[i], (image_f, image_s)) for i in range(j + 1)])
        values = lax.psum(terms, ("span", "flow"))
        for i in range(j + 1):
            image_f = image_f - values[i] * basis[i][0]
            image_s = image_s - values[i] * basis[i][1]
        rest = jnp.sqrt(
            lax.psum(local_inner((image_f, image_s), (image_f, image_s)), ("span", "flow"))
        )
        for i in range(j + 1):
            hess[i][j] = values[i]
        hess[j + 1][j] = rest
        basis.append((image_f / rest, image_s / rest))
    coeffs = least_squares(hess, beta, jnp.float32(0.0), KRYLOV)
    x_fluid = jnp.zeros_like(rhs_fluid)
    x_solid = jnp.zeros_like(rhs_solid)
    for j in range(KRYLOV):
        x_fluid = x_fluid + coeffs[j] * basis[j][0]
        x_solid = x_solid + coeffs[j] * basis[j][1]
    return (x_fluid, x_solid)


def small_solve(hess, beta, zero, steps):
    cos_list, sin_list, upper, inverse = ([], [], [], [])
    rhs_g = [beta] + [zero for _ in range(steps)]
    for j in range(steps):
        column = [hess[i][j] for i in range(j + 2)]
        for i in range(j):
            top = cos_list[i] * column[i] + sin_list[i] * column[i + 1]
            column[i + 1] = -sin_list[i] * column[i] + cos_list[i] * column[i + 1]
            column[i] = top
        scale = lax.rsqrt(column[j] * column[j] + column[j + 1] * column[j + 1])
        cos_now = column[j] * scale
        sin_now = column[j + 1] * scale
        rhs_g[j + 1] = -sin_now * rhs_g[j]
        rhs_g[j] = cos_now * rhs_g[j]
        cos_list.append(cos_now)
        sin_list.append(sin_now)
        upper.append(column[:j])
        inverse.append(scale)
    coeffs = [None] * steps
    for j in range(steps - 1, -1, -1):
        total = rhs_g[j]
        for k in range(j + 1, steps):
            total = total - upper[k][j] * coeffs[k]
        coeffs[j] = total * inverse[j]
    return coeffs


def kernel(
    ns, nf,
    rf_hbm, rs_hbm, bl_hbm, we_hbm, kd_hbm, wf_ref, ws_ref, wc_hbm,
    xf_ref, xs_ref, ok_ref, wc,
    z, u, q, qm, bl, we, wm, kd, hs, hq, sq, sinks, wall, place, pairs, mpairs, scal, ra, rb,
    tl, th, lp, sb, pk, cb, ir, ib, wl, wh, wsr, pws, wn, pid, el, eh, es,
    in_sem, s_halo, r_halo, s_edge, r_edge, s_wall, r_wall, s_red, r_red, s_pair, r_pair, s_once, r_once,
):
    f32 = jnp.float32
    s = lax.axis_index("span")
    f = lax.axis_index("flow")
    up = (lax.rem(s + 1, ns), f)
    down = (lax.rem(s + ns - 1, ns), f)
    right = (s, lax.rem(f + 1, nf))
    left = (s, lax.rem(f + nf - 1, nf))
    corners = ((up[0], right[1]), (down[0], right[1]), (up[0], left[1]), (down[0], left[1]))

    loads = [
        pltpu.make_async_copy(rf_hbm, z.at[0], in_sem.at[0]),
        pltpu.make_async_copy(rs_hbm, u.at[0, pl.ds(8, 32)], in_sem.at[1]),
        pltpu.make_async_copy(we_hbm, we, in_sem.at[2]),
        pltpu.make_async_copy(bl_hbm, bl, in_sem.at[3]),
        pltpu.make_async_copy(kd_hbm, kd.at[pl.ds(8, 32)], in_sem.at[4]),
        pltpu.make_async_copy(wc_hbm, wc, in_sem.at[5]),
    ]
    for load in loads:
        load.start()

    cb[...] = jnp.zeros((len(PAIRS), 6, 8, 128), f32)

    barrier = pltpu.get_barrier_semaphore()

    def far_first(n):
        return sorted(range(1, n), key=lambda d: -min(d, n - d))

    flow_peers = [(s, lax.rem(f + d, nf)) for d in far_first(nf)]
    span_peers = [(lax.rem(s + d, ns), f) for d in far_first(ns)]
    for to in span_peers + flow_peers:
        pl.semaphore_signal(barrier, inc=1, device_id=to, device_id_type=MESH)
    for to in corners:
        pl.semaphore_signal(barrier, inc=1, device_id=to, device_id_type=MESH)
    row8 = lax.broadcasted_iota(jnp.int32, (8, 128), 0)
    row16 = lax.broadcasted_iota(jnp.int32, (2, 8, 128), 0) * 8 + lax.broadcasted_iota(
        jnp.int32, (2, 8, 128), 1
    )
    row32 = lax.broadcasted_iota(jnp.int32, (32, 128), 0)
    lane32 = lax.broadcasted_iota(jnp.int32, (32, 128), 1)
    lane1 = lax.broadcasted_iota(jnp.int32, (1, 128), 1)
    eye = row32 == lane32
    loads[5].wait()
    patch = wf_ref[0, 0]
    metal_row = ws_ref[0, 0]
    coef = wc[0]
    wall_mask = jnp.where(row16 == patch, 1.0, 0.0).astype(f32)
    metal_mask = jnp.where(row32 == metal_row, 1.0, 0.0).astype(f32)
    place[pl.ds(f, 1), :] = jnp.where(lane1 == f, metal_row.astype(f32), 0.0)
    has_down = jnp.where(s > 0, 1.0, 0.0).astype(f32)
    has_up = jnp.where(s < ns - 1, 1.0, 0.0).astype(f32)
    has_left = jnp.where(f > 0, 1.0, 0.0).astype(f32)
    has_right = jnp.where(f < nf - 1, 1.0, 0.0).astype(f32)
    row48 = lax.broadcasted_iota(jnp.int32, (48, 128), 0)
    inside = jnp.where(row48 < 8, has_down, jnp.where(row48 < 40, 1.0, has_up))

    def send_rows_flow(buf, k):
        for to in flow_peers:
            pltpu.make_async_remote_copy(
                src_ref=buf.at[pl.ds(f, 1)], dst_ref=buf.at[pl.ds(f, 1)],
                send_sem=s_wall.at[k], recv_sem=r_wall.at[k], device_id=to, device_id_type=MESH,
            ).start()

    def rows_flow(buf, k):
        return pltpu.make_async_remote_copy(
            src_ref=buf.at[pl.ds(0, nf - 1)], dst_ref=buf.at[pl.ds(0, nf - 1)],
            send_sem=s_wall.at[k], recv_sem=r_wall.at[k], device_id=right, device_id_type=MESH,
        )

    def send_rows_span(buf, k):
        for to in span_peers:
            pltpu.make_async_remote_copy(
                src_ref=buf.at[pl.ds(s, 1)], dst_ref=buf.at[pl.ds(s, 1)],
                send_sem=s_red.at[k], recv_sem=r_red.at[k], device_id=to, device_id_type=MESH,
            ).start()

    def rows_span(buf, k):
        return pltpu.make_async_remote_copy(
            src_ref=buf.at[pl.ds(0, ns - 1)], dst_ref=buf.at[pl.ds(0, ns - 1)],
            send_sem=s_red.at[k], recv_sem=r_red.at[k], device_id=up, device_id_type=MESH,
        )

    def halos(k):
        def copy(n, src, dst, to):
            return pltpu.make_async_remote_copy(
                src_ref=src, dst_ref=dst, send_sem=s_halo.at[k, n], recv_sem=r_halo.at[k, n],
                device_id=to, device_id_type=MESH,
            )

        return [
            copy(0, z.at[k, :, 1], hs.at[k, 0], up),
            copy(1, z.at[k, :, 0], hs.at[k, 1], down),
            copy(2, sq.at[k, 0], hq.at[k, 0], right),
            copy(3, sq.at[k, 1], hq.at[k, 1], left),
        ]

    def rows_to_bands(buf, n):
        def copy(m, src, dst, to):
            return pltpu.make_async_remote_copy(
                src_ref=buf.at[pl.ds(src, 8)], dst_ref=buf.at[pl.ds(dst, 8)],
                send_sem=s_edge.at[n, m], recv_sem=r_edge.at[n, m],
                device_id=to, device_id_type=MESH,
            )

        return [copy(0, 32, 0, up), copy(1, 8, 40, down)]

    def edges(k):
        return rows_to_bands(sinks.at[k], k)

    def first_edges():
        return rows_to_bands(u.at[0], KRYLOV) + rows_to_bands(kd, KRYLOV + 1)

    def send_halos(k):
        out = halos(k)
        out[0].start()
        out[1].start()
        for g in range(6):
            for a in range(2):
                i = 2 * g + a
                sq[k, 0, i : i + 1, :] = z[k, g, a, 7:8, :]
                sq[k, 1, i : i + 1, :] = z[k, g, a, 0:1, :]
        out[2].start()
        out[3].start()

    def remote(src, dst, send, recv, to):
        return pltpu.make_async_remote_copy(
            src_ref=src, dst_ref=dst, send_sem=send, recv_sem=recv, device_id=to, device_id_type=MESH
        )

    def pair_copies(k):
        p = PAIRS.index(k)

        def copy(n, src, dst, to):
            return remote(src, dst, s_pair.at[p, n], r_pair.at[p, n], to)

        return [
            copy(0, z.at[k, :, 1], tl.at[p, :, 1], up),
            copy(1, z.at[k, :, 0], th.at[p, :, 0], down),
            copy(4, pk.at[p, :, pl.ds(5, 1)], cb.at[p, :, pl.ds(0, 1)], corners[0]),
            copy(5, pk.at[p, :, pl.ds(4, 1)], cb.at[p, :, pl.ds(1, 1)], corners[1]),
            copy(6, pk.at[p, :, pl.ds(1, 1)], cb.at[p, :, pl.ds(4, 1)], corners[2]),
            copy(7, pk.at[p, :, pl.ds(0, 1)], cb.at[p, :, pl.ds(5, 1)], corners[3]),
            copy(12, lp.at[p, :, 1], tl.at[p, :, 0], up),
            copy(13, lp.at[p, :, 0], th.at[p, :, 1], down),
            copy(2, pk.at[p, :, pl.ds(4, 4)], sb.at[p, :, pl.ds(0, 4)], right),
            copy(3, pk.at[p, :, pl.ds(0, 4)], sb.at[p, :, pl.ds(4, 4)], left),
        ]

    def inflow_copies(k):
        p = PAIRS.index(k)
        return [
            remote(
                ir.at[p, pl.ds(0, 1)], ib.at[p, pl.ds(n, 1)],
                s_pair.at[p, 8 + n], r_pair.at[p, 8 + n], to,
            )
            for n, to in enumerate((up, down, right, left))
        ]

    def once_copies():
        def copy(n, src, dst, to):
            return remote(src, dst, s_once.at[n], r_once.at[n], to)

        out = [
            copy(0, we.at[:, 1], wl, up),
            copy(1, we.at[:, 0], wh, down),
            copy(2, pws.at[:, pl.ds(4, 4)], wsr.at[:, pl.ds(0, 4)], right),
            copy(3, pws.at[:, pl.ds(0, 4)], wsr.at[:, pl.ds(4, 4)], left),
        ]
        return out + [
            copy(4 + m, pid.at[pl.ds(4, 1)], pid.at[pl.ds(m, 1)], to)
            for m, to in enumerate((up, down, right, left))
        ]

    PACK = ((0, 0, 0), (1, 0, 1), (4, 7, 0), (5, 7, 1))

    def pack_once():
        for i in range(6):
            for m, b, a in PACK:
                pws[i, m : m + 1, :] = we[i, a, b : b + 1, :]
                pws[i, m + 2 : m + 3, :] = we[i, a, b : b + 1, :]
        pid[4:5, :] = jnp.broadcast_to(patch.astype(f32), (1, 128))

    def prepare_pairs():
        wn[0] = jnp.where(row8 == 0, has_left * wl[2], 0.0)
        wn[1] = jnp.where(row8 == 7, has_right * wl[3], 0.0)
        wn[2] = jnp.where(row8 == 0, has_left * wh[2], 0.0)
        wn[3] = jnp.where(row8 == 7, has_right * wh[3], 0.0)
        first = (row8 == 0) | (row8 == 4)
        wn[4] = jnp.where(first, has_down * wsr[0], has_up * wsr[1])
        wn[7] = jnp.where(row8 < 4, wsr[3], wsr[2])
        here = row8.astype(f32)
        wn[8] = jnp.where(here + 8.0 == pid[0:1, :], 1.0, 0.0)
        wn[9] = jnp.where(here == pid[1:2, :], 1.0, 0.0)
        side = jnp.where((row8 == 0) & (pid[2:3, :] == 7.0), 1.0, 0.0)
        side = side + jnp.where((row8 == 1) & (pid[2:3, :] == 15.0), 1.0, 0.0)
        side = side + jnp.where((row8 == 4) & (pid[3:4, :] == 0.0), 1.0, 0.0)
        wn[10] = side + jnp.where((row8 == 5) & (pid[3:4, :] == 8.0), 1.0, 0.0)

    def beside_cells(k):
        p = PAIRS.index(k)
        for g in range(6):
            el[g] = (
                tl[p, g, 0] - wl[1] * z[k, g, 0]
                - wn[0] * cb[p, g, 0:1, :] - wn[1] * cb[p, g, 4:5, :]
            )
            eh[g] = (
                th[p, g, 1] - wh[0] * z[k, g, 1]
                - wn[2] * cb[p, g, 1:2, :] - wn[3] * cb[p, g, 5:6, :]
            )
            es[g] = pltpu.roll(sb[p, g], 6, 0) - wn[4] * cb[p, g] - wn[7] * pk[p, g]

    def beside_inflow(k):
        p = PAIRS.index(k)
        el[5] = el[5] - wn[8] * ib[p, 0:1, :]
        eh[5] = eh[5] - wn[9] * ib[p, 1:2, :]
        es[5] = es[5] - wn[10] * jnp.where(row8 < 4, ib[p, 2:3, :], ib[p, 3:4, :])

    def local_part(k):
        field = [z[k, g] for g in range(6)]
        for g in range(6):
            v = field[g]
            total = bl[g, 0] * field[0]
            for h in range(1, 6):
                total = total + bl[g, h] * field[h]
            total = total - we[4] * pltpu.roll(v, 1, 2) - we[5] * pltpu.roll(v, 127, 2)
            total = total - wm[0] * pltpu.roll(v, 1, 1) - wm[1] * pltpu.roll(v, 7, 1)
            z[k + 1, g, 0] = total[0] - we[1, 0] * v[1]
            z[k + 1, g, 1] = total[1] - we[0, 1] * v[0]

    def halo_part(k, metal_here, low, high, west, east):
        inflow = coef * metal_here
        for g in range(6):
            for a in range(2):
                total = z[k + 1, g, a]
                if a == 0:
                    total = total - wm[4, 0] * low(g)
                else:
                    total = total - wm[4, 1] * high(g)
                total = total - wm[2, a] * west(g, a) - wm[3, a] * east(g, a)
                if g == 5:
                    total = total - wall_mask[a] * inflow
                z[k + 1, g, a] = total

    def own_metal(values):
        return jnp.sum(metal_mask * values, axis=0, keepdims=True)

    def wall_value(k):
        picked = wall_mask[0] * z[k, 5, 0] + wall_mask[1] * z[k, 5, 1]
        return coef * jnp.sum(picked, axis=0, keepdims=True)

    def metal_local(k):
        v = u[k]
        total = (4.0 + kd[...]) * v - pltpu.roll(v, 1, 1) - pltpu.roll(v, 127, 1)
        return (total - pltpu.roll(v, 1, 0) - pltpu.roll(v, 47, 0)) * inside

    def metal_halo(k):
        if k == 0:
            for copy in first_edges():
                copy.wait_recv()
            u[0, 0:8, :] = u[0, 0:8, :] * has_down
            u[0, 40:48, :] = u[0, 40:48, :] * has_up
        else:
            for copy in edges(k - 1):
                copy.wait_recv()
            u[k, 0:8, :] = u[k, 0:8, :] - has_down * sinks[k - 1, 0:8, :]
            u[k, 40:48, :] = u[k, 40:48, :] - has_up * sinks[k - 1, 40:48, :]

    def sink_of(k):
        rows_flow(wall.at[k], k).wait_recv()
        return jnp.dot(
            state["pick"], wall[k], precision=lax.Precision.HIGHEST, preferred_element_type=f32
        )

    def dot_row(store, i, j):
        total = store[i, 0, 0] * store[j, 0, 0] + store[i, 0, 1] * store[j, 0, 1]
        for g in range(1, 6):
            total = total + store[i, g, 0] * store[j, g, 0] + store[i, g, 1] * store[j, g, 1]
        return jnp.sum(total, axis=0, keepdims=True)

    def metal_dot_row(i, j):
        t = qm[i] * qm[j]
        t = (t[0:8] + t[8:16]) + (t[16:24] + t[24:32])
        return jnp.sum(t, axis=0, keepdims=True)

    def packed(rows, low, high):
        sums = jnp.sum(rows[low:high, :], axis=1, keepdims=True)
        return jnp.sum(jnp.where(eye[low:high], sums, 0.0), axis=0, keepdims=True)

    def unpack(total):
        sums = jnp.sum(jnp.where(eye, total, 0.0), axis=1, keepdims=True)
        scal[...] = jnp.broadcast_to(sums, (32, 128))

    loads[0].wait()
    for g in range(6):
        for a in range(2):
            i = 2 * g + a
            sq[0, 0, i : i + 1, :] = z[0, g, a, 7:8, :]
            sq[0, 1, i : i + 1, :] = z[0, g, a, 0:1, :]
    sq[:, :, 12:16, :] = jnp.zeros((KRYLOV, 2, 4, 128), f32)
    pl.semaphore_wait(barrier, ns + nf + 2)
    if PLAN[0][1] == 1:
        for copy in halos(0):
            copy.start()
    loads[1].wait()
    pairs[...] = jnp.zeros((32, 128), f32)
    mpairs[...] = jnp.zeros((32, 128), f32)
    loads[2].wait()
    wm[0] = jnp.where(row8 == 0, 0.0, we[2])
    wm[1] = jnp.where(row8 == 7, 0.0, we[3])
    wm[2] = jnp.where(row8 == 0, has_left * we[2], 0.0)
    wm[3] = jnp.where(row8 == 7, has_right * we[3], 0.0)
    wm[4, 0] = has_down * we[0, 0]
    wm[4, 1] = has_up * we[1, 1]
    loads[3].wait()
    loads[4].wait()
    for copy in first_edges():
        copy.start()

    own = []
    state = {}

    def wall_step(k):
        wall[k, pl.ds(f, 1), :] = wall_value(k)
        send_rows_flow(wall.at[k], k)

    def metal_step(k):
        if k == 1:
            rows_flow(place, KRYLOV).wait_recv()
            places = jnp.sum(place[...], axis=0, keepdims=True)
            state["pick"] = jnp.where((row32.astype(f32) == places) & (lane32 < 32), 1.0, 0.0)[:, 0:32]
        if k > 0:
            metal_halo(k - 1)
            u[k] = metal_local(k - 1)
            sinks[k - 1, 8:40, :] = sink_of(k - 1)
            for copy in edges(k - 1):
                copy.start()
            u[k, 8:40, :] = u[k, 8:40, :] - sinks[k - 1, 8:40, :]
        own.append(own_metal(u[k, 8:40, :]))

    def early_gram():
        n = 0
        for i in range(EARLY):
            for j in range(i, EARLY):
                pairs[n : n + 1, :] = dot_row(z, i, j)
                n += 1
        ra[0, pl.ds(f, 1), :] = packed(pairs, 0, 32)
        send_rows_flow(ra.at[0], KRYLOV + 1)

    def early_span():
        rows_flow(ra.at[0], KRYLOV + 1).wait_recv()
        rb[0, pl.ds(s, 1), :] = jnp.sum(ra[0], axis=0, keepdims=True)
        send_rows_span(rb.at[0], 0)

    def basis():
        rows_span(rb.at[0], 0).wait_recv()
        unpack(jnp.sum(rb[0], axis=0, keepdims=True))
        gram = {}
        n = 0
        for i in range(EARLY):
            for j in range(i, EARLY):
                gram[i, j] = scal[n : n + 1, :]
                n += 1
        r = {}
        inv = []
        trust = []
        for i in range(EARLY):
            for j in range(i, EARLY):
                t = gram[i, j]
                for h in range(i):
                    t = t - r[h, i] * r[h, j]
                if i == j:
                    floor = gram[i, i] * 1e-5
                    trust.append(t > floor)
                    t = jnp.maximum(t, floor)
                    inv.append(lax.rsqrt(t))
                r[i, j] = t * inv[i]
        ratio = [r[i, i + 1] * inv[i] for i in range(EARLY - 1)]
        coef_a = [ratio[0]]
        coef_b = [None, r[1, 1] * inv[0]]
        good = trust[1]
        for i in range(1, EARLY - 1):
            good = good & trust[i + 1]
            coef_a.append(jnp.where(good, ratio[i] - ratio[i - 1], coef_a[i - 1]))
            guess = coef_b[1] * 1.22
            coef_b.append(jnp.where(good, r[i + 1, i + 1] * inv[i], guess))
        while len(coef_a) < KRYLOV:
            coef_a.append(coef_a[-1])
        while len(coef_b) < KRYLOV + 1:
            coef_b.append(coef_b[-1])
        poly = [[inv[0]]]
        for i in range(KRYLOV):
            back = 1.0 / coef_b[i + 1]
            new = []
            for j in range(i + 2):
                t = None
                if j >= 1:
                    t = poly[i][j - 1]
                if j <= i:
                    t = -coef_a[i] * poly[i][j] if t is None else t - coef_a[i] * poly[i][j]
                if i >= 1 and j <= i - 1:
                    t = t - coef_b[i] * poly[i - 1][j]
                new.append(t * back)
            poly.append(new)
        size = [jnp.sqrt(gram[i, i]) for i in range(EARLY)]
        growth = size[-1] / size[-2]
        while len(size) < KRYLOV:
            size.append(size[-1] * growth)
        spread = []
        for i in range(KRYLOV):
            t = jnp.abs(poly[i][0]) * size[0]
            for j in range(1, i + 1):
                t = t + jnp.abs(poly[i][j]) * size[j]
            spread.append(t)
        return coef_a, coef_b, poly, spread

    def combine(low, high, first):
        poly = state["basis"][2]
        for i in range(low, KRYLOV + 1):
            terms = range(low, min(i, high) + 1)
            if not terms:
                continue
            for g in range(6):
                t = None if first else q[i, g]
                for j in terms:
                    t = poly[i][j] * z[j, g] if t is None else t + poly[i][j] * z[j, g]
                q[i, g] = t

    def metal_combine(low, high, first):
        poly = state["basis"][2]
        for i in range(low, KRYLOV + 1):
            t = None if first else qm[i]
            for j in range(low, min(i, high) + 1):
                rows = u[j, 8:40, :]
                t = poly[i][j] * rows if t is None else t + poly[i][j] * rows
            qm[i] = t

    def place_of(j, i):
        return 24 + j if i == KRYLOV else i * (i + 1) // 2 + j

    def gram_rows(low, high):
        for i in range(low, high + 1):
            for j in range(i + 1):
                n = place_of(j, i)
                pairs[n : n + 1, :] = dot_row(q, j, i)

    def metal_gram_rows(low, high):
        for i in range(low, high + 1):
            for j in range(i + 1):
                n = place_of(j, i)
                mpairs[n : n + 1, :] = metal_dot_row(j, i)

    early = [k for k, _ in PLAN if k >= EARLY - 1][0]
    when = [k for k, _ in PLAN].index(early)
    for step, (k, width) in enumerate(PLAN):
        if width == 2:
            p = PAIRS.index(k)
            copies = pair_copies(k)
            for copy in copies[:2]:
                copy.start()
            for g in range(6):
                for m, b, a in PACK:
                    pk[p, g, m : m + 1, :] = z[k, g, a, b : b + 1, :]
            for copy in copies[2:6]:
                copy.start()
        elif k > 0:
            send_halos(k)
        if step == when:
            early_gram()
        wall_step(k)
        if k == 0:
            send_rows_flow(place, KRYLOV)
            pack_once()
            for copy in once_copies():
                copy.start()
        local_part(k)
        if width == 2:
            for g in range(6):
                for a in range(2):
                    lp[p, g, a] = z[k + 1, g, a]
                for m, b, a in PACK:
                    pk[p, g, m + 2 : m + 3, :] = z[k + 1, g, a, b : b + 1, :]
            for copy in copies[6:]:
                copy.start()
        metal_step(k)
        if width == 2:
            p = PAIRS.index(k)
            ir[p, 0:1, :] = coef * own[k]
            for copy in inflow_copies(k):
                copy.start()
        if step == when + 1:
            early_span()
        if step == len(PLAN) - 1:
            state["basis"] = basis()
            combine(0, k, True)
            gram_rows(0, k)
        if width == 1:
            for copy in halos(k):
                copy.wait_recv()
            halo_part(
                k, own[k], lambda g: hs[k, 0, g], lambda g: hs[k, 1, g],
                lambda g, a: hq[k, 0, 2 * g + a : 2 * g + a + 1, :],
                lambda g, a: hq[k, 1, 2 * g + a : 2 * g + a + 1, :],
            )
        else:
            if k == PAIRS[0]:
                for copy in once_copies():
                    copy.wait_recv()
                prepare_pairs()
            for copy in pair_copies(k):
                copy.wait_recv()
            halo_part(
                k, own[k], lambda g: tl[p, g, 1], lambda g: th[p, g, 0],
                lambda g, a: sb[p, g, a : a + 1, :],
                lambda g, a: sb[p, g, 4 + a : 5 + a, :],
            )
            wall_step(k + 1)
            beside_cells(k)
            local_part(k + 1)
            if k + 1 == KRYLOV - 1:
                combine(k + 1, k + 1, False)
                gram_rows(k + 1, k + 1)
            for copy in inflow_copies(k):
                copy.wait_recv()
            beside_inflow(k)
            metal_step(k + 1)
            halo_part(
                k + 1, own[k + 1], lambda g: el[g], lambda g: eh[g],
                lambda g, a: es[g, a : a + 1, :],
                lambda g, a: es[g, 4 + a : 5 + a, :],
            )

    last = KRYLOV
    combine(last, last, False)
    gram_rows(last, last)
    ra[1, pl.ds(f, 1), :] = packed(pairs, 0, 32)
    send_rows_flow(ra.at[1], KRYLOV + 2)
    coef_a, coef_b, poly, spread = state["basis"]
    metal_combine(0, last - 1, True)
    metal_gram_rows(0, last - 1)
    metal_halo(last - 1)
    rows = metal_local(last - 1)[8:40, :] - sink_of(last - 1)
    qm[last] = qm[last] + poly[last][last] * rows
    metal_gram_rows(last, last)
    metal_done = packed(mpairs, 0, 32)
    rows_flow(ra.at[1], KRYLOV + 2).wait_recv()
    rb[1, pl.ds(s, 1), :] = jnp.sum(ra[1], axis=0, keepdims=True) + metal_done
    send_rows_span(rb.at[1], 1)
    for k, width in PLAN:
        for copy in halos(k) if width == 1 else pair_copies(k) + inflow_copies(k):
            copy.wait_send()
    for copy in once_copies():
        copy.wait_send()
    for copy in first_edges():
        copy.wait_send()
    for k in range(KRYLOV - 1):
        for copy in edges(k):
            copy.wait_send()
    for k in range(KRYLOV):
        rows_flow(wall.at[k], k).wait_send()
    rows_flow(place, KRYLOV).wait_send()
    rows_flow(ra.at[0], KRYLOV + 1).wait_send()
    rows_flow(ra.at[1], KRYLOV + 2).wait_send()
    rows_span(rb.at[0], 0).wait_send()
    rows_span(rb.at[1], 1).wait()
    unpack(jnp.sum(rb[1], axis=0, keepdims=True))
    gram = {}
    n = 0
    for i in range(KRYLOV + 1):
        for j in range(i + 1):
            m = 24 + j if i == KRYLOV else n
            gram[j, i] = scal[m : m + 1, :]
            n += 1
    r = {}
    low = None
    for i in range(KRYLOV + 1):
        scale = None
        for j in range(i, KRYLOV + 1):
            t = gram[i, j]
            for h in range(i):
                t = t - r[h, i] * r[h, j]
            if i == j:
                rel = t / gram[i, i]
                low = rel if low is None else jnp.minimum(low, rel)
                scale = lax.rsqrt(t)
            r[i, j] = t * scale
    zero = jnp.zeros((1, 128), f32)
    hess = [[zero] * KRYLOV for _ in range(KRYLOV + 1)]
    for j in range(KRYLOV):
        for i in range(j + 2):
            t = r[i, j + 1] * coef_b[j + 1]
            if i <= j:
                t = t + r[i, j] * coef_a[j]
            if i <= j - 1:
                t = t + r[i, j - 1] * coef_b[j]
            hess[i][j] = t
    y = small_solve(hess, r[0, 0] / poly[0][0], zero, KRYLOV)
    top = jnp.abs(y[0])
    total = jnp.abs(y[0]) * spread[0]
    for k in range(1, KRYLOV):
        top = jnp.maximum(top, jnp.abs(y[k]))
        total = total + jnp.abs(y[k]) * spread[k]
    fine = (low > 1e-2) & (total < 1e3 * top)
    ok_ref[...] = jnp.where(fine, 1.0, 0.0)
    for g in range(6):
        t = y[0] * q[0, g]
        for k in range(1, KRYLOV):
            t = t + y[k] * q[k, g]
        xf_ref[g] = t
    out = None
    for j in range(KRYLOV):
        c = y[j] * poly[j][j]
        for k in range(j + 1, KRYLOV):
            c = c + y[k] * poly[k][j]
        out = c * u[j, 8:40, :] if out is None else out + c * u[j, 8:40, :]
    xs_ref[...] = out


def store(a_ref, b_ref, a_out, b_out, sem):
    copies = [
        pltpu.make_async_copy(a_ref, a_out, sem.at[0]),
        pltpu.make_async_copy(b_ref, b_out, sem.at[1]),
    ]
    for copy in copies:
        copy.start()
    for copy in copies:
        copy.wait()


def shards(ns, nf, *args):
    rhs_fluid, rhs_solid = args[0], args[1]
    f32 = jnp.float32
    hbm = pl.BlockSpec(memory_space=pltpu.HBM)
    vmem = pl.BlockSpec(memory_space=pltpu.VMEM)
    smem = pl.BlockSpec(memory_space=pltpu.SMEM)
    dma = pltpu.SemaphoreType.DMA
    x_fluid, x_solid, ok, coef = pl.pallas_call(
        functools.partial(kernel, ns, nf),
        name="gmres",
        out_shape=(
            jax.ShapeDtypeStruct(rhs_fluid.shape, f32),
            jax.ShapeDtypeStruct(rhs_solid.shape, f32),
            jax.ShapeDtypeStruct((1, 128), f32),
            jax.ShapeDtypeStruct(args[-1].shape, f32),
        ),
        in_specs=[hbm] * 5 + [smem] * 2 + [hbm],
        out_specs=(vmem,) * 4,
        scratch_shapes=[
            pltpu.VMEM((KRYLOV + 1, 6, 2, 8, 128), f32),
            pltpu.VMEM((KRYLOV, 48, 128), f32),
            pltpu.VMEM((KRYLOV + 1, 6, 2, 8, 128), f32),
            pltpu.VMEM((KRYLOV + 1, 32, 128), f32),
            pltpu.VMEM((6, 6, 2, 8, 128), f32),
            pltpu.VMEM((6, 2, 8, 128), f32),
            pltpu.VMEM((5, 2, 8, 128), f32),
            pltpu.VMEM((48, 128), f32),
            pltpu.VMEM((KRYLOV, 2, 6, 8, 128), f32),
            pltpu.VMEM((KRYLOV, 2, 16, 128), f32),
            pltpu.VMEM((KRYLOV, 2, 16, 128), f32),
            pltpu.VMEM((KRYLOV - 1, 48, 128), f32),
            pltpu.VMEM((KRYLOV, 32, 128), f32),
            pltpu.VMEM((32, 128), f32),
            pltpu.VMEM((32, 128), f32),
            pltpu.VMEM((32, 128), f32),
            pltpu.VMEM((32, 128), f32),
            pltpu.VMEM((2, 32, 128), f32),
            pltpu.VMEM((2, 16, 128), f32),
            pltpu.VMEM((len(PAIRS), 6, 2, 8, 128), f32),
            pltpu.VMEM((len(PAIRS), 6, 2, 8, 128), f32),
            pltpu.VMEM((len(PAIRS), 6, 2, 8, 128), f32),
            pltpu.VMEM((len(PAIRS), 6, 8, 128), f32),
            pltpu.VMEM((len(PAIRS), 6, 8, 128), f32),
            pltpu.VMEM((len(PAIRS), 6, 8, 128), f32),
            pltpu.VMEM((len(PAIRS), 8, 128), f32),
            pltpu.VMEM((len(PAIRS), 8, 128), f32),
            pltpu.VMEM((6, 8, 128), f32),
            pltpu.VMEM((6, 8, 128), f32),
            pltpu.VMEM((6, 8, 128), f32),
            pltpu.VMEM((6, 8, 128), f32),
            pltpu.VMEM((11, 8, 128), f32),
            pltpu.VMEM((8, 128), f32),
            pltpu.VMEM((6, 8, 128), f32),
            pltpu.VMEM((6, 8, 128), f32),
            pltpu.VMEM((6, 8, 128), f32),
            dma((6,)),
            dma((KRYLOV, 4)), dma((KRYLOV, 4)),
            dma((KRYLOV + 2, 2)), dma((KRYLOV + 2, 2)),
            dma((KRYLOV + 3,)), dma((KRYLOV + 3,)),
            dma((2,)), dma((2,)),
            dma((len(PAIRS), 14)), dma((len(PAIRS), 14)),
            dma((8,)), dma((8,)),
        ],
        compiler_params=pltpu.CompilerParams(
            collective_id=0, has_side_effects=True, vmem_limit_bytes=8 * 1024 * 1024
        ),
    )(*args)
    def place_out(*a):
        return pl.pallas_call(
            store,
            name="place_out",
            out_shape=(
                jax.ShapeDtypeStruct(rhs_fluid.shape, f32),
                jax.ShapeDtypeStruct(rhs_solid.shape, f32),
            ),
            in_specs=[vmem, vmem],
            out_specs=(hbm, hbm),
            scratch_shapes=[dma((2,))],
        )(x_fluid, x_solid)

    return lax.cond(ok[0, 0] > 0.5, place_out, lambda *a: arnoldi(*a), *args[:-1], coef)


def solution(mesh):
    in_specs = (
        P(None, "span", "flow", None),
        P("span", None),
        P(None, None, "span", "flow", None),
        P(None, "span", "flow", None),
        P("span", None),
        P("span", "flow"),
        P("span", "flow"),
        P("span", "flow", None),
    )
    out_specs = (P(None, "span", "flow", None), P("span", None))
    return jax.shard_map(
        functools.partial(shards, mesh.shape["span"], mesh.shape["flow"]),
        mesh=mesh, in_specs=in_specs, out_specs=out_specs, check_vma=False,
    )
```

```python
import functools

import jax
import jax.numpy as jnp
from jax import lax
from jax.experimental import pallas as pl
from jax.experimental.pallas import tpu as pltpu
from jax.sharding import PartitionSpec as P

KRYLOV = 6
MESH = pl.DeviceIdType.MESH
EARLY = 2
PLAN = ((0, 1), (1, 1), (2, 1), (3, 1), (4, 2))
PAIRS = tuple(k for k, width in PLAN if width == 2)


def extended(shard, sides, width):
    for axis, dim in sides:
        count, length = (lax.axis_size(axis), shard.shape[dim])
        up = [(i, (i + 1) % count) for i in range(count - 1)]
        down = [(j, i) for i, j in up]
        last = lax.slice_in_dim(shard, length - width, length, axis=dim)
        first = lax.slice_in_dim(shard, 0, width, axis=dim)
        before = lax.ppermute(last, axis, up)
        after = lax.ppermute(first, axis, down)
        shard = jnp.concatenate([before, shard, after], axis=dim)
    return shard


def back_substitute(upper, rhs_g, steps):
    coeffs = [None] * steps
    for j in range(steps - 1, -1, -1):
        total = rhs_g[j]
        for k in range(j + 1, steps):
            total = total - upper[k][j] * coeffs[k]
        coeffs[j] = total / upper[j][j]
    return coeffs


def least_squares(hess, beta, zero, steps):
    cos_list, sin_list, upper = ([], [], [])
    rhs_g = [beta] + [zero for _ in range(steps)]
    for j in range(steps):
        column = [hess[i][j] for i in range(j + 2)]
        for i in range(j):
            top = cos_list[i] * column[i] + sin_list[i] * column[i + 1]
            column[i + 1] = -sin_list[i] * column[i] + cos_list[i] * column[i + 1]
            column[i] = top
        radius = jnp.sqrt(column[j] * column[j] + column[j + 1] * column[j + 1])
        cos_now = column[j] / radius
        sin_now = column[j + 1] / radius
        column[j] = radius
        rhs_g[j + 1] = -sin_now * rhs_g[j]
        rhs_g[j] = cos_now * rhs_g[j]
        cos_list.append(cos_now)
        sin_list.append(sin_now)
        upper.append(column[: j + 1])
    return back_substitute(upper, rhs_g, steps)


def arnoldi(rhs_fluid, rhs_solid, blocks, weights, kdiag, wall_fluid, wall_solid, wall_coef):
    rows_a = rhs_fluid.shape[1]
    rows_b = rhs_fluid.shape[2]
    width = rhs_fluid.shape[3]
    cells = rows_a * rows_b
    band_rows = rhs_solid.shape[0]
    patch_rows = wall_fluid[0]
    patch_metal = wall_solid[0]
    coef = wall_coef[0]
    fluid_pick = (jnp.arange(cells, dtype=jnp.int32)[:, None] == patch_rows[None, :]).astype(
        jnp.float32
    )
    metal_pick = (jnp.arange(band_rows, dtype=jnp.int32)[:, None] == patch_metal[None, :]).astype(
        jnp.float32
    )
    first_flow = (lax.axis_index("flow") == 0).astype(jnp.float32)
    highest = lax.Precision.HIGHEST

    def local_inner(left, right):
        return jnp.sum(left[0] * right[0]) + first_flow * jnp.sum(left[1] * right[1])

    beta = jnp.sqrt(
        lax.psum(local_inner((rhs_fluid, rhs_solid), (rhs_fluid, rhs_solid)), ("span", "flow"))
    )
    basis = [(rhs_fluid / beta, rhs_solid / beta)]
    hess = [[jnp.float32(0.0) for _ in range(KRYLOV)] for _ in range(KRYLOV + 1)]
    for j in range(KRYLOV):
        field = basis[j][0]
        metal_u = basis[j][1]
        padded = extended(field, (("span", 1), ("flow", 2)), 1)
        local = jnp.einsum("fgabc,gabc->fabc", blocks, field, precision=highest)
        beside = weights[0][None] * padded[:, :-2, 1:-1] + weights[1][None] * padded[:, 2:, 1:-1]
        beside = (
            beside
            + weights[2][None] * padded[:, 1:-1, :-2]
            + weights[3][None] * padded[:, 1:-1, 2:]
        )
        beside = (
            beside
            + weights[4][None] * jnp.roll(field, 1, axis=3)
            + weights[5][None] * jnp.roll(field, -1, axis=3)
        )
        metal_at = jnp.dot(metal_pick.T, metal_u, precision=highest)
        inflow = jnp.dot(fluid_pick, coef * metal_at, precision=highest).reshape(
            rows_a, rows_b, width
        )
        image_f = (local - beside).at[5].add(-inflow)
        wall_vals = coef * jnp.dot(fluid_pick.T, field[5].reshape(cells, width), precision=highest)
        sink = lax.psum(jnp.dot(metal_pick, wall_vals, precision=highest), "flow")
        upad = extended(metal_u, (("span", 0),), 1)
        beside_all = (
            upad[:-2] + upad[2:] + jnp.roll(metal_u, 1, axis=1) + jnp.roll(metal_u, -1, axis=1)
        )
        image_s = (4.0 + kdiag) * metal_u - beside_all - sink
        terms = jnp.stack([local_inner(basis[i], (image_f, image_s)) for i in range(j + 1)])
        values = lax.psum(terms, ("span", "flow"))
        for i in range(j + 1):
            image_f = image_f - values[i] * basis[i][0]
            image_s = image_s - values[i] * basis[i][1]
        rest = jnp.sqrt(
            lax.psum(local_inner((image_f, image_s), (image_f, image_s)), ("span", "flow"))
        )
        for i in range(j + 1):
            hess[i][j] = values[i]
        hess[j + 1][j] = rest
        basis.append((image_f / rest, image_s / rest))
    coeffs = least_squares(hess, beta, jnp.float32(0.0), KRYLOV)
    x_fluid = jnp.zeros_like(rhs_fluid)
    x_solid = jnp.zeros_like(rhs_solid)
    for j in range(KRYLOV):
        x_fluid = x_fluid + coeffs[j] * basis[j][0]
        x_solid = x_solid + coeffs[j] * basis[j][1]
    return (x_fluid, x_solid)


def small_solve(hess, beta, zero, steps):
    cos_list, sin_list, upper, inverse = ([], [], [], [])
    rhs_g = [beta] + [zero for _ in range(steps)]
    for j in range(steps):
        column = [hess[i][j] for i in range(j + 2)]
        for i in range(j):
            top = cos_list[i] * column[i] + sin_list[i] * column[i + 1]
            column[i + 1] = -sin_list[i] * column[i] + cos_list[i] * column[i + 1]
            column[i] = top
        scale = lax.rsqrt(column[j] * column[j] + column[j + 1] * column[j + 1])
        cos_now = column[j] * scale
        sin_now = column[j + 1] * scale
        rhs_g[j + 1] = -sin_now * rhs_g[j]
        rhs_g[j] = cos_now * rhs_g[j]
        cos_list.append(cos_now)
        sin_list.append(sin_now)
        upper.append(column[:j])
        inverse.append(scale)
    coeffs = [None] * steps
    for j in range(steps - 1, -1, -1):
        total = rhs_g[j]
        for k in range(j + 1, steps):
            total = total - upper[k][j] * coeffs[k]
        coeffs[j] = total * inverse[j]
    return coeffs


def kernel(
    ns, nf,
    rf_hbm, rs_hbm, bl_hbm, we_hbm, kd_hbm, wf_ref, ws_ref, wc_hbm,
    xf_ref, xs_ref, ok_ref, wc,
    z, u, q, qm, bl, we, wm, kd, hs, hq, sq, sinks, wall, place, pairs, mpairs, scal, ra, rb,
    tl, th, lp, sb, pk, cb, ir, ib, wl, wh, wsr, pws, wn, pid, el, eh, es,
    in_sem, s_halo, r_halo, s_edge, r_edge, s_wall, r_wall, s_red, r_red, s_pair, r_pair, s_once, r_once,
):
    f32 = jnp.float32
    s = lax.axis_index("span")
    f = lax.axis_index("flow")
    up = (lax.rem(s + 1, ns), f)
    down = (lax.rem(s + ns - 1, ns), f)
    right = (s, lax.rem(f + 1, nf))
    left = (s, lax.rem(f + nf - 1, nf))
    corners = ((up[0], right[1]), (down[0], right[1]), (up[0], left[1]), (down[0], left[1]))

    loads = [
        pltpu.make_async_copy(rf_hbm, z.at[0], in_sem.at[0]),
        pltpu.make_async_copy(rs_hbm, u.at[0, pl.ds(8, 32)], in_sem.at[1]),
        pltpu.make_async_copy(we_hbm, we, in_sem.at[2]),
        pltpu.make_async_copy(bl_hbm, bl, in_sem.at[3]),
        pltpu.make_async_copy(kd_hbm, kd.at[pl.ds(8, 32)], in_sem.at[4]),
        pltpu.make_async_copy(wc_hbm, wc, in_sem.at[5]),
    ]
    for load in loads:
        load.start()

    cb[...] = jnp.zeros((len(PAIRS), 6, 8, 128), f32)

    barrier = pltpu.get_barrier_semaphore()

    def far_first(n):
        return sorted(range(1, n), key=lambda d: -min(d, n - d))

    flow_peers = [(s, lax.rem(f + d, nf)) for d in far_first(nf)]
    span_peers = [(lax.rem(s + d, ns), f) for d in far_first(ns)]
    for to in span_peers + flow_peers:
        pl.semaphore_signal(barrier, inc=1, device_id=to, device_id_type=MESH)
    for to in corners:
        pl.semaphore_signal(barrier, inc=1, device_id=to, device_id_type=MESH)
    row8 = lax.broadcasted_iota(jnp.int32, (8, 128), 0)
    row16 = lax.broadcasted_iota(jnp.int32, (2, 8, 128), 0) * 8 + lax.broadcasted_iota(
        jnp.int32, (2, 8, 128), 1
    )
    row32 = lax.broadcasted_iota(jnp.int32, (32, 128), 0)
    lane32 = lax.broadcasted_iota(jnp.int32, (32, 128), 1)
    lane1 = lax.broadcasted_iota(jnp.int32, (1, 128), 1)
    eye = row32 == lane32
    loads[5].wait()
    patch = wf_ref[0, 0]
    metal_row = ws_ref[0, 0]
    coef = wc[0]
    wall_mask = jnp.where(row16 == patch, 1.0, 0.0).astype(f32)
    metal_mask = jnp.where(row32 == metal_row, 1.0, 0.0).astype(f32)
    place[pl.ds(f, 1), :] = jnp.where(lane1 == f, metal_row.astype(f32), 0.0)
    has_down = jnp.where(s > 0, 1.0, 0.0).astype(f32)
    has_up = jnp.where(s < ns - 1, 1.0, 0.0).astype(f32)
    has_left = jnp.where(f > 0, 1.0, 0.0).astype(f32)
    has_right = jnp.where(f < nf - 1, 1.0, 0.0).astype(f32)
    row48 = lax.broadcasted_iota(jnp.int32, (48, 128), 0)
    inside = jnp.where(row48 < 8, has_down, jnp.where(row48 < 40, 1.0, has_up))

    def send_rows_flow(buf, k):
        for to in flow_peers:
            pltpu.make_async_remote_copy(
                src_ref=buf.at[pl.ds(f, 1)], dst_ref=buf.at[pl.ds(f, 1)],
                send_sem=s_wall.at[k], recv_sem=r_wall.at[k], device_id=to, device_id_type=MESH,
            ).start()

    def rows_flow(buf, k):
        return pltpu.make_async_remote_copy(
            src_ref=buf.at[pl.ds(0, nf - 1)], dst_ref=buf.at[pl.ds(0, nf - 1)],
            send_sem=s_wall.at[k], recv_sem=r_wall.at[k], device_id=right, device_id_type=MESH,
        )

    def send_rows_span(buf, k):
        for to in span_peers:
            pltpu.make_async_remote_copy(
                src_ref=buf.at[pl.ds(s, 1)], dst_ref=buf.at[pl.ds(s, 1)],
                send_sem=s_red.at[k], recv_sem=r_red.at[k], device_id=to, device_id_type=MESH,
            ).start()

    def rows_span(buf, k):
        return pltpu.make_async_remote_copy(
            src_ref=buf.at[pl.ds(0, ns - 1)], dst_ref=buf.at[pl.ds(0, ns - 1)],
            send_sem=s_red.at[k], recv_sem=r_red.at[k], device_id=up, device_id_type=MESH,
        )

    def halos(k):
        def copy(n, src, dst, to):
            return pltpu.make_async_remote_copy(
                src_ref=src, dst_ref=dst, send_sem=s_halo.at[k, n], recv_sem=r_halo.at[k, n],
                device_id=to, device_id_type=MESH,
            )

        return [
            copy(0, z.at[k, :, 1], hs.at[k, 0], up),
            copy(1, z.at[k, :, 0], hs.at[k, 1], down),
            copy(2, sq.at[k, 0], hq.at[k, 0], right),
            copy(3, sq.at[k, 1], hq.at[k, 1], left),
        ]

    def rows_to_bands(buf, n):
        def copy(m, src, dst, to):
            return pltpu.make_async_remote_copy(
                src_ref=buf.at[pl.ds(src, 8)], dst_ref=buf.at[pl.ds(dst, 8)],
                send_sem=s_edge.at[n, m], recv_sem=r_edge.at[n, m],
                device_id=to, device_id_type=MESH,
            )

        return [copy(0, 32, 0, up), copy(1, 8, 40, down)]

    def edges(k):
        return rows_to_bands(sinks.at[k], k)

    def first_edges():
        return rows_to_bands(u.at[0], KRYLOV) + rows_to_bands(kd, KRYLOV + 1)

    def send_halos(k):
        out = halos(k)
        out[0].start()
        out[1].start()
        for g in range(6):
            for a in range(2):
                i = 2 * g + a
                sq[k, 0, i : i + 1, :] = z[k, g, a, 7:8, :]
                sq[k, 1, i : i + 1, :] = z[k, g, a, 0:1, :]
        out[2].start()
        out[3].start()

    def remote(src, dst, send, recv, to):
        return pltpu.make_async_remote_copy(
            src_ref=src, dst_ref=dst, send_sem=send, recv_sem=recv, device_id=to, device_id_type=MESH
        )

    def pair_copies(k):
        p = PAIRS.index(k)

        def copy(n, src, dst, to):
            return remote(src, dst, s_pair.at[p, n], r_pair.at[p, n], to)

        return [
            copy(0, z.at[k, :, 1], tl.at[p, :, 1], up),
            copy(1, z.at[k, :, 0], th.at[p, :, 0], down),
            copy(4, pk.at[p, :, pl.ds(5, 1)], cb.at[p, :, pl.ds(0, 1)], corners[0]),
            copy(5, pk.at[p, :, pl.ds(4, 1)], cb.at[p, :, pl.ds(1, 1)], corners[1]),
            copy(6, pk.at[p, :, pl.ds(1, 1)], cb.at[p, :, pl.ds(4, 1)], corners[2]),
            copy(7, pk.at[p, :, pl.ds(0, 1)], cb.at[p, :, pl.ds(5, 1)], corners[3]),
            copy(12, lp.at[p, :, 1], tl.at[p, :, 0], up),
            copy(13, lp.at[p, :, 0], th.at[p, :, 1], down),
            copy(2, pk.at[p, :, pl.ds(4, 4)], sb.at[p, :, pl.ds(0, 4)], right),
            copy(3, pk.at[p, :, pl.ds(0, 4)], sb.at[p, :, pl.ds(4, 4)], left),
        ]

    def inflow_copies(k):
        p = PAIRS.index(k)
        return [
            remote(
                ir.at[p, pl.ds(0, 1)], ib.at[p, pl.ds(n, 1)],
                s_pair.at[p, 8 + n], r_pair.at[p, 8 + n], to,
            )
            for n, to in enumerate((up, down, right, left))
        ]

    def once_copies():
        def copy(n, src, dst, to):
            return remote(src, dst, s_once.at[n], r_once.at[n], to)

        out = [
            copy(0, we.at[:, 1], wl, up),
            copy(1, we.at[:, 0], wh, down),
            copy(2, pws.at[:, pl.ds(4, 4)], wsr.at[:, pl.ds(0, 4)], right),
            copy(3, pws.at[:, pl.ds(0, 4)], wsr.at[:, pl.ds(4, 4)], left),
        ]
        return out + [
            copy(4 + m, pid.at[pl.ds(4, 1)], pid.at[pl.ds(m, 1)], to)
            for m, to in enumerate((up, down, right, left))
        ]

    PACK = ((0, 0, 0), (1, 0, 1), (4, 7, 0), (5, 7, 1))

    def pack_once():
        for i in range(6):
            for m, b, a in PACK:
                pws[i, m : m + 1, :] = we[i, a, b : b + 1, :]
                pws[i, m + 2 : m + 3, :] = we[i, a, b : b + 1, :]
        pid[4:5, :] = jnp.broadcast_to(patch.astype(f32), (1, 128))

    def prepare_pairs():
        wn[0] = jnp.where(row8 == 0, has_left * wl[2], 0.0)
        wn[1] = jnp.where(row8 == 7, has_right * wl[3], 0.0)
        wn[2] = jnp.where(row8 == 0, has_left * wh[2], 0.0)
        wn[3] = jnp.where(row8 == 7, has_right * wh[3], 0.0)
        first = (row8 == 0) | (row8 == 4)
        wn[4] = jnp.where(first, has_down * wsr[0], has_up * wsr[1])
        wn[7] = jnp.where(row8 < 4, wsr[3], wsr[2])
        here = row8.astype(f32)
        wn[8] = jnp.where(here + 8.0 == pid[0:1, :], 1.0, 0.0)
        wn[9] = jnp.where(here == pid[1:2, :], 1.0, 0.0)
        side = jnp.where((row8 == 0) & (pid[2:3, :] == 7.0), 1.0, 0.0)
        side = side + jnp.where((row8 == 1) & (pid[2:3, :] == 15.0), 1.0, 0.0)
        side = side + jnp.where((row8 == 4) & (pid[3:4, :] == 0.0), 1.0, 0.0)
        wn[10] = side + jnp.where((row8 == 5) & (pid[3:4, :] == 8.0), 1.0, 0.0)

    def beside_cells(k):
        p = PAIRS.index(k)
        for g in range(6):
            el[g] = (
                tl[p, g, 0] - wl[1] * z[k, g, 0]
                - wn[0] * cb[p, g, 0:1, :] - wn[1] * cb[p, g, 4:5, :]
            )
            eh[g] = (
                th[p, g, 1] - wh[0] * z[k, g, 1]
                - wn[2] * cb[p, g, 1:2, :] - wn[3] * cb[p, g, 5:6, :]
            )
            es[g] = pltpu.roll(sb[p, g], 6, 0) - wn[4] * cb[p, g] - wn[7] * pk[p, g]

    def beside_inflow(k):
        p = PAIRS.index(k)
        el[5] = el[5] - wn[8] * ib[p, 0:1, :]
        eh[5] = eh[5] - wn[9] * ib[p, 1:2, :]
        es[5] = es[5] - wn[10] * jnp.where(row8 < 4, ib[p, 2:3, :], ib[p, 3:4, :])

    def local_part(k):
        field = [z[k, g] for g in range(6)]
        for g in range(6):
            v = field[g]
            total = bl[g, 0] * field[0]
            for h in range(1, 6):
                total = total + bl[g, h] * field[h]
            total = total - we[4] * pltpu.roll(v, 1, 2) - we[5] * pltpu.roll(v, 127, 2)
            total = total - wm[0] * pltpu.roll(v, 1, 1) - wm[1] * pltpu.roll(v, 7, 1)
            z[k + 1, g, 0] = total[0] - we[1, 0] * v[1]
            z[k + 1, g, 1] = total[1] - we[0, 1] * v[0]

    def halo_part(k, metal_here, low, high, west, east):
        inflow = coef * metal_here
        for g in range(6):
            for a in range(2):
                total = z[k + 1, g, a]
                if a == 0:
                    total = total - wm[4, 0] * low(g)
                else:
                    total = total - wm[4, 1] * high(g)
                total = total - wm[2, a] * west(g, a) - wm[3, a] * east(g, a)
                if g == 5:
                    total = total - wall_mask[a] * inflow
                z[k + 1, g, a] = total

    def own_metal(values):
        return jnp.sum(metal_mask * values, axis=0, keepdims=True)

    def wall_value(k):
        picked = wall_mask[0] * z[k, 5, 0] + wall_mask[1] * z[k, 5, 1]
        return coef * jnp.sum(picked, axis=0, keepdims=True)

    def metal_local(k):
        v = u[k]
        total = (4.0 + kd[...]) * v - pltpu.roll(v, 1, 1) - pltpu.roll(v, 127, 1)
        return (total - pltpu.roll(v, 1, 0) - pltpu.roll(v, 47, 0)) * inside

    def metal_halo(k):
        if k == 0:
            for copy in first_edges():
                copy.wait_recv()
            u[0, 0:8, :] = u[0, 0:8, :] * has_down
            u[0, 40:48, :] = u[0, 40:48, :] * has_up
        else:
            for copy in edges(k - 1):
                copy.wait_recv()
            u[k, 0:8, :] = u[k, 0:8, :] - has_down * sinks[k - 1, 0:8, :]
            u[k, 40:48, :] = u[k, 40:48, :] - has_up * sinks[k - 1, 40:48, :]

    def sink_of(k):
        rows_flow(wall.at[k], k).wait_recv()
        return jnp.dot(
            state["pick"], wall[k], precision=lax.Precision.HIGHEST, preferred_element_type=f32
        )

    def dot_row(store, i, j):
        total = store[i, 0, 0] * store[j, 0, 0] + store[i, 0, 1] * store[j, 0, 1]
        for g in range(1, 6):
            total = total + store[i, g, 0] * store[j, g, 0] + store[i, g, 1] * store[j, g, 1]
        return jnp.sum(total, axis=0, keepdims=True)

    def metal_dot_row(i, j):
        t = qm[i] * qm[j]
        t = (t[0:8] + t[8:16]) + (t[16:24] + t[24:32])
        return jnp.sum(t, axis=0, keepdims=True)

    def packed(rows, low, high):
        sums = jnp.sum(rows[low:high, :], axis=1, keepdims=True)
        return jnp.sum(jnp.where(eye[low:high], sums, 0.0), axis=0, keepdims=True)

    def unpack(total):
        sums = jnp.sum(jnp.where(eye, total, 0.0), axis=1, keepdims=True)
        scal[...] = jnp.broadcast_to(sums, (32, 128))

    loads[0].wait()
    for g in range(6):
        for a in range(2):
            i = 2 * g + a
            sq[0, 0, i : i + 1, :] = z[0, g, a, 7:8, :]
            sq[0, 1, i : i + 1, :] = z[0, g, a, 0:1, :]
    sq[:, :, 12:16, :] = jnp.zeros((KRYLOV, 2, 4, 128), f32)
    pl.semaphore_wait(barrier, ns + nf + 2)
    for copy in halos(0):
        copy.start()
    loads[1].wait()
    pairs[...] = jnp.zeros((32, 128), f32)
    mpairs[...] = jnp.zeros((32, 128), f32)
    loads[2].wait()
    wm[0] = jnp.where(row8 == 0, 0.0, we[2])
    wm[1] = jnp.where(row8 == 7, 0.0, we[3])
    wm[2] = jnp.where(row8 == 0, has_left * we[2], 0.0)
    wm[3] = jnp.where(row8 == 7, has_right * we[3], 0.0)
    wm[4, 0] = has_down * we[0, 0]
    wm[4, 1] = has_up * we[1, 1]
    loads[3].wait()
    loads[4].wait()
    for copy in first_edges():
        copy.start()

    own = []
    state = {}

    def wall_step(k):
        wall[k, pl.ds(f, 1), :] = wall_value(k)
        send_rows_flow(wall.at[k], k)

    def metal_step(k):
        if k == 1:
            rows_flow(place, KRYLOV).wait_recv()
            places = jnp.sum(place[...], axis=0, keepdims=True)
            state["pick"] = jnp.where((row32.astype(f32) == places) & (lane32 < 32), 1.0, 0.0)[:, 0:32]
        if k > 0:
            sinks[k - 1, 8:40, :] = sink_of(k - 1)
            for copy in edges(k - 1):
                copy.start()
            metal_halo(k - 1)
            u[k] = metal_local(k - 1)
            u[k, 8:40, :] = u[k, 8:40, :] - sinks[k - 1, 8:40, :]
        own.append(own_metal(u[k, 8:40, :]))

    def early_gram():
        n = 0
        for i in range(EARLY):
            for j in range(i, EARLY):
                pairs[n : n + 1, :] = dot_row(z, i, j)
                n += 1
        ra[0, pl.ds(f, 1), :] = packed(pairs, 0, 32)
        send_rows_flow(ra.at[0], KRYLOV + 1)

    def early_span():
        rows_flow(ra.at[0], KRYLOV + 1).wait_recv()
        rb[0, pl.ds(s, 1), :] = jnp.sum(ra[0], axis=0, keepdims=True)
        send_rows_span(rb.at[0], 0)

    def basis():
        rows_span(rb.at[0], 0).wait_recv()
        unpack(jnp.sum(rb[0], axis=0, keepdims=True))
        gram = {}
        n = 0
        for i in range(EARLY):
            for j in range(i, EARLY):
                gram[i, j] = scal[n : n + 1, :]
                n += 1
        r = {}
        inv = []
        trust = []
        for i in range(EARLY):
            for j in range(i, EARLY):
                t = gram[i, j]
                for h in range(i):
                    t = t - r[h, i] * r[h, j]
                if i == j:
                    floor = gram[i, i] * 1e-5
                    trust.append(t > floor)
                    t = jnp.maximum(t, floor)
                    inv.append(lax.rsqrt(t))
                r[i, j] = t * inv[i]
        ratio = [r[i, i + 1] * inv[i] for i in range(EARLY - 1)]
        coef_a = [ratio[0]]
        coef_b = [None, r[1, 1] * inv[0]]
        good = trust[1]
        for i in range(1, EARLY - 1):
            good = good & trust[i + 1]
            coef_a.append(jnp.where(good, ratio[i] - ratio[i - 1], coef_a[i - 1]))
            guess = coef_b[1] * 1.22
            coef_b.append(jnp.where(good, r[i + 1, i + 1] * inv[i], guess))
        while len(coef_a) < KRYLOV:
            coef_a.append(coef_a[-1])
        while len(coef_b) < KRYLOV + 1:
            coef_b.append(coef_b[-1])
        poly = [[inv[0]]]
        for i in range(KRYLOV):
            back = 1.0 / coef_b[i + 1]
            new = []
            for j in range(i + 2):
                t = None
                if j >= 1:
                    t = poly[i][j - 1]
                if j <= i:
                    t = -coef_a[i] * poly[i][j] if t is None else t - coef_a[i] * poly[i][j]
                if i >= 1 and j <= i - 1:
                    t = t - coef_b[i] * poly[i - 1][j]
                new.append(t * back)
            poly.append(new)
        size = [jnp.sqrt(gram[i, i]) for i in range(EARLY)]
        growth = size[-1] / size[-2]
        while len(size) < KRYLOV:
            size.append(size[-1] * growth)
        spread = []
        for i in range(KRYLOV):
            t = jnp.abs(poly[i][0]) * size[0]
            for j in range(1, i + 1):
                t = t + jnp.abs(poly[i][j]) * size[j]
            spread.append(t)
        return coef_a, coef_b, poly, spread

    def combine(low, high, first):
        poly = state["basis"][2]
        for i in range(low, KRYLOV + 1):
            terms = range(low, min(i, high) + 1)
            if not terms:
                continue
            for g in range(6):
                t = None if first else q[i, g]
                for j in terms:
                    t = poly[i][j] * z[j, g] if t is None else t + poly[i][j] * z[j, g]
                q[i, g] = t

    def metal_combine(low, high, first):
        poly = state["basis"][2]
        for i in range(low, KRYLOV + 1):
            t = None if first else qm[i]
            for j in range(low, min(i, high) + 1):
                rows = u[j, 8:40, :]
                t = poly[i][j] * rows if t is None else t + poly[i][j] * rows
            qm[i] = t

    def place_of(j, i):
        return 24 + j if i == KRYLOV else i * (i + 1) // 2 + j

    def gram_rows(low, high):
        for i in range(low, high + 1):
            for j in range(i + 1):
                n = place_of(j, i)
                pairs[n : n + 1, :] = dot_row(q, j, i)

    def metal_gram_rows(low, high):
        for i in range(low, high + 1):
            for j in range(i + 1):
                n = place_of(j, i)
                mpairs[n : n + 1, :] = metal_dot_row(j, i)

    early = [k for k, _ in PLAN if k >= EARLY - 1][0]
    when = [k for k, _ in PLAN].index(early)
    for step, (k, width) in enumerate(PLAN):
        if k > 0:
            if width == 1:
                send_halos(k)
            else:
                p = PAIRS.index(k)
                copies = pair_copies(k)
                for copy in copies[:2]:
                    copy.start()
                for g in range(6):
                    for m, b, a in PACK:
                        pk[p, g, m : m + 1, :] = z[k, g, a, b : b + 1, :]
                for copy in copies[2:6]:
                    copy.start()
        if step == when:
            early_gram()
        wall_step(k)
        if k == 0:
            send_rows_flow(place, KRYLOV)
            pack_once()
            for copy in once_copies():
                copy.start()
        local_part(k)
        if width == 2:
            for g in range(6):
                for a in range(2):
                    lp[p, g, a] = z[k + 1, g, a]
                for m, b, a in PACK:
                    pk[p, g, m + 2 : m + 3, :] = z[k + 1, g, a, b : b + 1, :]
            for copy in copies[6:]:
                copy.start()
        metal_step(k)
        if width == 2:
            p = PAIRS.index(k)
            ir[p, 0:1, :] = coef * own[k]
            for copy in inflow_copies(k):
                copy.start()
        if step == when + 1:
            early_span()
        if step == when + 3:
            state["basis"] = basis()
            combine(0, k, True)
            gram_rows(0, k)
        if width == 1:
            for copy in halos(k):
                copy.wait_recv()
            halo_part(
                k, own[k], lambda g: hs[k, 0, g], lambda g: hs[k, 1, g],
                lambda g, a: hq[k, 0, 2 * g + a : 2 * g + a + 1, :],
                lambda g, a: hq[k, 1, 2 * g + a : 2 * g + a + 1, :],
            )
        else:
            if k == PAIRS[0]:
                for copy in once_copies():
                    copy.wait_recv()
                prepare_pairs()
            for copy in pair_copies(k):
                copy.wait_recv()
            halo_part(
                k, own[k], lambda g: tl[p, g, 1], lambda g: th[p, g, 0],
                lambda g, a: sb[p, g, a : a + 1, :],
                lambda g, a: sb[p, g, 4 + a : 5 + a, :],
            )
            wall_step(k + 1)
            beside_cells(k)
            local_part(k + 1)
            if k + 1 == KRYLOV - 1:
                combine(k + 1, k + 1, False)
                gram_rows(k + 1, k + 1)
            for copy in inflow_copies(k):
                copy.wait_recv()
            beside_inflow(k)
            metal_step(k + 1)
            halo_part(
                k + 1, own[k + 1], lambda g: el[g], lambda g: eh[g],
                lambda g, a: es[g, a : a + 1, :],
                lambda g, a: es[g, 4 + a : 5 + a, :],
            )

    last = KRYLOV
    combine(last, last, False)
    gram_rows(last, last)
    ra[1, pl.ds(f, 1), :] = packed(pairs, 0, 32)
    send_rows_flow(ra.at[1], KRYLOV + 2)
    coef_a, coef_b, poly, spread = state["basis"]
    metal_combine(0, last - 1, True)
    metal_gram_rows(0, last - 1)
    metal_halo(last - 1)
    rows = metal_local(last - 1)[8:40, :] - sink_of(last - 1)
    qm[last] = qm[last] + poly[last][last] * rows
    metal_gram_rows(last, last)
    metal_done = packed(mpairs, 0, 32)
    rows_flow(ra.at[1], KRYLOV + 2).wait_recv()
    rb[1, pl.ds(s, 1), :] = jnp.sum(ra[1], axis=0, keepdims=True) + metal_done
    send_rows_span(rb.at[1], 1)
    for k, width in PLAN:
        for copy in halos(k) if width == 1 else pair_copies(k) + inflow_copies(k):
            copy.wait_send()
    for copy in once_copies():
        copy.wait_send()
    for copy in first_edges():
        copy.wait_send()
    for k in range(KRYLOV - 1):
        for copy in edges(k):
            copy.wait_send()
    for k in range(KRYLOV):
        rows_flow(wall.at[k], k).wait_send()
    rows_flow(place, KRYLOV).wait_send()
    rows_flow(ra.at[0], KRYLOV + 1).wait_send()
    rows_flow(ra.at[1], KRYLOV + 2).wait_send()
    rows_span(rb.at[0], 0).wait_send()
    rows_span(rb.at[1], 1).wait()
    unpack(jnp.sum(rb[1], axis=0, keepdims=True))
    gram = {}
    n = 0
    for i in range(KRYLOV + 1):
        for j in range(i + 1):
            m = 24 + j if i == KRYLOV else n
            gram[j, i] = scal[m : m + 1, :]
            n += 1
    r = {}
    low = None
    for i in range(KRYLOV + 1):
        scale = None
        for j in range(i, KRYLOV + 1):
            t = gram[i, j]
            for h in range(i):
                t = t - r[h, i] * r[h, j]
            if i == j:
                rel = t / gram[i, i]
                low = rel if low is None else jnp.minimum(low, rel)
                scale = lax.rsqrt(t)
            r[i, j] = t * scale
    zero = jnp.zeros((1, 128), f32)
    hess = [[zero] * KRYLOV for _ in range(KRYLOV + 1)]
    for j in range(KRYLOV):
        for i in range(j + 2):
            t = r[i, j + 1] * coef_b[j + 1]
            if i <= j:
                t = t + r[i, j] * coef_a[j]
            if i <= j - 1:
                t = t + r[i, j - 1] * coef_b[j]
            hess[i][j] = t
    y = small_solve(hess, r[0, 0] / poly[0][0], zero, KRYLOV)
    top = jnp.abs(y[0])
    total = jnp.abs(y[0]) * spread[0]
    for k in range(1, KRYLOV):
        top = jnp.maximum(top, jnp.abs(y[k]))
        total = total + jnp.abs(y[k]) * spread[k]
    fine = (low > 1e-2) & (total < 1e3 * top)
    ok_ref[...] = jnp.where(fine, 1.0, 0.0)
    for g in range(6):
        t = y[0] * q[0, g]
        for k in range(1, KRYLOV):
            t = t + y[k] * q[k, g]
        xf_ref[g] = t
    out = None
    for j in range(KRYLOV):
        c = y[j] * poly[j][j]
        for k in range(j + 1, KRYLOV):
            c = c + y[k] * poly[k][j]
        out = c * u[j, 8:40, :] if out is None else out + c * u[j, 8:40, :]
    xs_ref[...] = out


def store(a_ref, b_ref, a_out, b_out, sem):
    copies = [
        pltpu.make_async_copy(a_ref, a_out, sem.at[0]),
        pltpu.make_async_copy(b_ref, b_out, sem.at[1]),
    ]
    for copy in copies:
        copy.start()
    for copy in copies:
        copy.wait()


def shards(ns, nf, *args):
    rhs_fluid, rhs_solid = args[0], args[1]
    f32 = jnp.float32
    hbm = pl.BlockSpec(memory_space=pltpu.HBM)
    vmem = pl.BlockSpec(memory_space=pltpu.VMEM)
    smem = pl.BlockSpec(memory_space=pltpu.SMEM)
    dma = pltpu.SemaphoreType.DMA
    x_fluid, x_solid, ok, coef = pl.pallas_call(
        functools.partial(kernel, ns, nf),
        name="gmres",
        out_shape=(
            jax.ShapeDtypeStruct(rhs_fluid.shape, f32),
            jax.ShapeDtypeStruct(rhs_solid.shape, f32),
            jax.ShapeDtypeStruct((1, 128), f32),
            jax.ShapeDtypeStruct(args[-1].shape, f32),
        ),
        in_specs=[hbm] * 5 + [smem] * 2 + [hbm],
        out_specs=(vmem,) * 4,
        scratch_shapes=[
            pltpu.VMEM((KRYLOV + 1, 6, 2, 8, 128), f32),
            pltpu.VMEM((KRYLOV, 48, 128), f32),
            pltpu.VMEM((KRYLOV + 1, 6, 2, 8, 128), f32),
            pltpu.VMEM((KRYLOV + 1, 32, 128), f32),
            pltpu.VMEM((6, 6, 2, 8, 128), f32),
            pltpu.VMEM((6, 2, 8, 128), f32),
            pltpu.VMEM((5, 2, 8, 128), f32),
            pltpu.VMEM((48, 128), f32),
            pltpu.VMEM((KRYLOV, 2, 6, 8, 128), f32),
            pltpu.VMEM((KRYLOV, 2, 16, 128), f32),
            pltpu.VMEM((KRYLOV, 2, 16, 128), f32),
            pltpu.VMEM((KRYLOV - 1, 48, 128), f32),
            pltpu.VMEM((KRYLOV, 32, 128), f32),
            pltpu.VMEM((32, 128), f32),
            pltpu.VMEM((32, 128), f32),
            pltpu.VMEM((32, 128), f32),
            pltpu.VMEM((32, 128), f32),
            pltpu.VMEM((2, 32, 128), f32),
            pltpu.VMEM((2, 16, 128), f32),
            pltpu.VMEM((len(PAIRS), 6, 2, 8, 128), f32),
            pltpu.VMEM((len(PAIRS), 6, 2, 8, 128), f32),
            pltpu.VMEM((len(PAIRS), 6, 2, 8, 128), f32),
            pltpu.VMEM((len(PAIRS), 6, 8, 128), f32),
            pltpu.VMEM((len(PAIRS), 6, 8, 128), f32),
            pltpu.VMEM((len(PAIRS), 6, 8, 128), f32),
            pltpu.VMEM((len(PAIRS), 8, 128), f32),
            pltpu.VMEM((len(PAIRS), 8, 128), f32),
            pltpu.VMEM((6, 8, 128), f32),
            pltpu.VMEM((6, 8, 128), f32),
            pltpu.VMEM((6, 8, 128), f32),
            pltpu.VMEM((6, 8, 128), f32),
            pltpu.VMEM((11, 8, 128), f32),
            pltpu.VMEM((8, 128), f32),
            pltpu.VMEM((6, 8, 128), f32),
            pltpu.VMEM((6, 8, 128), f32),
            pltpu.VMEM((6, 8, 128), f32),
            dma((6,)),
            dma((KRYLOV, 4)), dma((KRYLOV, 4)),
            dma((KRYLOV + 2, 2)), dma((KRYLOV + 2, 2)),
            dma((KRYLOV + 3,)), dma((KRYLOV + 3,)),
            dma((2,)), dma((2,)),
            dma((len(PAIRS), 14)), dma((len(PAIRS), 14)),
            dma((8,)), dma((8,)),
        ],
        compiler_params=pltpu.CompilerParams(
            collective_id=0, has_side_effects=True, vmem_limit_bytes=8 * 1024 * 1024
        ),
    )(*args)
    def place_out(*a):
        return pl.pallas_call(
            store,
            name="place_out",
            out_shape=(
                jax.ShapeDtypeStruct(rhs_fluid.shape, f32),
                jax.ShapeDtypeStruct(rhs_solid.shape, f32),
            ),
            in_specs=[vmem, vmem],
            out_specs=(hbm, hbm),
            scratch_shapes=[dma((2,))],
        )(x_fluid, x_solid)

    return lax.cond(ok[0, 0] > 0.5, place_out, lambda *a: arnoldi(*a), *args[:-1], coef)


def solution(mesh):
    in_specs = (
        P(None, "span", "flow", None),
        P("span", None),
        P(None, None, "span", "flow", None),
        P(None, "span", "flow", None),
        P("span", None),
        P("span", "flow"),
        P("span", "flow"),
        P("span", "flow", None),
    )
    out_specs = (P(None, "span", "flow", None), P("span", None))
    return jax.shard_map(
        functools.partial(shards, mesh.shape["span"], mesh.shape["flow"]),
        mesh=mesh, in_specs=in_specs, out_specs=out_specs, check_vma=False,
    )
```
